32 devices in a mesh: frames: 16 (over z, y, x), mp: 2 (over core).
Axes of the slice: x: 2, y: 2, z: 4, core: 2. Of those that a mesh axis runs over, the one named last changes fastest.
Arguments:
- tokens: bfloat16 [2, 16, 256, 1024], P(None, 'frames', 'mp'), may hold values from -6 to 6
- cotangent: bfloat16 [2, 16, 256, 1024], P(None, 'frames', 'mp'), may hold values from -6 to 6
- scene_ids: int32 [2, 16], replicated, may hold values from 0 to 7, never falling along the last dimension, each value on 1 to 4 neighbouring positions
- input_weight: bfloat16 [2, 1024, 3, 1024], P(None, 'frames', None, 'mp'), may hold values from -0.1875 to 0.1875
- output_weight: bfloat16 [2, 1024, 1024], P(None, 'frames', 'mp'), may hold values from -1 to 1
- up_weight: bfloat16 [2, 1024, 4096], P(None, 'frames', 'mp'), may hold values from -0.1875 to 0.1875
- down_weight: bfloat16 [2, 1024, 4096], P(None, 'frames', 'mp'), may hold values from -0.09375 to 0.09375
- norm_params: float32 [2, 6, 1024], replicated
- head_gains: float32 [2, 2, 64], replicated, may hold values from 0.5 to 1.5
Outputs:
- result: bfloat16 [2, 16, 256, 1024], P(None, 'frames', 'mp')
- token_grad: float32 [2, 16, 256, 1024], P(None, 'frames', 'mp')
- input_grad: float32 [2, 1024, 3, 1024], P(None, 'frames', None, 'mp')
- output_grad: float32 [2, 1024, 1024], P(None, 'frames', 'mp')
- up_grad: float32 [2, 1024, 4096], P(None, 'frames', 'mp')
- down_grad: float32 [2, 1024, 4096], P(None, 'frames', 'mp')
- norm_grad: float32 [2, 6, 1024], replicated
- gain_grad: float32 [2, 2, 64], replicated
The draws below stay inside these ranges and needn't reach their ends.
Inputs may be any that keep to these rules, and one draw needn't show every extreme that they name: `scene_ids`: along each row the scene numbers never fall, so the frames of one scene are consecutive; each scene has 1 to 4 frames and some scene has exactly 4.
All inputs are finite; a program needn't handle non-finite values.
Results may differ from the reference program's by a relative error of at most 0.015.
Values may be sent and summed in bfloat16 or wider, within the bound.
No kernel may reach another device: no remote copies, remote signals or barrier semaphores. Data moves between devices by JAX's collectives and lax.ppermute only.
A program may use at most 256 MiB of HBM per device.

```python
import math
import jax
import jax.numpy as jnp
import numpy as np
from jax import lax

D = 1024
HD = 64
FF = 4096
FRAME = 256
MB = 2
MAXF = 4
FRAMES = 16
SCENES = 8


def draw_norm_params(key, part):
    key_gain, key_bias = jax.random.split(jax.random.fold_in(key, 17))
    row_index = lax.broadcasted_iota(jnp.int32, (2, 6, D), 1)
    is_bias = jnp.logical_or(row_index == 1, row_index == 4)
    gain_draw = jax.random.uniform(key_gain, (2, 6, D), jnp.float32, 0.5, 1.5)
    bias_draw = 0.3 * jax.random.normal(key_bias, (2, 6, D), jnp.float32)
    return jnp.where(is_bias, bias_draw, gain_draw)


def with_spikes(drawn, own_key, source, target, blocks, factor):
    owner, partner = [(jnp.arange(drawn.shape[dim]) // (drawn.shape[dim] // blocks)).reshape([-1 if axis == dim else 1 for axis in range(drawn.ndim)]) for dim in (source, target)]
    chosen = jax.random.permutation(own_key, blocks)[partner]
    strong = (owner == chosen) | (owner == (partner + blocks // 2) % blocks)
    return jnp.where(strong, factor * drawn, drawn)


def shard_levels(key, extent, shards, smallest, high):
    level, own = 1.0, jax.random.fold_in(key, 6)
    for position, parts in shards:
        heights = jnp.exp(jax.random.uniform(jax.random.fold_in(own, position), (parts,), jnp.float32, smallest / len(shards), high / len(shards)))
        level = level * jnp.repeat(heights, extent[position] // parts).reshape([-1 if axis == position else 1 for axis in range(len(extent))])
    return level


def profile(number_of, total, limit, skew):
    weights = [(1 << 20) // math.isqrt(rank ** skew) + 1 for rank in range(2, number_of + 1)]
    spare, given = total - limit - (number_of - 1), [1] * (number_of - 1)
    while spare > 0:
        free = [i for i in range(number_of - 1) if given[i] < limit]
        pool, left = sum([weights[i] for i in free]), spare
        for i in free:
            extra = min(limit - given[i], max(1, left * weights[i] // pool), spare)
            given[i] = given[i] + extra
            spare = spare - extra
    return np.array([limit] + given)


def ragged(own_key, number_of, total, reach, skew):
    if number_of == 2:
        one = jax.random.randint(own_key, (), max(1, total - reach), min(reach, total - 1) + 1)
        return jnp.stack([one, total - one])
    tallies = jnp.asarray(profile(number_of, total, reach, skew), jnp.int32)
    couples = (number_of - 1) // 2
    donor, sink = tallies[1:1 + 2 * couples:2], tallies[2:2 + 2 * couples:2]
    slack = jnp.minimum(donor - 1, reach - sink)
    moved = jax.random.randint(jax.random.fold_in(own_key, 1), (couples,), 0, 1 << 20) % (slack + 1)
    tallies = tallies.at[1:1 + 2 * couples:2].set(donor - moved).at[2:2 + 2 * couples:2].set(sink + moved)
    return tallies[jax.random.permutation(jax.random.fold_in(own_key, 2), number_of)]


def gaussian(stream_key, shape, scale, bound, shards=(), kind=jnp.bfloat16):
    gain = shard_levels(stream_key, shape, shards, -0.22, 0.18) if shards else 1.0
    result = jax.random.normal(stream_key, shape, jnp.float32) * scale * gain
    return jnp.minimum(jnp.maximum(result, -bound), bound).astype(kind)


def gaussian_with(rng, dims, deviation, bound, cuts, heavy, kind=jnp.bfloat16):
    values = deviation * jax.random.normal(rng, dims, jnp.float32)
    if cuts:
        values = values * shard_levels(rng, dims, cuts, -0.22, 0.18)
    return jnp.clip(with_spikes(values, jax.random.fold_in(rng, 3), *heavy), -bound, bound).astype(kind)


def setup_inputs(seed: int = 0) -> dict:
    key_list = jax.random.split(jax.random.key(seed), 10)
    return {
        "tokens": gaussian(key_list[0], (MB, FRAMES, FRAME, D), 1.0, 6.0, ((1, 16), (2, 2))),
        "cotangent": gaussian_with(key_list[1], (MB, FRAMES, FRAME, D), 1.0, 6.0, ((1, 16), (2, 2)), (1, 3, 16, 2.0)),
        "scene_ids": jax.vmap(lambda own: jnp.searchsorted(jnp.cumsum(ragged(own, SCENES, FRAMES, MAXF, 2)), jnp.arange(FRAMES), side="right"))(jax.random.split(key_list[2], MB)).reshape((MB, FRAMES)).astype(jnp.int32),
        "input_weight": gaussian(key_list[3], (2, D, 3, D), D ** -0.5, 0.1875, ((1, 16), (3, 2))),
        "output_weight": gaussian(key_list[4], (2, D, D), (D // 32) ** -0.5, 1.0, ((1, 16), (2, 2))),
        "up_weight": gaussian(key_list[5], (2, D, FF), D ** -0.5, 0.1875, ((1, 16), (2, 2))),
        "down_weight": gaussian(key_list[6], (2, D, FF), FF ** -0.5, 0.09375, ((1, 16), (2, 2))),
        "norm_params": draw_norm_params(jax.random.fold_in(key_list[9], 71), 0),
        "head_gains": jnp.clip(1.0 + 0.1 * jax.random.normal(key_list[8], (2, 2, HD), jnp.float32), 0.5, 1.5),
    }


ROW_EPS = 1e-06
HEAD_EPS = 1e-05
NEG_FILL = -1e+30
HIGHEST = lax.Precision.HIGHEST

@jax.custom_vjp
def low(v):
    return lax.optimization_barrier(v.astype(jnp.bfloat16)).astype(jnp.float32)

@jax.custom_vjp
def low_back(v):
    return v

def low_keep(v):
    return (low(v), None)

def low_pass(kept, grad):
    return (grad,)

def back_keep(v):
    return (v, None)

def back_low(kept, grad):
    return (low(grad),)
low.defvjp(low_keep, low_pass)
low_back.defvjp(back_keep, back_low)

def layer_norm(values, gain_row, bias_row, epsilon):
    centred = values - lax.optimization_barrier(jnp.mean(values, axis=-1, keepdims=True))
    spread = lax.optimization_barrier(jnp.mean(centred * centred, axis=-1, keepdims=True))
    return centred * lax.rsqrt(spread + epsilon) * gain_row + bias_row

def row_norm(values, gain_row, bias_row):
    return layer_norm(values, gain_row, bias_row, ROW_EPS)

def head_norm(values, gain_row):
    return layer_norm(values, gain_row, 0.0, HEAD_EPS)

def attend(queries, keys_near, values_near, allowed, factor):
    scores = low_back(jnp.einsum('qhd,khd->hqk', queries, keys_near, precision=HIGHEST) * factor)
    scores = jnp.where(allowed[None, None, :], scores, NEG_FILL)
    probs = low(jax.nn.softmax(scores, axis=-1))
    return jnp.einsum('hqk,khd->qhd', probs, values_near, precision=HIGHEST)

def block(residual, weight_in, weight_out, weight_up, weight_down, vectors, head_gain, scene_row, span_frames):
    frame_total, rows_frame, model_width = residual.shape
    head_dim = head_gain.shape[1]
    head_count = model_width // head_dim
    factor = head_dim ** (-0.5)
    normed = low(row_norm(residual, vectors[0], vectors[1]))
    projected = low_back(jnp.einsum('nrd,dcf->nrcf', normed, weight_in, precision=HIGHEST))
    head_parts = projected.reshape(frame_total, rows_frame, 3, head_count, head_dim)
    queries = low(head_norm(head_parts[:, :, 0], head_gain[0]))
    keys_all = low(head_norm(head_parts[:, :, 1], head_gain[1]))
    values_all = low(head_parts[:, :, 2])
    pad_shape = ((span_frames, span_frames), (0, 0), (0, 0), (0, 0))
    padded_keys = jnp.pad(keys_all, pad_shape)
    padded_values = jnp.pad(values_all, pad_shape)
    padded_scene = jnp.pad(scene_row, (span_frames, span_frames), constant_values=-1)
    window = 2 * span_frames + 1

    def one_frame(frame_queries, frame_index):
        keys_near = lax.dynamic_slice_in_dim(padded_keys, frame_index, window, 0).reshape(window * rows_frame, head_count, head_dim)
        values_near = lax.dynamic_slice_in_dim(padded_values, frame_index, window, 0).reshape(window * rows_frame, head_count, head_dim)
        scene_near = lax.dynamic_slice_in_dim(padded_scene, frame_index, window, 0)
        centre_scene = lax.dynamic_index_in_dim(padded_scene, frame_index + span_frames, 0, keepdims=False)
        allowed = jnp.repeat(scene_near == centre_scene, rows_frame)
        return attend(frame_queries, keys_near, values_near, allowed, factor)
    checked = jax.checkpoint(one_frame)
    attended = lax.map(lambda packed: checked(packed[0], packed[1]), (queries, jnp.arange(frame_total, dtype=jnp.int32)))
    attended = low(low_back(attended)).reshape(frame_total, rows_frame, model_width)
    branch = low_back(jnp.einsum('nrf,ef->nre', attended, weight_out, precision=HIGHEST))
    residual_mid = residual + vectors[2] * branch
    normed_mid = low(row_norm(residual_mid, vectors[3], vectors[4]))
    hidden_pre = low_back(jnp.einsum('nrd,df->nrf', normed_mid, weight_up, precision=HIGHEST))
    active = low(jax.nn.gelu(hidden_pre, approximate=False))
    mlp_out = low_back(jnp.einsum('nrf,ef->nre', active, weight_down, precision=HIGHEST))
    return residual_mid + vectors[5] * mlp_out

def reference(tokens, cotangent, scene_ids, input_weight, output_weight, up_weight, down_weight, norm_params, head_gains):

    def forward(token_values, weight_in, weight_out, weight_up, weight_down, norm_values, gain_values):
        outputs = []
        for portion in range(MB):
            residual = token_values[portion]
            for layer in range(2):
                span_frames = 0 if layer == 0 else MAXF - 1
                residual = block(residual, weight_in[layer], weight_out[layer], weight_up[layer], weight_down[layer], norm_values[layer], gain_values[layer], scene_ids[portion], span_frames)
            outputs.append(residual)
        return jnp.stack(outputs)
    primals = (tokens.astype(jnp.float32), input_weight.astype(jnp.float32), output_weight.astype(jnp.float32), up_weight.astype(jnp.float32), down_weight.astype(jnp.float32), norm_params.astype(jnp.float32), head_gains.astype(jnp.float32))
    outputs, pullback = jax.vjp(forward, *primals)
    gradients = pullback(cotangent.astype(jnp.float32))
    return (outputs.astype(jnp.bfloat16), gradients[0], gradients[1], gradients[2], gradients[3], gradients[4], gradients[5], gradients[6])
```

```python
import functools

import jax
import jax.numpy as jnp
import numpy as np
from jax import lax
from jax.experimental import pallas as pl
from jax.experimental.pallas import tpu as pltpu
from jax.sharding import PartitionSpec as P

BF = jnp.bfloat16
F32 = jnp.float32
ROW_EPS = 1e-06
HEAD_EPS = 1e-05
PIECES = 16
SWAPS = 1
COST = 1
PLANE = 4
REACH = 3
AXES = ("frames", "mp")

NN = (((1,), (0,)), ((), ()))
NT = (((1,), (1,)), ((), ()))
TN = (((0,), (0,)), ((), ()))

VM = pl.BlockSpec(memory_space=pltpu.VMEM)
SM = pl.BlockSpec(memory_space=pltpu.SMEM)
ANY = pl.BlockSpec(memory_space=pl.ANY)


def dot(left, right, dims=NN):
    return lax.dot_general(left, right, dims, preferred_element_type=F32)


def call(body, outs, in_specs, out_specs, scratch, flops, moved, name):
    return pl.pallas_call(
        body,
        out_shape=outs,
        in_specs=in_specs,
        out_specs=out_specs,
        scratch_shapes=scratch,
        compiler_params=pltpu.CompilerParams(vmem_limit_bytes=60 * 1024 * 1024),
        cost_estimate=pl.CostEstimate(flops=flops // COST, bytes_accessed=moved // COST, transcendentals=0),
        name=name,
    )


class Routes:
    def __init__(self, n):
        lines = n // PLANE
        self.n, self.lines = n, lines
        order = [0] + list(range(1, lines, 2)) + sorted(range(2, lines, 2), reverse=True)
        following = {z: order[(i + 1) % lines] for i, z in enumerate(order)}
        spot = {z: i for i, z in enumerate(order)}
        self.back = np.array([[order[(spot[z] - k) % lines] for z in range(lines)] for k in range(lines)], np.int32)
        self.steps = np.array([[(spot[z] - spot[w]) % lines for w in range(lines)] for z in range(lines)], np.int32)
        self.ring = [
            (f * 2 + c, (following[f // PLANE] * PLANE + f % PLANE) * 2 + c) for f in range(n) for c in range(2)
        ]
        self.one = [(f * 2 + c, (f ^ (1 + c)) * 2 + c) for f in range(n) for c in range(2)]
        self.two = [(f * 2 + c, (f ^ (2 - c)) * 2 + c) for f in range(n) for c in range(2)]

    def send(self, block, route):
        return lax.ppermute(block, AXES, route)

    def swap(self, block):
        return lax.ppermute(block, "mp", [(0, 1), (1, 0)])

    def swap_parts(self, block):
        rows = block.shape[0] // SWAPS
        return jnp.concatenate([self.swap(block[i * rows : (i + 1) * rows]) for i in range(SWAPS)])

    def member(self, block, distance):
        return lax.ppermute(block, "frames", [(f, f ^ distance) for f in range(self.n)])

    def members(self, blocks):
        return [blocks[0]] + [self.member(blocks[d], d) for d in range(1, PLANE)]

    def up(self, block):
        return lax.ppermute(block, "frames", [(f, f + PLANE) for f in range(self.n - PLANE)])

    def down(self, block):
        return lax.ppermute(block, "frames", [(f + PLANE, f) for f in range(self.n - PLANE)])

    def tables(self):
        frame, core = lax.axis_index("frames"), lax.axis_index("mp")
        low, high = 1 + core, 2 - core
        bits = jnp.arange(2, dtype=jnp.int32)
        line = PLANE * jnp.asarray(self.back)[:, frame // PLANE]
        near = ((frame // low) % 2 ^ bits) * low
        far = ((frame // high) % 2 ^ bits) * high
        middle = line[None, :, None] + near[None, None, :] + far[:, None, None]
        first = line[None, None, :] + near[None, :, None] + far[:, None, None]
        every = jnp.arange(self.n, dtype=jnp.int32)
        k = jnp.repeat(jnp.asarray(self.steps)[frame // PLANE], PLANE)
        j = (every // low) % 2 ^ (frame // low) % 2
        h = (every // high) % 2 ^ (frame // high) % 2
        half = self.n // 2
        place_middle = h * half + k * 2 + j
        place_first = h * half + j * self.lines + k
        return [t.reshape(-1).astype(jnp.int32) for t in (middle, first, place_middle, place_first)]

    def total(self, block):
        block = block + self.swap(block)
        distance = 1
        while distance < self.n:
            block = block + self.member(block, distance)
            distance *= 2
        return block


class Clock:
    def __init__(self, active):
        self.active, self.waited = active, []

    def wait(self, *values):
        self.waited = (self.waited + list(values))[-6:]

    def late(self, value):
        if not (self.active and self.waited):
            return value
        return lax.optimization_barrier((value, self.waited))[0]


class Gather:
    def __init__(self, routes, clock, shard, line_first, name):
        self.routes, self.clock, self.near, self.line_first, self.name = routes, clock, shard, line_first, name

    def line(self):
        with jax.named_scope(self.name + "_line"):
            source = self.clock.late(self.near)
            pieces = [source]
            for _ in range(1, self.routes.lines):
                pieces.append(self.routes.send(pieces[-1], self.routes.ring))
            self.near = jnp.stack(pieces) if self.line_first else jnp.concatenate(pieces)

    def one(self):
        with jax.named_scope(self.name + "_one"):
            source = self.clock.late(self.near)
            got = self.routes.send(source, self.routes.one)
            self.near = jnp.concatenate([source, got]) if self.line_first else jnp.stack([source, got])

    def two(self):
        with jax.named_scope(self.name + "_two"):
            self.near = self.clock.late(self.near)
            self.far = self.routes.send(self.near, self.routes.two)

    def wait(self):
        self.clock.wait(self.near)

    def end(self):
        self.clock.wait(self.far)
        return self.near, self.far


class Scatter:
    def __init__(self, routes, clock, pair, line_last, name):
        self.routes, self.clock, self.line_last, self.name = routes, clock, line_last, name
        keep, give = pair
        self.shape = ((2, routes.lines) if line_last else (routes.lines, 2)) + keep.shape[1:]
        self.keep, self.give = keep.reshape(self.shape), give

    def wait(self):
        self.clock.wait(*self.last)

    def two(self):
        with jax.named_scope(self.name + "_two"):
            give = self.clock.late(self.give)
            got = self.routes.send(give, self.routes.two)
            self.last = [got]
            self.got = got.reshape(self.shape)

    def pair(self, *index):
        return self.keep[index].astype(F32) + self.got[index].astype(F32)

    def one(self):
        with jax.named_scope(self.name + "_one"):
            block = self.pair(1).astype(BF) if self.line_last else self.run[1].astype(BF)
            self.more = self.routes.send(self.clock.late(block), self.routes.one)
            self.last = [self.more]
            if not self.line_last:
                self.run = self.run[0] + self.more.astype(F32)

    def local(self, k):
        return self.pair(0, k) + self.more[k].astype(F32) if self.line_last else self.pair(k)

    def line(self):
        with jax.named_scope(self.name + "_line"):
            lines = self.routes.lines
            run = self.local(1 % lines)
            for k in range(1, lines):
                block = run.astype(BF)
                got = self.routes.send(self.clock.late(block) if k == 1 else block, self.routes.ring)
                run = self.local((k + 1) % lines) + got.astype(F32)
            self.last = [got]
            self.run = run


class Whole:
    def __init__(self, value):
        self.run = self.give = value

    def line(self):
        pass

    one = two = wait = line

    def end(self):
        return self.run


def fetch(meta, base, near, far, into, sems):
    half, rows = near.shape[0], near.shape[1]
    copies = []
    for side, source in ((0, near), (1, far)):
        for p in range(half):
            q = side * half + p
            row = pl.multiple_of(meta[base + q] * rows, rows)
            copy = pltpu.make_async_copy(source.at[p], into.at[pl.ds(row, rows), :], sems.at[q])
            copy.start()
            copies.append(copy)
    return copies


def finish(copies):
    for copy in copies:
        copy.wait()


def norm_parts(values):
    centred = values - jnp.mean(values, axis=-1, keepdims=True)
    scale = lax.rsqrt(jnp.mean(centred * centred, axis=-1, keepdims=True) + ROW_EPS)
    return centred * scale, scale


def head_matrix(width, head):
    row = lax.broadcasted_iota(jnp.int32, (width, width), 0) // head
    column = lax.broadcasted_iota(jnp.int32, (width, width), 1) // head
    return jnp.where(row == column, 1.0 / head, 0.0).astype(BF)


def head_mean(values, matrix):
    high = values.astype(BF)
    low = (values - high.astype(F32)).astype(BF)
    return dot(high, matrix) + dot(low, matrix)


def head_parts(values, matrix):
    centred = values - head_mean(values, matrix)
    scale = lax.rsqrt(head_mean(centred * centred, matrix) + HEAD_EPS)
    return centred * scale, scale


def project(normed, weight, gains, matrix, put, rows=256, lanes=256):
    width = gains.shape[1]
    total = normed.shape[0]
    factor = HEAD_SCALE

    for part in range(3):
        for start in range(0, width, lanes):
            columns = part * width + start

            @pl.loop(0, total // rows)
            def _(i):
                r = pl.ds(pl.multiple_of(i * rows, rows), rows)
                values = dot(normed[r, :], weight[:, columns : columns + lanes])
                if part < 2:
                    unit, _ = head_parts(values, matrix)
                    values = unit * gains[part : part + 1, start : start + lanes]
                values = values.astype(BF)
                if part == 0:
                    values = (values.astype(F32) * factor).astype(BF)
                put(part, r, start, lanes, values)


HEAD_SCALE = 0.125


def only_first(values):
    lane = lax.broadcasted_iota(jnp.int32, values.shape, 1)
    return jnp.where(lane < values.shape[1] // 2, values, jnp.zeros_like(values))


def only_second(values):
    lane = lax.broadcasted_iota(jnp.int32, values.shape, 1)
    return jnp.where(lane < values.shape[1] // 2, jnp.zeros_like(values), values)


def pick(first, second):
    lane = lax.broadcasted_iota(jnp.int32, first.shape, 1)
    return jnp.where(lane < first.shape[1] // 2, first, second)


def gelu_parts(v):
    size = jnp.abs(v)
    bell = jnp.exp(v * v * -0.5)
    t = 1.0 / (1.0 + size * 0.23164189)
    tail = t * (0.127414796 + t * (-0.142248368 + t * (0.7107068705 + t * (-0.7265760135 + t * 0.5307027145))))
    tail = tail * bell
    phi = jnp.where(v >= 0.0, 1.0 - tail, tail)
    return v * phi, phi + v * bell * 0.3989422804014327


def attention_frame_kernel(frame, head, meta, rows_ref, near, far, norms, gains, normed, qkv, attended, part, weight, sems):
    copies = fetch(meta, PIECES, near, far, weight, sems)
    total, model = rows_ref.shape
    width = gains.shape[1]

    @pl.loop(0, total // 64)
    def _(i):
        r = pl.ds(pl.multiple_of(i * 64, 64), 64)
        unit, _ = norm_parts(rows_ref[r, :].astype(F32))
        normed[r, :] = (unit * norms[0:1, :] + norms[1:2, :]).astype(BF)

    finish(copies)
    matrix = head_matrix(256, head)

    def put(part, r, start, lanes, values):
        qkv[part, r, start : start + lanes] = values

    project(normed, weight, gains, matrix, put)
    pairs = width // 128

    @pl.loop(0, (total // frame) * pairs)
    def _(i):
        r = pl.ds(pl.multiple_of((i // pairs) * frame, frame), frame)
        lanes = pl.ds(pl.multiple_of((i % pairs) * 128, 128), 128)
        q, k, v = qkv[0, r, lanes], qkv[1, r, lanes], qkv[2, r, lanes]
        found = []
        for mask in (only_first, only_second):
            weights = jnp.exp(dot(mask(q), k, NT))
            found.append(dot(weights.astype(BF), v) / jnp.sum(weights, axis=-1, keepdims=True))
        attended[r, lanes] = pick(found[0], found[1]).astype(BF)

    for start in range(0, model, 256):
        part[:, start : start + 256] = dot(
            attended[...], weight[start : start + 256, 3 * width : 4 * width], NT
        ).astype(BF)


def attention_frame(meta, rows, near, far, norms, gains, frame, head):
    total, model = rows.shape
    width = gains.shape[1]
    return call(
        functools.partial(attention_frame_kernel, frame, head),
        (
            jax.ShapeDtypeStruct((total, model), BF),
            jax.ShapeDtypeStruct((3, total, width), BF),
            jax.ShapeDtypeStruct((total, width), BF),
            jax.ShapeDtypeStruct((total, model), BF),
        ),
        [SM, VM, ANY, ANY, VM, VM],
        (VM, VM, VM, VM),
        [pltpu.VMEM((model, 4 * width), BF), pltpu.SemaphoreType.DMA((PIECES,))],
        8 * total * model * width,
        2 * 4 * model * width,
        "attention_frame",
    )(meta, rows, near, far, norms, gains)


def feed_up_kernel(meta, x, one, two, un, uf, norms, mid, normed, active, slope, up, sems):
    copies = fetch(meta, PIECES, un, uf, up, sems)
    total, model = x.shape
    hidden = up.shape[1]

    @pl.loop(0, total // 64)
    def _(i):
        r = pl.ds(pl.multiple_of(i * 64, 64), 64)
        branch = one[r, :].astype(F32) + two[r, :].astype(F32)
        values = x[r, :].astype(F32) + norms[2:3, :] * branch
        mid[r, :] = values
        unit, _ = norm_parts(values)
        normed[r, :] = (unit * norms[3:4, :] + norms[4:5, :]).astype(BF)

    finish(copies)
    step, rows = 512, 256
    for start in range(0, hidden, step):

        @pl.loop(0, total // rows)
        def _(i):
            r = pl.ds(pl.multiple_of(i * rows, rows), rows)
            before = dot(normed[r, :], up[:, start : start + step])
            after_, rise = gelu_parts(before)
            active[r, start : start + step] = after_.astype(BF)
            slope[r, start : start + step] = rise.astype(BF)


def feed_up(meta, x, one, two, up, norms):
    total, model = x.shape
    hidden = up[0].shape[2]
    return call(
        feed_up_kernel,
        (
            jax.ShapeDtypeStruct((total, model), F32),
            jax.ShapeDtypeStruct((total, model), BF),
            jax.ShapeDtypeStruct((total, hidden), BF),
            jax.ShapeDtypeStruct((total, hidden), BF),
        ),
        [SM, VM, VM, VM, ANY, ANY, VM],
        (VM,) * 4,
        [pltpu.VMEM((model, hidden), BF), pltpu.SemaphoreType.DMA((PIECES,))],
        2 * total * model * hidden,
        2 * model * hidden,
        "feed_up",
    )(meta, x, one, two, *up, norms)


def feed_down_kernel(meta, active, dn, df, part, down, sems):
    model = part.shape[1]
    finish(fetch(meta, 0, dn, df, down, sems))
    for start in range(0, model, 256):
        part[:, start : start + 256] = dot(active[...], down[start : start + 256, :], NT).astype(BF)


def feed_down(meta, active, down):
    total, hidden = active.shape
    model = down[0].shape[1] * PIECES
    return call(
        feed_down_kernel,
        jax.ShapeDtypeStruct((total, model), BF),
        [SM, VM, ANY, ANY],
        VM,
        [pltpu.VMEM((model, hidden), BF), pltpu.SemaphoreType.DMA((PIECES,))],
        2 * total * model * hidden,
        2 * model * hidden,
        "feed_down",
    )(meta, active, *down)


def queries_kernel(head, meta, mid, one, two, near, far, before, norms, gains, x, normed, s0, s1, s2, s3, weight, held, sems):
    copies = fetch(meta, PIECES, near, far, weight, sems)
    total, model = mid.shape
    width = gains.shape[1]
    me = meta[META_ME]

    @pl.loop(0, total // 64)
    def _(i):
        r = pl.ds(pl.multiple_of(i * 64, 64), 64)
        values = mid[r, :] + before[5:6, :] * (one[r, :].astype(F32) + two[r, :].astype(F32))
        x[r, :] = values
        unit, _ = norm_parts(values)
        normed[r, :] = (unit * norms[0:1, :] + norms[1:2, :]).astype(BF)

    finish(copies)

    def put(part, r, start, lanes, values):
        held[part, r, start : start + lanes] = values

    project(normed, weight, gains, head_matrix(256, head), put)
    for d, slot in enumerate((s0, s1, s2, s3)):
        lanes = pl.ds(pl.multiple_of((me ^ d) * 128, 128), 128)
        for part in range(3):
            slot[part] = held[part, :, lanes]


def queries(meta, mid, one, two, near, far, before, norms, gains, head):
    total, model = mid.shape
    width = gains.shape[1]
    slot = jax.ShapeDtypeStruct((3, total, 128), BF)
    return call(
        functools.partial(queries_kernel, head),
        (jax.ShapeDtypeStruct((total, model), F32), jax.ShapeDtypeStruct((total, model), BF)) + (slot,) * 4,
        [SM, VM, VM, VM, ANY, ANY, VM, VM, VM],
        (VM,) * 6,
        [
            pltpu.VMEM((model, 4 * width), BF),
            pltpu.VMEM((3, total, width), BF),
            pltpu.SemaphoreType.DMA((PIECES,)),
        ],
        6 * total * model * width,
        8 * model * width,
        "queries",
    )(meta, mid, one, two, near, far, before, norms, gains)


def edge_kernel(meta, s0, s1, s2, s3, rise, fall):
    me = meta[META_ME]
    for d, slot in enumerate((s0, s1, s2, s3)):
        j = me ^ d

        @pl.when(j >= 1)
        def _():
            rise[jnp.maximum(j - 1, 0)] = slot[1:3]

        @pl.when(j <= REACH - 1)
        def _():
            fall[jnp.minimum(j, REACH - 1)] = slot[1:3]


def edges(meta, slots):
    total = slots[0].shape[1]
    out = jax.ShapeDtypeStruct((REACH, 2, total, 128), BF)
    return call(edge_kernel, (out, out), [SM] + [VM] * 4, (VM, VM), [], 0, 4 * REACH * 2 * total * 128 * 2, "edges")(
        meta, *slots
    )


def load_window(meta, slots, below, above, own, window, sems):
    me = meta[META_ME]
    copies = []
    for d, slot in enumerate(slots):
        j = me ^ d
        copies.append(pltpu.make_async_copy(slot.at[0], own.at[j], sems.at[0, d]))
        copies.append(pltpu.make_async_copy(slot.at[pl.ds(1, 2)], window.at[REACH + j], sems.at[1, d]))
    for k in range(REACH):
        copies.append(pltpu.make_async_copy(below.at[k], window.at[k], sems.at[2, k]))
        copies.append(pltpu.make_async_copy(above.at[k], window.at[REACH + PLANE + k], sems.at[3, k]))
    for copy in copies:
        copy.start()
    return copies


def scene_kernel(frame, meta, s0, s1, s2, s3, below, above, o0, o1, o2, o3, sums, found, own, window, held, sems):
    finish(load_window(meta, (s0, s1, s2, s3), below, above, own, window, sems))
    me = meta[META_ME]
    total = own.shape[1]
    parts = total // frame

    @pl.loop(0, parts * PLANE)
    def _(i):
        m, j = i // PLANE, i % PLANE
        r = pl.ds(pl.multiple_of(m * frame, frame), frame)
        q = own[j, r, :]
        first, second = only_first(q), only_second(q)
        held[...] = jnp.zeros_like(held)

        @pl.loop(meta[META_SCENES + i * 2], meta[META_SCENES + i * 2 + 1])
        def _(w):
            k, v = window[w, 0, r, :], window[w, 1, r, :]
            one = jnp.exp(dot(first, k, NT))
            two = jnp.exp(dot(second, k, NT))
            held[0] += pick(dot(one.astype(BF), v), dot(two.astype(BF), v))
            for h, weights in ((1, one), (2, two)):
                tally = weights[:, 0:128]
                for start in range(128, frame, 128):
                    tally = tally + weights[:, start : start + 128]
                held[h] += tally

        lane = pick(
            jnp.broadcast_to(jnp.sum(held[1], axis=-1, keepdims=True), (frame, 128)),
            jnp.broadcast_to(jnp.sum(held[2], axis=-1, keepdims=True), (frame, 128)),
        )
        inverse = 1.0 / lane
        sums[j, r, :] = inverse
        found[j, r, :] = held[0] * inverse

    for d, out in enumerate((o0, o1, o2, o3)):
        out[...] = found[me ^ d].astype(BF)


def scene(meta, slots, below, above, frame):
    total = slots[0].shape[1]
    out = jax.ShapeDtypeStruct((total, 128), BF)
    wide = 2 * REACH + PLANE
    return call(
        functools.partial(scene_kernel, frame),
        (out,) * 4 + (jax.ShapeDtypeStruct((PLANE, total, 128), F32),) * 2,
        [SM] + [ANY] * 6,
        (VM,) * 6,
        [
            pltpu.VMEM((PLANE, total, 128), BF),
            pltpu.VMEM((wide, 2, total, 128), BF),
            pltpu.VMEM((3, frame, 128), F32),
            pltpu.SemaphoreType.DMA((4, PLANE)),
        ],
        4 * PLANE * total * PLANE * frame * 128 * 2,
        4 * wide * total * 128,
        "scene",
    )(meta, *slots, below, above)


def output_kernel(meta, o0, o1, o2, o3, near, far, attended, part, weight, sems):
    copies = fetch(meta, PIECES, near, far, weight, sems)
    me = meta[META_ME]
    width = attended.shape[1]
    model = part.shape[1]
    for d, slot in enumerate((o0, o1, o2, o3)):
        attended[:, pl.ds(pl.multiple_of((me ^ d) * 128, 128), 128)] = slot[...]
    finish(copies)
    for start in range(0, model, 256):
        part[:, start : start + 256] = dot(attended[...], weight[start : start + 256, :], NT).astype(BF)


def outputs(meta, slots, near, far, width):
    total = slots[0].shape[0]
    model = near.shape[1] * PIECES
    return call(
        output_kernel_narrow(width),
        (jax.ShapeDtypeStruct((total, width), BF), jax.ShapeDtypeStruct((total, model), BF)),
        [SM] + [VM] * 4 + [ANY, ANY],
        (VM, VM),
        [pltpu.VMEM((model, width), BF), pltpu.SemaphoreType.DMA((PIECES,))],
        2 * total * model * width,
        2 * model * width,
        "outputs",
    )(meta, *slots, near, far)


def output_kernel_narrow(width):
    def body(meta, o0, o1, o2, o3, near, far, *rest):
        columns = pl.ds(3 * width, width)
        output_kernel(meta, o0, o1, o2, o3, near.at[:, :, columns], far.at[:, :, columns], *rest)

    return body


def feed_back_kernel(meta, g, slope, un, uf, dn, df, norms, d_mlp, d_hidden, part, up, down, sems):
    copies = fetch(meta, 0, dn, df, down, sems.at[0])
    later = fetch(meta, PIECES, un, uf, up, sems.at[1])
    total, model = g.shape
    hidden = up.shape[1]

    @pl.loop(0, total // 64)
    def _(i):
        r = pl.ds(pl.multiple_of(i * 64, 64), 64)
        d_mlp[r, :] = (g[r, :].astype(F32) * norms[5:6, :]).astype(BF)

    finish(copies)
    step = 256
    for start in range(0, hidden, step):
        d_active = dot(d_mlp[...], down[:, start : start + step])
        d_hidden[:, start : start + step] = (d_active * slope[:, start : start + step].astype(F32)).astype(BF)
    finish(later)
    for start in range(0, model, 256):
        part[:, start : start + 256] = dot(d_hidden[...], up[start : start + 256, :], NT).astype(BF)


def feed_back(meta, g, slope, up, down, norms):
    total, model = g.shape
    hidden = slope.shape[1]
    return call(
        feed_back_kernel,
        (
            jax.ShapeDtypeStruct((total, model), BF),
            jax.ShapeDtypeStruct((total, hidden), BF),
            jax.ShapeDtypeStruct((total, model), BF),
        ),
        [SM, VM, VM, ANY, ANY, ANY, ANY, VM],
        (VM,) * 3,
        [
            pltpu.VMEM((model, hidden), BF),
            pltpu.VMEM((model, hidden), BF),
            pltpu.SemaphoreType.DMA((2, PIECES)),
        ],
        4 * total * model * hidden,
        8 * model * hidden,
        "feed_back",
    )(meta, g, slope, *up, *down, norms)


def weight_grad_kernel(base, widths, meta, *refs):
    count = len(widths)
    lefts, rights = refs[:count], refs[count : 2 * count]
    keep, give, staged, sems = refs[2 * count :]
    half, rows = keep.shape[0], keep.shape[1]
    model = lefts[0].shape[1]
    block = 256
    per = block // rows

    def copy_out(b, act):
        slot = b % 2
        for s in range(per):
            place = meta[base + b * per + s]
            source = staged.at[slot, pl.ds(s * rows, rows), :]

            @pl.when(place < half)
            def _():
                getattr(pltpu.make_async_copy(source, keep.at[jnp.minimum(place, half - 1)], sems.at[slot, s]), act)()

            @pl.when(place >= half)
            def _():
                getattr(pltpu.make_async_copy(source, give.at[jnp.maximum(place - half, 0)], sems.at[slot, s]), act)()

    for b in range(model // block):
        if b >= 2:
            copy_out(b - 2, "wait")
        start = 0
        for left, right, width in zip(lefts, rights, widths):
            staged[b % 2, :, start : start + width] = dot(
                left[:, b * block : (b + 1) * block], right[...], TN
            ).astype(BF)
            start += width
        copy_out(b, "start")
    for b in range(max(0, model // block - 2), model // block):
        copy_out(b, "wait")


def weight_grad(meta, base, lefts, rights, name):
    widths = [right.shape[1] for right in rights]
    total, model = lefts[0].shape
    rows = model // PIECES
    wide = sum(widths)
    out = jax.ShapeDtypeStruct((PIECES // 2, rows, wide), BF)
    return call(
        functools.partial(weight_grad_kernel, base, widths),
        (out, out),
        [SM] + [VM] * (2 * len(widths)),
        (ANY, ANY),
        [pltpu.VMEM((2, 256, wide), BF), pltpu.SemaphoreType.DMA((2, 256 // rows))],
        2 * total * model * wide,
        2 * model * wide + 2 * total * (model + wide),
        name,
    )(meta, *lefts, *rights)


def norm_back_kernel(frame, count, meta, *refs):
    inner = count > 2
    g, x, one, two, norms = refs[:5]
    if inner:
        pa, pb = refs[5:7]
        ma, mb = refs[7:9] if count > 3 else (None, None)
        out, d_branch, sums, tally = refs[-4:]
        gain = norms[3:4, :]
    else:
        out, sums, tally = refs[-3:]
        gain = norms[0:1, :]
    total, model = x.shape
    core = meta[META_CORE]
    rows = 64
    tally[...] = jnp.zeros_like(tally)

    @pl.loop(0, total // rows)
    def _(i):
        r = pl.ds(pl.multiple_of(i * rows, rows), rows)
        unit, scale = norm_parts(x[r, :].astype(F32))
        d = one[r, :].astype(F32) + two[r, :].astype(F32)
        dg = d * gain
        mean = jnp.mean(dg, axis=-1, keepdims=True)
        slant = jnp.mean(dg * unit, axis=-1, keepdims=True)
        before = g[r, :].astype(F32)
        after = before + scale * (dg - mean - unit * slant)
        out[r, :] = after
        if inner:
            d_branch[r, :] = (after * norms[2:3, :]).astype(BF)

        @pl.when((i // (frame // 2 // rows)) % 2 == core)
        def _():
            def add(k, values):
                tally[k] += jnp.sum(values.reshape(rows // 8, 8, model), axis=0)

            add(0, d * unit)
            add(1, d)
            if inner:
                add(2, after * (pa[r, :].astype(F32) + pb[r, :].astype(F32)))
            if count > 3:
                add(3, before * (ma[r, :].astype(F32) + mb[r, :].astype(F32)))

    sums[...] = jnp.sum(tally[...], axis=1)


def norm_back(meta, g, x, one, two, norms, frame, extra=None):
    total, model = x.shape
    inner = extra is not None
    count = 2 + len(extra) // 2 if inner else 2
    outs = [jax.ShapeDtypeStruct((total, model), F32)]
    if inner:
        outs.append(jax.ShapeDtypeStruct((total, model), BF))
    outs.append(jax.ShapeDtypeStruct((count, model), F32))
    return call(
        functools.partial(norm_back_kernel, frame, count),
        tuple(outs),
        [SM] + [VM] * (5 + len(extra or ())),
        (VM,) * len(outs),
        [pltpu.VMEM((count, 8, model), F32)],
        20 * total * model,
        16 * total * model,
        "norm_back_inner" if inner else "norm_back",
    )(meta, g, x, one, two, norms, *(extra or ()))


def project_back(normed, weight, gains, matrix, take, d_projected, sums):
    width = gains.shape[1]
    total = normed.shape[0]
    rows, lanes = 256, 256
    sums[...] = jnp.zeros_like(sums)
    for part in range(2):
        for start in range(0, width, lanes):
            columns = part * width + start

            @pl.loop(0, total // rows)
            def _(i):
                r = pl.ds(pl.multiple_of(i * rows, rows), rows)
                unit, scale = head_parts(dot(normed[r, :], weight[:, columns : columns + lanes]), matrix)
                d = take(part, r, start, lanes)
                dg = d * gains[part : part + 1, start : start + lanes]
                mean = head_mean(dg, matrix)
                slant = head_mean(dg * unit, matrix)
                d_projected[r, columns : columns + lanes] = (scale * (dg - mean - unit * slant)).astype(BF)
                tally = jnp.sum((d * unit).reshape(rows // 8, 8, lanes), axis=0)
                sums[part * 8 : part * 8 + 8, start : start + lanes] += tally


def frame_back_kernel(frame, head, meta, d_branch, normed, qkv, near, far, gains, d_projected, part, sums, weight, d_att, dq, dk, sems):
    copies = fetch(meta, PIECES, near, far, weight, sems)
    total, model = normed.shape
    width = gains.shape[1]
    finish(copies)
    for start in range(0, width, 256):
        d_att[:, start : start + 256] = dot(
            d_branch[...], weight[:, 3 * width + start : 3 * width + start + 256]
        ).astype(BF)
    pairs = width // 128

    @pl.loop(0, (total // frame) * pairs)
    def _(i):
        r = pl.ds(pl.multiple_of((i // pairs) * frame, frame), frame)
        column = pl.multiple_of((i % pairs) * 128, 128)
        lanes = pl.ds(column, 128)
        q, k, v = qkv[0, r, lanes], qkv[1, r, lanes], qkv[2, r, lanes]
        d_out = d_att[r, lanes]
        found = []
        for mask in (only_first, only_second):
            weights = jnp.exp(dot(mask(q), k, NT))
            probs = weights / jnp.sum(weights, axis=-1, keepdims=True)
            d_probs = dot(mask(d_out), v, NT)
            delta = jnp.sum(probs * d_probs, axis=-1, keepdims=True)
            d_scores = (probs * (d_probs - delta)).astype(BF)
            found.append((dot(d_scores, k), dot(d_scores, q, TN), dot(probs.astype(BF), d_out, TN)))
        dq[r, lanes] = pick(found[0][0], found[1][0]) * HEAD_SCALE
        dk[r, lanes] = pick(found[0][1], found[1][1])
        d_projected[r, pl.ds(pl.multiple_of(2 * width + column, 128), 128)] = pick(found[0][2], found[1][2]).astype(BF)

    def take(which, r, start, lanes):
        return (dq, dk)[which][r, start : start + lanes]

    project_back(normed, weight, gains, head_matrix(256, head), take, d_projected, sums)
    for start in range(0, model, 256):
        part[:, start : start + 256] = dot(d_projected[...], weight[start : start + 256, 0 : 3 * width], NT).astype(BF)


def frame_back(meta, d_branch, normed, qkv, near, far, gains, frame, head):
    total, model = normed.shape
    width = gains.shape[1]
    return call(
        functools.partial(frame_back_kernel, frame, head),
        (
            jax.ShapeDtypeStruct((total, 3 * width), BF),
            jax.ShapeDtypeStruct((total, model), BF),
            jax.ShapeDtypeStruct((16, width), F32),
        ),
        [SM, VM, VM, VM, ANY, ANY, VM],
        (VM,) * 3,
        [
            pltpu.VMEM((model, 4 * width), BF),
            pltpu.VMEM((total, width), BF),
            pltpu.VMEM((total, width), F32),
            pltpu.VMEM((total, width), F32),
            pltpu.SemaphoreType.DMA((PIECES,)),
        ],
        12 * total * model * width,
        8 * model * width,
        "frame_back",
    )(meta, d_branch, normed, qkv, near, far, gains)


def attended_back_kernel(meta, d_branch, near, far, s0, s1, s2, s3, weight, held, sems):
    finish(fetch(meta, PIECES, near, far, weight, sems))
    me = meta[META_ME]
    width = weight.shape[1]
    for start in range(0, width, 256):
        held[:, start : start + 256] = dot(d_branch[...], weight[:, start : start + 256]).astype(BF)
    for d, slot in enumerate((s0, s1, s2, s3)):
        slot[...] = held[:, pl.ds(pl.multiple_of((me ^ d) * 128, 128), 128)]


def attended_back(meta, d_branch, near, far, width):
    total, model = d_branch.shape

    def body(meta, d_branch, near, far, *rest):
        columns = pl.ds(3 * width, width)
        attended_back_kernel(meta, d_branch, near.at[:, :, columns], far.at[:, :, columns], *rest)

    return call(
        body,
        (jax.ShapeDtypeStruct((total, 128), BF),) * 4,
        [SM, VM, ANY, ANY],
        (VM,) * 4,
        [
            pltpu.VMEM((model, width), BF),
            pltpu.VMEM((total, width), BF),
            pltpu.SemaphoreType.DMA((PIECES,)),
        ],
        2 * total * model * width,
        2 * model * width,
        "attended_back",
    )(meta, d_branch, near, far)


def scene_back_kernel(frame, meta, s0, s1, s2, s3, below, above, sums, whole, g0, g1, g2, g3, q0, q1, q2, q3, d_own, d_below, d_above, own, window, d_out, delta, dq, d_window, sems, more):
    copies = load_window(meta, (s0, s1, s2, s3), below, above, own, window, sems)
    me = meta[META_ME]
    for d, slot in enumerate((g0, g1, g2, g3)):
        copies.append(pltpu.make_async_copy(slot, d_out.at[me ^ d], more.at[d]))
        copies[-1].start()
    d_window[...] = jnp.zeros_like(d_window)
    finish(copies)
    total = own.shape[1]
    parts = total // frame

    @pl.loop(0, parts * PLANE)
    def _(i):
        m, j = i // PLANE, i % PLANE
        r = pl.ds(pl.multiple_of(m * frame, frame), frame)
        q, go = own[j, r, :], d_out[j, r, :]
        product = go.astype(F32) * whole[j, r, :]
        inverse = sums[j, r, :]
        heads = []
        for mask, lane in ((only_first, 0), (only_second, 64)):
            heads.append(
                (mask(q), mask(go), inverse[:, lane : lane + 1], jnp.sum(mask(product), axis=-1, keepdims=True))
            )
        dq[...] = jnp.zeros_like(dq)

        @pl.loop(meta[META_SCENES + i * 2], meta[META_SCENES + i * 2 + 1])
        def _(w):
            k, v = window[w, 0, r, :], window[w, 1, r, :]
            found = []
            for head_q, head_go, scale, shift in heads:
                probs = jnp.exp(dot(head_q, k, NT)) * scale
                d_scores = (probs * (dot(head_go, v, NT) - shift)).astype(BF)
                found.append((dot(d_scores, k), dot(d_scores, q, TN), dot(probs.astype(BF), go, TN)))
            dq[...] += pick(found[0][0], found[1][0])
            d_window[w, 0, r, :] += pick(found[0][1], found[1][1])
            d_window[w, 1, r, :] += pick(found[0][2], found[1][2])

        delta[j, r, :] = dq[...] * HEAD_SCALE

    for d, out in enumerate((q0, q1, q2, q3)):
        out[...] = delta[me ^ d].astype(BF)
    for k in range(PLANE):
        d_own[k] = d_window[REACH + k]
    for k in range(REACH):
        d_below[k] = d_window[k].astype(BF)
        d_above[k] = d_window[REACH + PLANE + k].astype(BF)


def scene_back(meta, slots, below, above, sums, found, d_found, frame):
    total = slots[0].shape[1]
    wide = 2 * REACH + PLANE
    out = jax.ShapeDtypeStruct((total, 128), BF)
    edge = jax.ShapeDtypeStruct((REACH, 2, total, 128), BF)
    return call(
        functools.partial(scene_back_kernel, frame),
        (out,) * 4 + (jax.ShapeDtypeStruct((PLANE, 2, total, 128), F32), edge, edge),
        [SM] + [ANY] * 6 + [VM] * 2 + [ANY] * 4,
        (VM,) * 7,
        [
            pltpu.VMEM((PLANE, total, 128), BF),
            pltpu.VMEM((wide, 2, total, 128), BF),
            pltpu.VMEM((PLANE, total, 128), BF),
            pltpu.VMEM((PLANE, total, 128), F32),
            pltpu.VMEM((frame, 128), F32),
            pltpu.VMEM((wide, 2, total, 128), F32),
            pltpu.SemaphoreType.DMA((4, PLANE)),
            pltpu.SemaphoreType.DMA((PLANE,)),
        ],
        10 * PLANE * total * PLANE * frame * 128 * 2,
        8 * wide * total * 128,
        "scene_back",
    )(meta, *slots, below, above, sums, found, *d_found)


def edge_sum_kernel(meta, d_own, from_below, from_above, t0, t1, t2, t3):
    me = meta[META_ME]
    for d, out in enumerate((t0, t1, t2, t3)):
        j = me ^ d
        low = jnp.where(j <= REACH - 1, 1.0, 0.0)
        high = jnp.where(j >= 1, 1.0, 0.0)
        at, top = jnp.minimum(j, REACH - 1), jnp.maximum(j - 1, 0)
        for part in range(2):
            values = d_own[j, part] + low * from_below[at, part].astype(F32)
            out[part] = (values + high * from_above[top, part].astype(F32)).astype(BF)


def edge_sum(meta, d_own, from_below, from_above):
    total = d_own.shape[2]
    out = jax.ShapeDtypeStruct((2, total, 128), BF)
    return call(
        edge_sum_kernel,
        (out,) * 4,
        [SM, VM, VM, VM],
        (VM,) * 4,
        [],
        8 * PLANE * total * 128,
        20 * PLANE * total * 128,
        "edge_sum",
    )(meta, d_own, from_below, from_above)


def queries_back_kernel(head, meta, q0, q1, q2, q3, t0, t1, t2, t3, normed, near, far, gains, d_projected, part, sums, weight, dq, dk, sems):
    copies = fetch(meta, PIECES, near, far, weight, sems)
    me = meta[META_ME]
    model = normed.shape[1]
    width = gains.shape[1]
    for d, (query, pair) in enumerate(zip((q0, q1, q2, q3), (t0, t1, t2, t3))):
        column = pl.multiple_of((me ^ d) * 128, 128)
        dq[:, pl.ds(column, 128)] = query[...].astype(F32)
        dk[:, pl.ds(column, 128)] = pair[0].astype(F32)
        d_projected[:, pl.ds(pl.multiple_of(2 * width + column, 128), 128)] = pair[1]
    finish(copies)

    def take(which, r, start, lanes):
        return (dq, dk)[which][r, start : start + lanes]

    project_back(normed, weight, gains, head_matrix(256, head), take, d_projected, sums)
    for start in range(0, model, 256):
        part[:, start : start + 256] = dot(d_projected[...], weight[start : start + 256, 0 : 3 * width], NT).astype(BF)


def queries_back(meta, d_queries, d_pairs, normed, near, far, gains, head):
    total, model = normed.shape
    width = gains.shape[1]
    return call(
        functools.partial(queries_back_kernel, head),
        (
            jax.ShapeDtypeStruct((total, 3 * width), BF),
            jax.ShapeDtypeStruct((total, model), BF),
            jax.ShapeDtypeStruct((16, width), F32),
        ),
        [SM] + [VM] * 9 + [ANY, ANY, VM],
        (VM,) * 3,
        [
            pltpu.VMEM((model, 4 * width), BF),
            pltpu.VMEM((total, width), F32),
            pltpu.VMEM((total, width), F32),
            pltpu.SemaphoreType.DMA((PIECES,)),
        ],
        10 * total * model * width,
        8 * model * width,
        "queries_back",
    )(meta, *d_queries, *d_pairs, normed, near, far, gains)


META_CORE = 4 * PIECES
META_ME = META_CORE + 1
META_SCENES = META_ME + 1


def body(tokens, cotangent, scene_ids, input_weight, output_weight, up_weight, down_weight, norm_params, head_gains):
    portions, _, share, model = tokens.shape
    frame = 2 * share
    total = portions * frame
    head = head_gains.shape[2]
    width = input_weight.shape[3]
    routes = Routes(lax.axis_size("frames"))
    n = routes.n
    index, core = lax.axis_index("frames"), lax.axis_index("mp")
    plain = n != PIECES

    identity = jnp.arange(PIECES, dtype=jnp.int32)
    tables = [identity] * 4 if plain else routes.tables()
    scene_here = scene_ids[:, (index // PLANE) * PLANE + jnp.arange(PLANE)]
    before = jnp.sum(scene_ids[:, None, :] < scene_here[:, :, None], axis=-1)
    until = jnp.sum(scene_ids[:, None, :] <= scene_here[:, :, None], axis=-1)
    spans = jnp.stack([before, until], axis=-1) - (index // PLANE) * PLANE + REACH
    meta = jnp.concatenate(
        [*tables, core[None], (index % PLANE)[None], spans.reshape(-1)]
    ).astype(jnp.int32)

    def all_rows(block):
        own = block[:, 0]
        other = routes.swap(own)
        both = jnp.where(core == 0, jnp.stack([own, other], 1), jnp.stack([other, own], 1))
        return both.reshape(total, model)

    def own_rows(values):
        return lax.dynamic_index_in_dim(values.reshape(portions, 2, share, -1), core, 1, keepdims=True)

    shards = []
    for layer in range(2):
        joined = jnp.concatenate(
            [input_weight[layer].reshape(-1, 3 * width), output_weight[layer]], axis=1
        )
        shards.append((joined, up_weight[layer], down_weight[layer]))
    gains = [jnp.tile(head_gains[layer], (1, width // head)) for layer in range(2)]

    def whole(shard):
        gathered = lax.all_gather(shard, "frames", axis=0, tiled=True).reshape(PIECES, -1, shard.shape[1])
        return gathered[: PIECES // 2], gathered[PIECES // 2 :]

    clock = Clock(False)
    names = ("input", "up", "down")
    kinds = (True, True, False)
    if not plain:
        (ga0, gu0, gd0), (ga1, gu1, gd1) = [
            [Gather(routes, clock, shard, kinds[at], names[at] + str(layer)) for at, shard in enumerate(shards[layer])]
            for layer in range(2)
        ]
    else:
        (ga0, gu0, gd0), (ga1, gu1, gd1) = [[Whole(whole(shard)) for shard in layer] for layer in shards]

    def scatter(pair, line_last, name):
        if plain:
            rows_ = jnp.concatenate(pair).reshape(model, -1).astype(F32)
            return Whole(lax.psum_scatter(rows_, "frames", scatter_dimension=0, tiled=True))
        return Scatter(routes, clock, pair, line_last, name)

    late, wait = clock.late, clock.wait

    ga0.line()
    gd0.one()
    gd1.one()
    rows = all_rows(tokens)
    d_result = all_rows(cotangent)
    ga0.wait()
    gd0.wait()
    gd1.wait()
    wait(rows, d_result)
    ga0.one()
    gu0.line()
    ga0.wait()
    ga0.two()
    gu0.wait()
    gd0.line()
    w0 = ga0.end()
    gu0.one()
    normed0, qkv0, attended0, a0 = attention_frame(
        meta, late(rows), *w0, norm_params[0], gains[0], frame, head
    )
    wait(a0)
    b0 = routes.swap_parts(a0)
    gu0.wait()
    gu0.two()
    gd0.wait()
    wait(b0)
    ga1.line()
    up0 = gu0.end()
    gd0.two()
    mid0, normed_mid0, active0, slope0 = feed_up(meta, rows, a0, late(b0), up0, norm_params[0])
    wait(active0)
    ga1.wait()
    gu1.line()
    down0 = gd0.end()
    ga1.one()
    m0 = feed_down(meta, late(active0), down0)
    wait(m0)
    n0 = routes.swap_parts(m0)
    wait(n0)
    ga1.wait()
    ga1.two()
    gu1.wait()
    gd1.line()
    w1 = ga1.end()
    gu1.one()
    x1, normed1, *slots = queries(
        meta, mid0, m0, late(n0), *w1, norm_params[0], norm_params[1], gains[1], head
    )
    wait(slots[0])
    gu1.wait()
    slots = routes.members(slots)
    wait(*slots[1:])
    rise, fall = edges(meta, slots)
    below, above = routes.up(rise), routes.down(fall)
    gu1.two()
    wait(below, above)
    gd1.wait()
    *found, sums, whole_found = scene(meta, slots, late(below), above, frame)
    home = routes.members(found)
    up1 = gu1.end()
    gd1.two()
    wait(*home[1:])
    attended1, a1 = outputs(meta, late(home), *w1, width)
    b1 = routes.swap_parts(a1)
    mid1, normed_mid1, active1, slope1 = feed_up(meta, x1, a1, b1, up1, norm_params[1])
    wait(active1)
    down1 = gd1.end()

    d_mlp, d_hidden, p = feed_back(meta, late(d_result), slope1, up1, down1, norm_params[1])
    wait(p)
    q = routes.swap_parts(p)
    sd1 = scatter(weight_grad(meta, 3 * PIECES, [late(d_mlp)], [active1], "down_grad"), True, "down_grad1")
    sd1.two()
    wait(q)
    g, d_branch, inner1 = norm_back(meta, d_result, mid1, p, late(q), norm_params[1], frame, (a1, b1))
    d_home = attended_back(meta, d_branch, *w1, width)
    wait(d_home[0])
    d_found = routes.members(d_home)
    su1 = scatter(weight_grad(meta, 2 * PIECES, [normed_mid1], [late(d_hidden)], "up_grad"), False, "up_grad1")
    wait(su1.give, *d_found[1:])
    sd1.wait()
    sd1.one()
    su1.two()
    *d_queries, d_own, d_below, d_above = scene_back(
        meta, slots, late(below), above, sums, whole_found, d_found, frame
    )
    wait(d_own)
    from_above, from_below = routes.down(d_below), routes.up(d_above)
    sd1.wait()
    su1.wait()
    sd1.line()
    d_queries = routes.members(d_queries)
    m1 = feed_down(meta, late(active1), down1)
    n1 = routes.swap_parts(m1)
    own_mlp = own_rows(m1).astype(F32) + own_rows(n1).astype(F32)
    result = own_rows(mid1) + norm_params[1, 5] * own_mlp
    scale1 = jnp.sum(cotangent.astype(F32).reshape(-1, model) * own_mlp.reshape(-1, model), axis=0)
    wait(m1, from_below, from_above)
    pairs = routes.members(edge_sum(meta, d_own, late(from_below), from_above))
    wait(*pairs[1:])
    wait(*d_queries[1:])
    su1.line()
    sd1.wait()
    d_projected, p, gain1 = queries_back(meta, d_queries, late(pairs), normed1, *w1, gains[1], head)
    wait(p)
    q = routes.swap_parts(p)
    sa1 = scatter(
        weight_grad(meta, 2 * PIECES, [normed1, d_branch], [late(d_projected), attended1], "input_grad"),
        False,
        "input_grad1",
    )
    sa1.two()
    wait(q)
    g, outer1 = norm_back(meta, g, x1, p, late(q), norm_params[1], frame)

    d_mlp, d_hidden, p = feed_back(meta, g, slope0, up0, down0, norm_params[0])
    wait(p)
    q = routes.swap_parts(p)
    sd0 = scatter(weight_grad(meta, 3 * PIECES, [late(d_mlp)], [active0], "down_grad"), True, "down_grad0")
    wait(sd0.give, q)
    sa1.wait()
    su1.wait()
    sd0.two()
    sa1.line()
    su1.one()
    su0 = scatter(weight_grad(meta, 3 * PIECES, [normed_mid0], [late(d_hidden)], "up_grad"), True, "up_grad0")
    g, d_branch, inner0 = norm_back(meta, g, mid0, p, q, norm_params[0], frame, (a0, b0, m0, n0))
    wait(d_branch, su0.give)
    sd0.wait()
    sd0.one()
    su0.two()
    d_projected, p, gain0 = frame_back(
        meta, late(d_branch), normed0, qkv0, *w0, gains[0], frame, head
    )
    wait(p)
    q = routes.swap_parts(p)
    sd0.wait()
    su0.wait()
    sa1.wait()
    su0.one()
    sa1.one()
    sd0.line()
    sa0 = scatter(
        weight_grad(meta, 3 * PIECES, [normed0, d_branch], [late(d_projected), attended0], "input_grad"),
        True,
        "input_grad0",
    )
    wait(sa0.give, q)
    su0.wait()
    sa0.two()
    g, outer0 = norm_back(meta, g, rows, p, late(q), norm_params[0], frame)
    token_grad = own_rows(g)
    wait(g)
    sd0.wait()
    su0.line()

    norm_rows = [
        jnp.stack([outer[0], outer[1], inner[2], inner[0], inner[1], scale])
        for outer, inner, scale in ((outer0, inner0, inner0[3]), (outer1, inner1, scale1))
    ]
    gain_rows = [
        jnp.sum(gain.reshape(2, 8, width // head, head), axis=(1, 2)).reshape(1, -1)
        for gain in (gain0, gain1)
    ]
    gain_rows = jnp.pad(jnp.concatenate(gain_rows, axis=1), ((0, 0), (0, model - 4 * head)))
    small = routes.total(jnp.concatenate([*norm_rows, gain_rows]))
    norm_grad = small[: 2 * 6].reshape(2, 6, model)
    gain_grad = small[2 * 6, : 4 * head].reshape(2, 2, head)
    wait(small)
    sa0.wait()
    sa0.one()
    su0.wait()
    sa0.wait()
    sa0.line()
    scattered = [[step.run for step in layer] for layer in ((sa0, su0, sd0), (sa1, su1, sd1))]
    return (
        result.astype(BF),
        token_grad,
        jnp.stack([scattered[layer][0][:, : 3 * width].reshape(-1, 3, width) for layer in range(2)]),
        jnp.stack([scattered[layer][0][:, 3 * width :] for layer in range(2)]),
        jnp.stack([scattered[layer][1] for layer in range(2)]),
        jnp.stack([scattered[layer][2] for layer in range(2)]),
        norm_grad,
        gain_grad,
    )


def solution(mesh):
    rows = P(None, "frames", "mp", None)
    shard = P(None, "frames", "mp")
    wide = P(None, "frames", None, "mp")
    return jax.shard_map(
        body,
        mesh=mesh,
        in_specs=(rows, rows, P(), wide, shard, shard, shard, P(), P()),
        out_specs=(rows, rows, wide, shard, shard, shard, P(), P()),
        check_vma=False,
    )
```

```python
import functools

import jax
import jax.numpy as jnp
import numpy as np
from jax import lax
from jax.experimental import pallas as pl
from jax.experimental.pallas import tpu as pltpu
from jax.sharding import PartitionSpec as P

BF = jnp.bfloat16
F32 = jnp.float32
ROW_EPS = 1e-06
HEAD_EPS = 1e-05
PIECES = 16
SWAPS = 1
COST = 1
PLANE = 4
REACH = 3
AXES = ("frames", "mp")

NN = (((1,), (0,)), ((), ()))
NT = (((1,), (1,)), ((), ()))
TN = (((0,), (0,)), ((), ()))

VM = pl.BlockSpec(memory_space=pltpu.VMEM)
SM = pl.BlockSpec(memory_space=pltpu.SMEM)
ANY = pl.BlockSpec(memory_space=pl.ANY)
HBM = pl.BlockSpec(memory_space=pltpu.HBM)


def dot(left, right, dims=NN):
    return lax.dot_general(left, right, dims, preferred_element_type=F32)


def call(body, outs, in_specs, out_specs, scratch, flops, moved, name):
    return pl.pallas_call(
        body,
        out_shape=outs,
        in_specs=in_specs,
        out_specs=out_specs,
        scratch_shapes=scratch,
        compiler_params=pltpu.CompilerParams(vmem_limit_bytes=18 * 1024 * 1024),
        cost_estimate=pl.CostEstimate(flops=flops // COST, bytes_accessed=moved // COST, transcendentals=0),
        name=name,
    )


class Routes:
    def __init__(self, n):
        lines = n // PLANE
        self.n, self.lines = n, lines
        order = [0] + list(range(1, lines, 2)) + sorted(range(2, lines, 2), reverse=True)
        following = {z: order[(i + 1) % lines] for i, z in enumerate(order)}
        spot = {z: i for i, z in enumerate(order)}
        self.back = np.array([[order[(spot[z] - k) % lines] for z in range(lines)] for k in range(lines)], np.int32)
        self.steps = np.array([[(spot[z] - spot[w]) % lines for w in range(lines)] for z in range(lines)], np.int32)
        self.ring = [
            (f * 2 + c, (following[f // PLANE] * PLANE + f % PLANE) * 2 + c) for f in range(n) for c in range(2)
        ]
        self.one = [(f * 2 + c, (f ^ (1 + c)) * 2 + c) for f in range(n) for c in range(2)]
        self.two = [(f * 2 + c, (f ^ (2 - c)) * 2 + c) for f in range(n) for c in range(2)]

    def send(self, block, route):
        return lax.ppermute(block, AXES, route)

    def swap(self, block):
        return lax.ppermute(block, "mp", [(0, 1), (1, 0)])

    def swap_parts(self, block):
        if SWAPS == 1:
            return self.swap(block)
        rows = block.shape[0] // SWAPS
        return jnp.concatenate([self.swap(block[i * rows : (i + 1) * rows]) for i in range(SWAPS)])

    def member(self, block, distance):
        return lax.ppermute(block, "frames", [(f, f ^ distance) for f in range(self.n)])

    def members(self, blocks):
        return [blocks[0]] + [self.member(blocks[d], d) for d in range(1, PLANE)]

    def up(self, block):
        return lax.ppermute(block, "frames", [(f, f + PLANE) for f in range(self.n - PLANE)])

    def down(self, block):
        return lax.ppermute(block, "frames", [(f + PLANE, f) for f in range(self.n - PLANE)])

    def tables(self):
        frame, core = lax.axis_index("frames"), lax.axis_index("mp")
        low, high = 1 + core, 2 - core
        bits = jnp.arange(2, dtype=jnp.int32)
        line = PLANE * jnp.asarray(self.back)[:, frame // PLANE]
        straight = PLANE * (frame // PLANE ^ jnp.arange(self.lines, dtype=jnp.int32))
        near = ((frame // low) % 2 ^ bits) * low
        far = ((frame // high) % 2 ^ bits) * high
        middle = line[None, :, None] + near[None, None, :] + far[:, None, None]
        first = line[None, None, :] + near[None, :, None] + far[:, None, None]
        direct = straight[None, None, :] + near[None, :, None] + far[:, None, None]
        every = jnp.arange(self.n, dtype=jnp.int32)
        k = jnp.repeat(jnp.asarray(self.steps)[frame // PLANE], PLANE)
        j = (every // low) % 2 ^ (frame // low) % 2
        h = (every // high) % 2 ^ (frame // high) % 2
        half = self.n // 2
        place_middle = h * half + k * 2 + j
        place_first = h * half + j * self.lines + k
        return [t.reshape(-1).astype(jnp.int32) for t in (middle, first, place_middle, place_first, direct)]


class Clock:
    def __init__(self, active):
        self.active, self.waited, self.pending = active, [], []

    def late(self, value):
        if not (self.active and self.waited):
            return value
        return lax.optimization_barrier((value, self.waited))[0]

    def add(self, value):
        self.pending.append(value)
        return value

    def close(self, *values):
        self.waited, self.pending = self.pending + list(values), []


class Gather:
    def __init__(self, routes, clock, shard, line_first, name):
        self.routes, self.clock, self.line_first, self.name = routes, clock, line_first, name
        self.shard, self.pieces, self.direct = shard, [shard], False

    def send(self, block, route, step):
        with jax.named_scope(self.name + step):
            return self.clock.add(self.routes.send(self.clock.late(block), route))

    def ring(self, steps=1):
        for i in range(steps):
            if i:
                moved = self.routes.send(self.pieces[-1], self.routes.ring)
                self.clock.pending[-1] = moved
            else:
                moved = self.send(self.pieces[-1], self.routes.ring, "_ring")
            self.pieces.append(moved)
        if self.line_first and len(self.pieces) == self.routes.lines:
            self.line = jnp.stack(self.pieces)

    def straight(self):
        self.direct = True
        for k in range(1, self.routes.lines):
            with jax.named_scope(self.name + "_line"):
                self.pieces.append(self.clock.add(self.routes.member(self.clock.late(self.shard), PLANE * k)))
        self.line = jnp.stack(self.pieces)

    def one(self):
        if self.line_first:
            self.got = self.send(self.line, self.routes.one, "_one")
        else:
            self.pieces = [jnp.stack([self.shard, self.send(self.shard, self.routes.one, "_one")])]

    def near(self, half):
        if self.line_first:
            return (self.line, self.got)[half]
        if not hasattr(self, "pairs"):
            self.pairs = {}
        if half not in self.pairs:
            self.pairs[half] = jnp.concatenate(self.pieces[2 * half : 2 * half + 2])
        return self.pairs[half]

    def two(self, half):
        far = self.send(self.near(half), self.routes.two, "_two")
        self.far = (self.far if half else []) + [far]

    def end(self, start=0, width=None):
        sources = [self.near(0), self.near(1), *self.far]
        base = (4 if self.direct else 1) * PIECES if self.line_first else 0
        return Weight(sources, base, start, width)


class Scatter:
    def __init__(self, routes, clock, parts, line_last, name):
        self.routes, self.clock, self.line_last, self.name = routes, clock, line_last, name
        self.keep, self.give = parts[:2], parts[2:]
        self.got, self.at, self.run = [None, None], 0, None

    def send(self, block, route, step):
        with jax.named_scope(self.name + step):
            return self.clock.add(self.routes.send(self.clock.late(block), route))

    def two(self, half):
        self.got[half] = self.send(self.give[half], self.routes.two, "_two")

    def one(self):
        if self.line_last:
            block = self.keep[1].astype(F32) + self.got[1].astype(F32)
            self.more = self.send(block.astype(BF), self.routes.one, "_one")
        else:
            self.run = self.run[0] + self.send(self.run[1].astype(BF), self.routes.one, "_one").astype(F32)

    def local(self, k):
        if self.line_last:
            return self.keep[0][k].astype(F32) + self.got[0][k].astype(F32) + self.more[k].astype(F32)
        half, rows = k // 2, slice(2 * (k % 2), 2 * (k % 2) + 2)
        return self.keep[half][rows].astype(F32) + self.got[half][rows].astype(F32)

    def ring(self):
        if self.run is None:
            self.at, self.run = 1, self.local(1)
        moved = self.send(self.run.astype(BF), self.routes.ring, "_ring")
        self.at = (self.at + 1) % self.routes.lines
        self.run = self.local(self.at) + moved.astype(F32)


class Weight:
    def __init__(self, sources, base, start=0, width=None):
        self.sources, self.count = tuple(sources), len(sources)
        self.width = width or self.sources[0].shape[-1]
        self.plan = (base, start, self.width)


class Whole:
    def __init__(self, value):
        self.run = value

    def ring(self, steps=1):
        pass

    def one(self):
        pass

    def straight(self):
        pass

    def two(self, half):
        pass

    def end(self, start=0, width=None):
        return Weight([self.run], None, start, width)


def with_weights(kernel, before, weights):
    def run(*refs):
        at = before
        given = []
        for weight in weights:
            given.append((weight.plan, refs[at : at + weight.count]))
            at += weight.count
        return kernel(*refs[:before], *given, *refs[at:])

    return run


def sources_of(weights):
    return [source for weight in weights for source in weight.sources]


def fetch(meta, plan, sources, into, sems):
    base, start, width = plan
    columns = pl.ds(start, width)
    copies = []
    if base is None:
        rows = into.shape[0] // 4
        for q in range(4):
            part = pl.ds(q * rows, rows)
            copies.append(pltpu.make_async_copy(sources[0].at[part, columns], into.at[part, :], sems.at[q]))
    else:
        rows, quarter = into.shape[0] // PIECES, PIECES // 4
        for q in range(PIECES):
            source = sources[q // quarter].at[q % quarter, :, columns]
            row = pl.multiple_of(meta[base + q] * rows, rows)
            copies.append(pltpu.make_async_copy(source, into.at[pl.ds(row, rows), :], sems.at[q]))
    for copy in copies:
        copy.start()
    return copies


def finish(copies):
    for copy in copies:
        copy.wait()


def norm_parts(values):
    centred = values - jnp.mean(values, axis=-1, keepdims=True)
    scale = lax.rsqrt(jnp.mean(centred * centred, axis=-1, keepdims=True) + ROW_EPS)
    return centred * scale, scale


def head_matrix(width, head):
    row = lax.broadcasted_iota(jnp.int32, (width, width), 0) // head
    column = lax.broadcasted_iota(jnp.int32, (width, width), 1) // head
    return jnp.where(row == column, 1.0 / head, 0.0).astype(BF)


def head_mean(values, matrix):
    high = values.astype(BF)
    low = (values - high.astype(F32)).astype(BF)
    return dot(high, matrix) + dot(low, matrix)


def head_parts(values, matrix):
    centred = values - head_mean(values, matrix)
    scale = lax.rsqrt(head_mean(centred * centred, matrix) + HEAD_EPS)
    return centred * scale, scale


def project(normed, weight, gains, matrix, put, rows=256, lanes=256):
    width = gains.shape[1]
    total = normed.shape[0]
    factor = HEAD_SCALE

    for part in range(3):
        for start in range(0, width, lanes):
            columns = part * width + start

            @pl.loop(0, total // rows)
            def _(i):
                r = pl.ds(pl.multiple_of(i * rows, rows), rows)
                values = dot(normed[r, :], weight[:, columns : columns + lanes])
                if part < 2:
                    unit, _ = head_parts(values, matrix)
                    values = unit * gains[part : part + 1, start : start + lanes]
                values = values.astype(BF)
                if part == 0:
                    values = (values.astype(F32) * factor).astype(BF)
                put(part, r, start, lanes, values)


HEAD_SCALE = 0.125


def only_first(values):
    lane = lax.broadcasted_iota(jnp.int32, values.shape, 1)
    return jnp.where(lane < values.shape[1] // 2, values, jnp.zeros_like(values))


def only_second(values):
    lane = lax.broadcasted_iota(jnp.int32, values.shape, 1)
    return jnp.where(lane < values.shape[1] // 2, jnp.zeros_like(values), values)


def pick(first, second):
    lane = lax.broadcasted_iota(jnp.int32, first.shape, 1)
    return jnp.where(lane < first.shape[1] // 2, first, second)


def gelu_parts(v):
    size = jnp.abs(v)
    bell = jnp.exp(v * v * -0.5)
    t = 1.0 / (1.0 + size * 0.23164189)
    tail = t * (0.127414796 + t * (-0.142248368 + t * (0.7107068705 + t * (-0.7265760135 + t * 0.5307027145))))
    tail = tail * bell
    phi = jnp.where(v >= 0.0, 1.0 - tail, tail)
    return v * phi, phi + v * bell * 0.3989422804014327


def attention_frame_kernel(frame, head, meta, w_in, w_out, rows_ref, norms, gains, normed, qkv, attended, part, weight, out, sems):
    copies = fetch(meta, *w_in, weight, sems.at[0])
    later = fetch(meta, *w_out, out, sems.at[1])
    total, model = rows_ref.shape
    width = gains.shape[1]

    @pl.loop(0, total // 64)
    def _(i):
        r = pl.ds(pl.multiple_of(i * 64, 64), 64)
        unit, _ = norm_parts(rows_ref[r, :].astype(F32))
        normed[r, :] = (unit * norms[0:1, :] + norms[1:2, :]).astype(BF)

    finish(copies)
    matrix = head_matrix(256, head)

    def put(part, r, start, lanes, values):
        qkv[part, r, start : start + lanes] = values

    project(normed, weight, gains, matrix, put)
    pairs = width // 128

    @pl.loop(0, (total // frame) * pairs)
    def _(i):
        r = pl.ds(pl.multiple_of((i // pairs) * frame, frame), frame)
        lanes = pl.ds(pl.multiple_of((i % pairs) * 128, 128), 128)
        q, k, v = qkv[0, r, lanes], qkv[1, r, lanes], qkv[2, r, lanes]
        found = []
        for mask in (only_first, only_second):
            weights = jnp.exp(dot(mask(q), k, NT))
            found.append(dot(weights.astype(BF), v) / jnp.sum(weights, axis=-1, keepdims=True))
        attended[r, lanes] = pick(found[0], found[1]).astype(BF)

    finish(later)
    for start in range(0, model, 256):
        part[:, start : start + 256] = dot(attended[...], out[start : start + 256, :], NT).astype(BF)


def attention_frame(meta, weights, rows, norms, gains, frame, head):
    total, model = rows.shape
    width = gains.shape[1]
    sources = sources_of(weights)
    return call(
        with_weights(functools.partial(attention_frame_kernel, frame, head), 1, weights),
        (
            jax.ShapeDtypeStruct((total, model), BF),
            jax.ShapeDtypeStruct((3, total, width), BF),
            jax.ShapeDtypeStruct((total, width), BF),
            jax.ShapeDtypeStruct((total, model), BF),
        ),
        [SM] + [HBM] * len(sources) + [VM, VM, VM],
        (VM, VM, VM, VM),
        [
            pltpu.VMEM((model, 3 * width), BF),
            pltpu.VMEM((model, width), BF),
            pltpu.SemaphoreType.DMA((2, PIECES)),
        ],
        8 * total * model * width,
        2 * 4 * model * width,
        "attention_frame",
    )(meta, *sources, rows, norms, gains)


def feed_up_kernel(meta, w_up, x, one, two, norms, mid, normed, active, slope, up, sems):
    copies = fetch(meta, *w_up, up, sems)
    total, model = x.shape
    hidden = up.shape[1]

    @pl.loop(0, total // 64)
    def _(i):
        r = pl.ds(pl.multiple_of(i * 64, 64), 64)
        branch = one[r, :].astype(F32) + two[r, :].astype(F32)
        values = x[r, :].astype(F32) + norms[2:3, :] * branch
        mid[r, :] = values
        unit, _ = norm_parts(values)
        normed[r, :] = (unit * norms[3:4, :] + norms[4:5, :]).astype(BF)

    finish(copies)
    step, rows = 512, 256
    for start in range(0, hidden, step):

        @pl.loop(0, total // rows)
        def _(i):
            r = pl.ds(pl.multiple_of(i * rows, rows), rows)
            before = dot(normed[r, :], up[:, start : start + step])
            after_, rise = gelu_parts(before)
            active[r, start : start + step] = after_.astype(BF)
            slope[r, start : start + step] = rise.astype(BF)


def feed_up(meta, up, x, one, two, norms):
    total, model = x.shape
    hidden = up.width
    return call(
        with_weights(feed_up_kernel, 1, [up]),
        (
            jax.ShapeDtypeStruct((total, model), F32),
            jax.ShapeDtypeStruct((total, model), BF),
            jax.ShapeDtypeStruct((total, hidden), BF),
            jax.ShapeDtypeStruct((total, hidden), BF),
        ),
        [SM] + [HBM] * up.count + [VM] * 4,
        (VM,) * 4,
        [pltpu.VMEM((model, hidden), BF), pltpu.SemaphoreType.DMA((PIECES,))],
        2 * total * model * hidden,
        2 * model * hidden,
        "feed_up",
    )(meta, *up.sources, x, one, two, norms)


def feed_down_kernel(meta, w_down, active, part, down, sems):
    model = part.shape[1]
    finish(fetch(meta, *w_down, down, sems))
    for start in range(0, model, 256):
        part[:, start : start + 256] = dot(active[...], down[start : start + 256, :], NT).astype(BF)


def feed_down(meta, down, active, model):
    total, hidden = active.shape
    return call(
        with_weights(feed_down_kernel, 1, [down]),
        jax.ShapeDtypeStruct((total, model), BF),
        [SM] + [HBM] * down.count + [VM],
        VM,
        [pltpu.VMEM((model, hidden), BF), pltpu.SemaphoreType.DMA((PIECES,))],
        2 * total * model * hidden,
        2 * model * hidden,
        "feed_down",
    )(meta, *down.sources, active)


def queries_kernel(head, meta, w_in, mid, one, two, before, norms, gains, x, normed, s0, s1, s2, s3, weight, held, sems):
    copies = fetch(meta, *w_in, weight, sems)
    total, model = mid.shape
    width = gains.shape[1]
    me = meta[META_ME]

    @pl.loop(0, total // 64)
    def _(i):
        r = pl.ds(pl.multiple_of(i * 64, 64), 64)
        values = mid[r, :] + before[5:6, :] * (one[r, :].astype(F32) + two[r, :].astype(F32))
        x[r, :] = values
        unit, _ = norm_parts(values)
        normed[r, :] = (unit * norms[0:1, :] + norms[1:2, :]).astype(BF)

    finish(copies)

    def put(part, r, start, lanes, values):
        held[part, r, start : start + lanes] = values

    project(normed, weight, gains, head_matrix(256, head), put)
    for d, slot in enumerate((s0, s1, s2, s3)):
        lanes = pl.ds(pl.multiple_of((me ^ d) * 128, 128), 128)
        for part in range(3):
            slot[part] = held[part, :, lanes]


def queries(meta, w_in, mid, one, two, before, norms, gains, head):
    total, model = mid.shape
    width = gains.shape[1]
    slot = jax.ShapeDtypeStruct((3, total, 128), BF)
    return call(
        with_weights(functools.partial(queries_kernel, head), 1, [w_in]),
        (jax.ShapeDtypeStruct((total, model), F32), jax.ShapeDtypeStruct((total, model), BF)) + (slot,) * 4,
        [SM] + [HBM] * w_in.count + [VM] * 6,
        (VM,) * 6,
        [
            pltpu.VMEM((model, 3 * width), BF),
            pltpu.VMEM((3, total, width), BF),
            pltpu.SemaphoreType.DMA((PIECES,)),
        ],
        6 * total * model * width,
        8 * model * width,
        "queries",
    )(meta, *w_in.sources, mid, one, two, before, norms, gains)


def edge_kernel(meta, s0, s1, s2, s3, rise, fall):
    me = meta[META_ME]
    for d, slot in enumerate((s0, s1, s2, s3)):
        j = me ^ d

        @pl.when(j >= 1)
        def _():
            rise[jnp.maximum(j - 1, 0)] = slot[1:3]

        @pl.when(j <= REACH - 1)
        def _():
            fall[jnp.minimum(j, REACH - 1)] = slot[1:3]


def edges(meta, slots):
    total = slots[0].shape[1]
    out = jax.ShapeDtypeStruct((REACH, 2, total, 128), BF)
    return call(edge_kernel, (out, out), [SM] + [VM] * 4, (VM, VM), [], 0, 4 * REACH * 2 * total * 128 * 2, "edges")(
        meta, *slots
    )


def load_window(meta, slots, below, above, own, window, sems):
    me = meta[META_ME]
    copies = []
    for d, slot in enumerate(slots):
        j = me ^ d
        copies.append(pltpu.make_async_copy(slot.at[0], own.at[j], sems.at[0, d]))
        copies.append(pltpu.make_async_copy(slot.at[pl.ds(1, 2)], window.at[REACH + j], sems.at[1, d]))
    for k in range(REACH):
        copies.append(pltpu.make_async_copy(below.at[k], window.at[k], sems.at[2, k]))
        copies.append(pltpu.make_async_copy(above.at[k], window.at[REACH + PLANE + k], sems.at[3, k]))
    for copy in copies:
        copy.start()
    return copies


def scene_kernel(frame, meta, s0, s1, s2, s3, below, above, o0, o1, o2, o3, sums, found, own, window, held, sems):
    finish(load_window(meta, (s0, s1, s2, s3), below, above, own, window, sems))
    me = meta[META_ME]
    total = own.shape[1]
    parts = total // frame

    @pl.loop(0, parts * PLANE)
    def _(i):
        m, j = i // PLANE, i % PLANE
        r = pl.ds(pl.multiple_of(m * frame, frame), frame)
        q = own[j, r, :]
        first, second = only_first(q), only_second(q)
        held[...] = jnp.zeros_like(held)

        @pl.loop(meta[META_SCENES + i * 2], meta[META_SCENES + i * 2 + 1])
        def _(w):
            k, v = window[w, 0, r, :], window[w, 1, r, :]
            one = jnp.exp(dot(first, k, NT))
            two = jnp.exp(dot(second, k, NT))
            held[0] += pick(dot(one.astype(BF), v), dot(two.astype(BF), v))
            for h, weights in ((1, one), (2, two)):
                tally = weights[:, 0:128]
                for start in range(128, frame, 128):
                    tally = tally + weights[:, start : start + 128]
                held[h] += tally

        lane = pick(
            jnp.broadcast_to(jnp.sum(held[1], axis=-1, keepdims=True), (frame, 128)),
            jnp.broadcast_to(jnp.sum(held[2], axis=-1, keepdims=True), (frame, 128)),
        )
        inverse = 1.0 / lane
        sums[j, r, :] = inverse
        found[j, r, :] = held[0] * inverse

    for d, out in enumerate((o0, o1, o2, o3)):
        out[...] = found[me ^ d].astype(BF)


def scene(meta, slots, below, above, frame):
    total = slots[0].shape[1]
    out = jax.ShapeDtypeStruct((total, 128), BF)
    wide = 2 * REACH + PLANE
    return call(
        functools.partial(scene_kernel, frame),
        (out,) * 4 + (jax.ShapeDtypeStruct((PLANE, total, 128), F32),) * 2,
        [SM] + [ANY] * 6,
        (VM,) * 6,
        [
            pltpu.VMEM((PLANE, total, 128), BF),
            pltpu.VMEM((wide, 2, total, 128), BF),
            pltpu.VMEM((3, frame, 128), F32),
            pltpu.SemaphoreType.DMA((4, PLANE)),
        ],
        4 * PLANE * total * PLANE * frame * 128 * 2,
        4 * wide * total * 128,
        "scene",
    )(meta, *slots, below, above)


def output_kernel(meta, w_out, o0, o1, o2, o3, attended, part, weight, sems):
    copies = fetch(meta, *w_out, weight, sems)
    me = meta[META_ME]
    model = part.shape[1]
    for d, slot in enumerate((o0, o1, o2, o3)):
        attended[:, pl.ds(pl.multiple_of((me ^ d) * 128, 128), 128)] = slot[...]
    finish(copies)
    for start in range(0, model, 256):
        part[:, start : start + 256] = dot(attended[...], weight[start : start + 256, :], NT).astype(BF)


def outputs(meta, w_out, slots, width, model):
    total = slots[0].shape[0]
    return call(
        with_weights(output_kernel, 1, [w_out]),
        (jax.ShapeDtypeStruct((total, width), BF), jax.ShapeDtypeStruct((total, model), BF)),
        [SM] + [HBM] * w_out.count + [VM] * 4,
        (VM, VM),
        [pltpu.VMEM((model, width), BF), pltpu.SemaphoreType.DMA((PIECES,))],
        2 * total * model * width,
        2 * model * width,
        "outputs",
    )(meta, *w_out.sources, *slots)


def feed_back_kernel(meta, w_down, w_up, g, slope, norms, d_mlp, d_hidden, part, up, down, sems):
    copies = fetch(meta, *w_down, down, sems.at[0])
    later = fetch(meta, *w_up, up, sems.at[1])
    total, model = g.shape
    hidden = up.shape[1]

    @pl.loop(0, total // 64)
    def _(i):
        r = pl.ds(pl.multiple_of(i * 64, 64), 64)
        d_mlp[r, :] = (g[r, :].astype(F32) * norms[5:6, :]).astype(BF)

    finish(copies)
    step = 256
    for start in range(0, hidden, step):
        d_active = dot(d_mlp[...], down[:, start : start + step])
        d_hidden[:, start : start + step] = (d_active * slope[:, start : start + step].astype(F32)).astype(BF)
    finish(later)
    for start in range(0, model, 256):
        part[:, start : start + 256] = dot(d_hidden[...], up[start : start + 256, :], NT).astype(BF)


def feed_back(meta, weights, g, slope, norms):
    total, model = g.shape
    hidden = slope.shape[1]
    sources = sources_of(weights)
    return call(
        with_weights(feed_back_kernel, 1, weights),
        (
            jax.ShapeDtypeStruct((total, model), BF),
            jax.ShapeDtypeStruct((total, hidden), BF),
            jax.ShapeDtypeStruct((total, model), BF),
        ),
        [SM] + [HBM] * len(sources) + [VM] * 3,
        (VM,) * 3,
        [
            pltpu.VMEM((model, hidden), BF),
            pltpu.VMEM((model, hidden), BF),
            pltpu.SemaphoreType.DMA((2, PIECES)),
        ],
        4 * total * model * hidden,
        8 * model * hidden,
        "feed_back",
    )(meta, *sources, g, slope, norms)


def weight_grad_kernel(base, widths, meta, *refs):
    count = len(widths)
    lefts, rights = refs[:count], refs[count : 2 * count]
    model = lefts[0].shape[1]
    if base is None:
        whole = refs[2 * count]
        for b in range(0, model, 256):
            start = 0
            for left, right, width in zip(lefts, rights, widths):
                whole[b : b + 256, start : start + width] = dot(left[:, b : b + 256], right[...], TN).astype(BF)
                start += width
        return
    parts, (staged, sems) = refs[2 * count : 2 * count + 4], refs[2 * count + 4 :]
    quarter, rows = parts[0].shape[0], parts[0].shape[1]
    block = 256
    per = block // rows

    def copy_out(b, act):
        slot = b % 2
        for s in range(per):
            place = meta[base + b * per + s]
            source = staged.at[slot, pl.ds(s * rows, rows), :]
            for part, out in enumerate(parts):

                @pl.when(place // quarter == part)
                def _():
                    getattr(pltpu.make_async_copy(source, out.at[lax.rem(place, quarter)], sems.at[slot, s]), act)()

    for b in range(model // block):
        if b >= 2:
            copy_out(b - 2, "wait")
        start = 0
        for left, right, width in zip(lefts, rights, widths):
            staged[b % 2, :, start : start + width] = dot(
                left[:, b * block : (b + 1) * block], right[...], TN
            ).astype(BF)
            start += width
        copy_out(b, "start")
    for b in range(max(0, model // block - 2), model // block):
        copy_out(b, "wait")


def weight_grad(meta, base, lefts, rights, name):
    widths = [right.shape[1] for right in rights]
    total, model = lefts[0].shape
    rows = model // PIECES
    wide = sum(widths)
    out = jax.ShapeDtypeStruct((PIECES // 4, rows, wide), BF)
    whole = base is None
    return call(
        functools.partial(weight_grad_kernel, base, widths),
        jax.ShapeDtypeStruct((model, wide), BF) if whole else (out,) * 4,
        [SM] + [VM] * (2 * len(widths)),
        VM if whole else (ANY,) * 4,
        [] if whole else [pltpu.VMEM((2, 256, wide), BF), pltpu.SemaphoreType.DMA((2, 256 // rows))],
        2 * total * model * wide,
        2 * model * wide + 2 * total * (model + wide),
        name,
    )(meta, *lefts, *rights)


def norm_back_kernel(frame, count, meta, *refs):
    inner = count > 2
    g, x, one, two, norms = refs[:5]
    if inner:
        pa, pb = refs[5:7]
        ma, mb = refs[7:9] if count > 3 else (None, None)
        out, d_branch, sums, tally = refs[-4:]
        gain = norms[3:4, :]
    else:
        out, sums, tally = refs[-3:]
        gain = norms[0:1, :]
    total, model = x.shape
    core = meta[META_CORE]
    rows = 64
    tally[...] = jnp.zeros_like(tally)

    @pl.loop(0, total // rows)
    def _(i):
        r = pl.ds(pl.multiple_of(i * rows, rows), rows)
        unit, scale = norm_parts(x[r, :].astype(F32))
        d = one[r, :].astype(F32) + two[r, :].astype(F32)
        dg = d * gain
        mean = jnp.mean(dg, axis=-1, keepdims=True)
        slant = jnp.mean(dg * unit, axis=-1, keepdims=True)
        before = g[r, :].astype(F32)
        after = before + scale * (dg - mean - unit * slant)
        out[r, :] = after
        if inner:
            d_branch[r, :] = (after * norms[2:3, :]).astype(BF)

        @pl.when((i // (frame // 2 // rows)) % 2 == core)
        def _():
            def add(k, values):
                tally[k] += jnp.sum(values.reshape(rows // 8, 8, model), axis=0)

            add(0, d * unit)
            add(1, d)
            if inner:
                add(2, after * (pa[r, :].astype(F32) + pb[r, :].astype(F32)))
            if count > 3:
                add(3, before * (ma[r, :].astype(F32) + mb[r, :].astype(F32)))

    sums[...] = jnp.sum(tally[...], axis=1)


def norm_back(meta, g, x, one, two, norms, frame, extra=None):
    total, model = x.shape
    inner = extra is not None
    count = 2 + len(extra) // 2 if inner else 2
    outs = [jax.ShapeDtypeStruct((total, model), F32)]
    if inner:
        outs.append(jax.ShapeDtypeStruct((total, model), BF))
    outs.append(jax.ShapeDtypeStruct((count, model), F32))
    return call(
        functools.partial(norm_back_kernel, frame, count),
        tuple(outs),
        [SM] + [VM] * (5 + len(extra or ())),
        (VM,) * len(outs),
        [pltpu.VMEM((count, 8, model), F32)],
        20 * total * model,
        16 * total * model,
        "norm_back_inner" if inner else "norm_back",
    )(meta, g, x, one, two, norms, *(extra or ()))


def project_back(normed, weight, gains, matrix, take, d_projected, sums):
    width = gains.shape[1]
    total = normed.shape[0]
    rows, lanes = 256, 256
    sums[...] = jnp.zeros_like(sums)
    for part in range(2):
        for start in range(0, width, lanes):
            columns = part * width + start

            @pl.loop(0, total // rows)
            def _(i):
                r = pl.ds(pl.multiple_of(i * rows, rows), rows)
                unit, scale = head_parts(dot(normed[r, :], weight[:, columns : columns + lanes]), matrix)
                d = take(part, r, start, lanes)
                dg = d * gains[part : part + 1, start : start + lanes]
                mean = head_mean(dg, matrix)
                slant = head_mean(dg * unit, matrix)
                d_projected[r, columns : columns + lanes] = (scale * (dg - mean - unit * slant)).astype(BF)
                tally = jnp.sum((d * unit).reshape(rows // 8, 8, lanes), axis=0)
                sums[part * 8 : part * 8 + 8, start : start + lanes] += tally


def frame_back_kernel(frame, head, meta, w_in, w_out, d_branch, normed, qkv, gains, d_projected, part, sums, weight, out, d_att, dq, dk, sems):
    copies = fetch(meta, *w_out, out, sems.at[1])
    later = fetch(meta, *w_in, weight, sems.at[0])
    total, model = normed.shape
    width = gains.shape[1]
    finish(copies)
    for start in range(0, width, 256):
        d_att[:, start : start + 256] = dot(d_branch[...], out[:, start : start + 256]).astype(BF)
    pairs = width // 128

    @pl.loop(0, (total // frame) * pairs)
    def _(i):
        r = pl.ds(pl.multiple_of((i // pairs) * frame, frame), frame)
        column = pl.multiple_of((i % pairs) * 128, 128)
        lanes = pl.ds(column, 128)
        q, k, v = qkv[0, r, lanes], qkv[1, r, lanes], qkv[2, r, lanes]
        d_out = d_att[r, lanes]
        found = []
        for mask in (only_first, only_second):
            weights = jnp.exp(dot(mask(q), k, NT))
            probs = weights / jnp.sum(weights, axis=-1, keepdims=True)
            d_probs = dot(mask(d_out), v, NT)
            delta = jnp.sum(probs * d_probs, axis=-1, keepdims=True)
            d_scores = (probs * (d_probs - delta)).astype(BF)
            found.append((dot(d_scores, k), dot(d_scores, q, TN), dot(probs.astype(BF), d_out, TN)))
        dq[r, lanes] = pick(found[0][0], found[1][0]) * HEAD_SCALE
        dk[r, lanes] = pick(found[0][1], found[1][1])
        d_projected[r, pl.ds(pl.multiple_of(2 * width + column, 128), 128)] = pick(found[0][2], found[1][2]).astype(BF)

    def take(which, r, start, lanes):
        return (dq, dk)[which][r, start : start + lanes]

    finish(later)
    project_back(normed, weight, gains, head_matrix(256, head), take, d_projected, sums)
    for start in range(0, model, 256):
        part[:, start : start + 256] = dot(d_projected[...], weight[start : start + 256, :], NT).astype(BF)


def frame_back(meta, weights, d_branch, normed, qkv, gains, frame, head):
    total, model = normed.shape
    width = gains.shape[1]
    sources = sources_of(weights)
    return call(
        with_weights(functools.partial(frame_back_kernel, frame, head), 1, weights),
        (
            jax.ShapeDtypeStruct((total, 3 * width), BF),
            jax.ShapeDtypeStruct((total, model), BF),
            jax.ShapeDtypeStruct((16, width), F32),
        ),
        [SM] + [HBM] * len(sources) + [VM] * 4,
        (VM,) * 3,
        [
            pltpu.VMEM((model, 3 * width), BF),
            pltpu.VMEM((model, width), BF),
            pltpu.VMEM((total, width), BF),
            pltpu.VMEM((total, width), F32),
            pltpu.VMEM((total, width), F32),
            pltpu.SemaphoreType.DMA((2, PIECES)),
        ],
        12 * total * model * width,
        8 * model * width,
        "frame_back",
    )(meta, *sources, d_branch, normed, qkv, gains)


def attended_back_kernel(meta, w_out, d_branch, s0, s1, s2, s3, weight, held, sems):
    finish(fetch(meta, *w_out, weight, sems))
    me = meta[META_ME]
    width = weight.shape[1]
    for start in range(0, width, 256):
        held[:, start : start + 256] = dot(d_branch[...], weight[:, start : start + 256]).astype(BF)
    for d, slot in enumerate((s0, s1, s2, s3)):
        slot[...] = held[:, pl.ds(pl.multiple_of((me ^ d) * 128, 128), 128)]


def attended_back(meta, w_out, d_branch, width):
    total, model = d_branch.shape
    return call(
        with_weights(attended_back_kernel, 1, [w_out]),
        (jax.ShapeDtypeStruct((total, 128), BF),) * 4,
        [SM] + [HBM] * w_out.count + [VM],
        (VM,) * 4,
        [
            pltpu.VMEM((model, width), BF),
            pltpu.VMEM((total, width), BF),
            pltpu.SemaphoreType.DMA((PIECES,)),
        ],
        2 * total * model * width,
        2 * model * width,
        "attended_back",
    )(meta, *w_out.sources, d_branch)


def scene_back_kernel(frame, meta, s0, s1, s2, s3, below, above, sums, whole, g0, g1, g2, g3, q0, q1, q2, q3, d_own, d_below, d_above, own, window, d_out, delta, dq, d_window, sems, more):
    copies = load_window(meta, (s0, s1, s2, s3), below, above, own, window, sems)
    me = meta[META_ME]
    for d, slot in enumerate((g0, g1, g2, g3)):
        copies.append(pltpu.make_async_copy(slot, d_out.at[me ^ d], more.at[d]))
        copies[-1].start()
    d_window[...] = jnp.zeros_like(d_window)
    finish(copies)
    total = own.shape[1]
    parts = total // frame

    @pl.loop(0, parts * PLANE)
    def _(i):
        m, j = i // PLANE, i % PLANE
        r = pl.ds(pl.multiple_of(m * frame, frame), frame)
        q, go = own[j, r, :], d_out[j, r, :]
        product = go.astype(F32) * whole[j, r, :]
        inverse = sums[j, r, :]
        heads = []
        for mask, lane in ((only_first, 0), (only_second, 64)):
            heads.append(
                (mask(q), mask(go), inverse[:, lane : lane + 1], jnp.sum(mask(product), axis=-1, keepdims=True))
            )
        dq[...] = jnp.zeros_like(dq)

        @pl.loop(meta[META_SCENES + i * 2], meta[META_SCENES + i * 2 + 1])
        def _(w):
            k, v = window[w, 0, r, :], window[w, 1, r, :]
            found = []
            for head_q, head_go, scale, shift in heads:
                probs = jnp.exp(dot(head_q, k, NT)) * scale
                d_scores = (probs * (dot(head_go, v, NT) - shift)).astype(BF)
                found.append((dot(d_scores, k), dot(d_scores, q, TN), dot(probs.astype(BF), go, TN)))
            dq[...] += pick(found[0][0], found[1][0])
            d_window[w, 0, r, :] += pick(found[0][1], found[1][1])
            d_window[w, 1, r, :] += pick(found[0][2], found[1][2])

        delta[j, r, :] = dq[...] * HEAD_SCALE

    for d, out in enumerate((q0, q1, q2, q3)):
        out[...] = delta[me ^ d].astype(BF)
    for k in range(PLANE):
        d_own[k] = d_window[REACH + k]
    for k in range(REACH):
        d_below[k] = d_window[k].astype(BF)
        d_above[k] = d_window[REACH + PLANE + k].astype(BF)


def scene_back(meta, slots, below, above, sums, found, d_found, frame):
    total = slots[0].shape[1]
    wide = 2 * REACH + PLANE
    out = jax.ShapeDtypeStruct((total, 128), BF)
    edge = jax.ShapeDtypeStruct((REACH, 2, total, 128), BF)
    return call(
        functools.partial(scene_back_kernel, frame),
        (out,) * 4 + (jax.ShapeDtypeStruct((PLANE, 2, total, 128), F32), edge, edge),
        [SM] + [ANY] * 6 + [VM] * 2 + [ANY] * 4,
        (VM,) * 7,
        [
            pltpu.VMEM((PLANE, total, 128), BF),
            pltpu.VMEM((wide, 2, total, 128), BF),
            pltpu.VMEM((PLANE, total, 128), BF),
            pltpu.VMEM((PLANE, total, 128), F32),
            pltpu.VMEM((frame, 128), F32),
            pltpu.VMEM((wide, 2, total, 128), F32),
            pltpu.SemaphoreType.DMA((4, PLANE)),
            pltpu.SemaphoreType.DMA((PLANE,)),
        ],
        10 * PLANE * total * PLANE * frame * 128 * 2,
        8 * wide * total * 128,
        "scene_back",
    )(meta, *slots, below, above, sums, found, *d_found)


def edge_sum_kernel(meta, d_own, from_below, from_above, t0, t1, t2, t3):
    me = meta[META_ME]
    for d, out in enumerate((t0, t1, t2, t3)):
        j = me ^ d
        low = jnp.where(j <= REACH - 1, 1.0, 0.0)
        high = jnp.where(j >= 1, 1.0, 0.0)
        at, top = jnp.minimum(j, REACH - 1), jnp.maximum(j - 1, 0)
        for part in range(2):
            values = d_own[j, part] + low * from_below[at, part].astype(F32)
            out[part] = (values + high * from_above[top, part].astype(F32)).astype(BF)


def edge_sum(meta, d_own, from_below, from_above):
    total = d_own.shape[2]
    out = jax.ShapeDtypeStruct((2, total, 128), BF)
    return call(
        edge_sum_kernel,
        (out,) * 4,
        [SM, VM, VM, VM],
        (VM,) * 4,
        [],
        8 * PLANE * total * 128,
        20 * PLANE * total * 128,
        "edge_sum",
    )(meta, d_own, from_below, from_above)


def queries_back_kernel(head, meta, w_in, q0, q1, q2, q3, t0, t1, t2, t3, normed, gains, d_projected, part, sums, weight, dq, dk, sems):
    copies = fetch(meta, *w_in, weight, sems)
    me = meta[META_ME]
    model = normed.shape[1]
    width = gains.shape[1]
    for d, (query, pair) in enumerate(zip((q0, q1, q2, q3), (t0, t1, t2, t3))):
        column = pl.multiple_of((me ^ d) * 128, 128)
        dq[:, pl.ds(column, 128)] = query[...].astype(F32)
        dk[:, pl.ds(column, 128)] = pair[0].astype(F32)
        d_projected[:, pl.ds(pl.multiple_of(2 * width + column, 128), 128)] = pair[1]
    finish(copies)

    def take(which, r, start, lanes):
        return (dq, dk)[which][r, start : start + lanes]

    project_back(normed, weight, gains, head_matrix(256, head), take, d_projected, sums)
    for start in range(0, model, 256):
        part[:, start : start + 256] = dot(d_projected[...], weight[start : start + 256, :], NT).astype(BF)


def queries_back(meta, w_in, d_queries, d_pairs, normed, gains, head):
    total, model = normed.shape
    width = gains.shape[1]
    return call(
        with_weights(functools.partial(queries_back_kernel, head), 1, [w_in]),
        (
            jax.ShapeDtypeStruct((total, 3 * width), BF),
            jax.ShapeDtypeStruct((total, model), BF),
            jax.ShapeDtypeStruct((16, width), F32),
        ),
        [SM] + [HBM] * w_in.count + [VM] * 10,
        (VM,) * 3,
        [
            pltpu.VMEM((model, 3 * width), BF),
            pltpu.VMEM((total, width), F32),
            pltpu.VMEM((total, width), F32),
            pltpu.SemaphoreType.DMA((PIECES,)),
        ],
        10 * total * model * width,
        8 * model * width,
        "queries_back",
    )(meta, *w_in.sources, *d_queries, *d_pairs, normed, gains)


META_CORE = 5 * PIECES
META_ME = META_CORE + 1
META_SCENES = META_ME + 1


def body(tokens, cotangent, scene_ids, input_weight, output_weight, up_weight, down_weight, norm_params, head_gains):
    portions, _, share, model = tokens.shape
    frame = 2 * share
    total = portions * frame
    head = head_gains.shape[2]
    width = input_weight.shape[3]
    routes = Routes(lax.axis_size("frames"))
    n = routes.n
    index, core = lax.axis_index("frames"), lax.axis_index("mp")
    plain = n != PIECES

    identity = jnp.arange(PIECES, dtype=jnp.int32)
    tables = [identity] * 5 if plain else routes.tables()
    scene_here = scene_ids[:, (index // PLANE) * PLANE + jnp.arange(PLANE)]
    before = jnp.sum(scene_ids[:, None, :] < scene_here[:, :, None], axis=-1)
    until = jnp.sum(scene_ids[:, None, :] <= scene_here[:, :, None], axis=-1)
    spans = jnp.stack([before, until], axis=-1) - (index // PLANE) * PLANE + REACH
    meta = jnp.concatenate(
        [*tables, core[None], (index % PLANE)[None], spans.reshape(-1)]
    ).astype(jnp.int32)

    def all_rows(block):
        own = block[:, 0]
        other = routes.swap(own)
        both = jnp.where(core == 0, jnp.stack([own, other], 1), jnp.stack([other, own], 1))
        return both.reshape(total, model)

    def own_rows(values):
        return lax.dynamic_index_in_dim(values.reshape(portions, 2, share, -1), core, 1, keepdims=True)

    gains = [jnp.tile(head_gains[layer], (1, width // head)) for layer in range(2)]
    clock = Clock(not plain)
    late, close = clock.late, clock.close
    joined = [
        jnp.concatenate([input_weight[layer].reshape(-1, 3 * width), output_weight[layer]], axis=1)
        for layer in range(2)
    ]

    def gather(shard, line_first, name):
        if plain or line_first is None:
            return Whole(lax.all_gather(shard, "frames", axis=0, tiled=True))
        return Gather(routes, clock, shard, line_first, name)

    def scatter(line_last, name, lefts, rights):
        if plain or line_last is None:
            grad = weight_grad(meta, None, lefts, rights, name)
            ready[name] = grad
            summed = lax.psum_scatter(grad.astype(F32) if plain else grad, "frames", scatter_dimension=0, tiled=True)
            return Whole(summed.astype(F32))
        parts = weight_grad(meta, (3 if line_last else 2) * PIECES, lefts, rights, name)
        ready[name] = parts[2]
        return Scatter(routes, clock, parts, line_last, name)

    ready = {}

    ga0 = gather(joined[0], True, "input0")
    gu0 = gather(up_weight[0], False, "up0")
    gd0 = gather(down_weight[0], False, "down0")
    ga1 = gather(joined[1], False, "input1")
    gu1 = gather(up_weight[1], False, "up1")
    gd1 = gather(down_weight[1], False, "down1")
    ga0.ring(3)
    for each in (gu0, gd0, ga1, gu1, gd1):
        each.one()
    rows = all_rows(tokens)
    d_result = all_rows(cotangent)
    close(rows, d_result)
    ga0.one()
    ga0.two(0)
    gu0.ring(2)
    close()
    ga0.two(1)
    gu0.ring()
    close()
    in0, out0 = ga0.end(0, 3 * width), ga0.end(3 * width, width)
    gu0.two(0)
    gd0.ring()
    normed0, qkv0, attended0, a0 = attention_frame(
        meta, [in0, out0], late(rows), norm_params[0], gains[0], frame, head
    )
    close(a0)
    b0 = clock.add(routes.swap(a0))
    gu0.two(1)
    gd0.ring()
    close()
    up0 = gu0.end()
    gd0.two(0)
    gd0.ring()
    mid0, normed_mid0, active0, slope0 = feed_up(meta, up0, rows, a0, late(b0), norm_params[0])
    close(active0)
    gd0.two(1)
    ga1.ring()
    close()
    down0 = gd0.end()
    ga1.two(0)
    ga1.ring()
    m0 = feed_down(meta, down0, late(active0), model)
    close(m0)
    n0 = clock.add(routes.swap(m0))
    ga1.ring()
    close()
    ga1.two(1)
    gu1.ring()
    close()
    in1, out1 = ga1.end(0, 3 * width), ga1.end(3 * width, width)
    gu1.two(0)
    gu1.ring()
    x1, normed1, *slots = queries(
        meta, in1, mid0, m0, late(n0), norm_params[0], norm_params[1], gains[1], head
    )
    close(slots[0])
    slots = routes.members(late(slots))
    gu1.ring()
    close(*slots[1:])
    rise, fall = edges(meta, late(slots))
    below, above = routes.up(rise), routes.down(fall)
    gu1.two(1)
    close(below, above)
    gd1.ring()
    *found, sums, whole_found = scene(meta, slots, late(below), above, frame)
    close(found[0])
    home = routes.members(late(found))
    gd1.ring()
    close(*home[1:])
    gd1.two(0)
    gd1.ring()
    attended1, a1 = outputs(meta, out1, late(home), width, model)
    b1 = routes.swap(a1)
    close(b1)
    up1 = gu1.end()
    gd1.two(1)
    mid1, normed_mid1, active1, slope1 = feed_up(meta, up1, x1, a1, late(b1), norm_params[1])
    close(active1)

    down1 = gd1.end()
    d_mlp, d_hidden, p = feed_back(meta, [down1, up1], late(d_result), slope1, norm_params[1])
    close(p)
    q = clock.add(routes.swap(p))
    sd1 = scatter(True, "down_grad1", [late(d_mlp)], [active1])
    close(ready["down_grad1"])
    sd1.two(1)
    g, d_branch, inner1 = norm_back(meta, d_result, mid1, p, late(q), norm_params[1], frame, (a1, b1))
    d_home = attended_back(meta, out1, d_branch, width)
    su1 = scatter(True, "up_grad1", [late(normed_mid1)], [d_hidden])
    close(d_home[0], ready["up_grad1"])
    d_found = routes.members(late(d_home))
    close(*d_found[1:])
    sd1.one()
    sd1.two(0)
    *d_queries, d_own, d_below, d_above = scene_back(
        meta, slots, late(below), above, sums, whole_found, d_found, frame
    )
    close(d_own)
    from_above, from_below = routes.down(late(d_below)), routes.up(late(d_above))
    d_queries = routes.members(late(d_queries))
    su1.two(1)
    m1 = feed_down(meta, down1, late(active1), model)
    close(m1, from_above, from_below, *d_queries[1:])
    n1 = clock.add(routes.swap(m1))
    sd1.ring()
    pairs = routes.members(edge_sum(meta, d_own, late(from_below), from_above))
    close(*pairs[1:])
    su1.one()
    sd1.ring()
    d_projected, p, gain1 = queries_back(meta, in1, d_queries, late(pairs), normed1, gains[1], head)
    close(p)
    q = clock.add(routes.swap(p))
    su1.two(0)
    sd1.ring()
    sa1 = scatter(False, "input_grad1", [normed1, d_branch], [late(d_projected), attended1])
    close(ready["input_grad1"])
    sa1.two(0)
    su1.ring()
    own_mlp = own_rows(m1).astype(F32) + own_rows(n1).astype(F32)
    result = own_rows(mid1) + norm_params[1, 5] * own_mlp
    scale1 = jnp.sum(cotangent.astype(F32).reshape(-1, model) * own_mlp.reshape(-1, model), axis=0)
    g, outer1 = norm_back(meta, g, x1, p, late(q), norm_params[1], frame)

    d_mlp, d_hidden, p = feed_back(meta, [down0, up0], g, slope0, norm_params[0])
    close(p)
    q = clock.add(routes.swap(p))
    sa1.two(1)
    sa1.ring()
    su1.ring()
    sd0 = scatter(False, "down_grad0", [late(d_mlp)], [active0])
    close(ready["down_grad0"])
    sd0.two(0)
    sa1.ring()
    su1.ring()
    su0 = scatter(True, "up_grad0", [late(normed_mid0)], [d_hidden])
    g, d_branch, inner0 = norm_back(meta, g, mid0, p, late(q), norm_params[0], frame, (a0, b0, m0, n0))
    close(d_branch, ready["up_grad0"])
    sd0.two(1)
    su0.two(1)
    sa1.ring()
    sd0.ring()
    d_projected, p, gain0 = frame_back(
        meta, [in0, out0], late(d_branch), normed0, qkv0, gains[0], frame, head
    )
    close(p)
    q = clock.add(routes.swap(late(p)))
    su0.two(0)
    sd0.ring()
    sa1.one()
    sa0 = scatter(False, "input_grad0", [normed0, d_branch], [late(d_projected), attended0])
    close(ready["input_grad0"])
    su0.one()
    sa0.two(0)
    sd0.ring()
    g, outer0 = norm_back(meta, g, rows, p, late(q), norm_params[0], frame)
    token_grad = own_rows(g)
    close(g)

    norm_rows = [
        jnp.stack([outer[0], outer[1], inner[2], inner[0], inner[1], scale])
        for outer, inner, scale in ((outer0, inner0, inner0[3]), (outer1, inner1, scale1))
    ]
    gain_rows = [
        jnp.sum(gain.reshape(2, 8, width // head, head), axis=(1, 2)).reshape(1, -1)
        for gain in (gain0, gain1)
    ]
    gain_rows = jnp.pad(jnp.concatenate(gain_rows, axis=1), ((0, 0), (0, model - 4 * head)))
    small = jnp.concatenate([*norm_rows, gain_rows])
    small = small + routes.swap(small)
    distances = [2**i for i in range(n.bit_length() - 1)]

    def sum_step(block, distance):
        return block + clock.add(routes.member(late(block), distance))

    small = sum_step(small, distances[0])
    sa0.two(1)
    sa0.ring()
    su0.ring()
    close()
    small = sum_step(small, distances[1])
    sd0.one()
    sa0.ring()
    su0.ring()
    close()
    for distance in distances[2:]:
        small = sum_step(small, distance)
    sa0.ring()
    su0.ring()
    sa0.one()
    norm_grad = small[: 2 * 6].reshape(2, 6, model)
    gain_grad = small[2 * 6, : 4 * head].reshape(2, 2, head)
    return (
        result.astype(BF),
        token_grad,
        jnp.stack([step.run[:, : 3 * width].reshape(-1, 3, width) for step in (sa0, sa1)]),
        jnp.stack([step.run[:, 3 * width :] for step in (sa0, sa1)]),
        jnp.stack([step.run for step in (su0, su1)]),
        jnp.stack([step.run for step in (sd0, sd1)]),
        norm_grad,
        gain_grad,
    )


def solution(mesh):
    rows = P(None, "frames", "mp", None)
    shard = P(None, "frames", "mp")
    wide = P(None, "frames", None, "mp")
    return jax.shard_map(
        body,
        mesh=mesh,
        in_specs=(rows, rows, P(), wide, shard, shard, shard, P(), P()),
        out_specs=(rows, rows, wide, shard, shard, shard, P(), P()),
        check_vma=False,
    )
```

```python
import functools

import jax
import jax.numpy as jnp
import numpy as np
from jax import lax
from jax.experimental import pallas as pl
from jax.experimental.pallas import tpu as pltpu
from jax.sharding import PartitionSpec as P

BF = jnp.bfloat16
F32 = jnp.float32
ROW_EPS = 1e-06
HEAD_EPS = 1e-05
PIECES = 16
SWAPS = 1
COST = 1
PLANE = 4
REACH = 3
AXES = ("frames", "mp")

NN = (((1,), (0,)), ((), ()))
NT = (((1,), (1,)), ((), ()))
TN = (((0,), (0,)), ((), ()))

VM = pl.BlockSpec(memory_space=pltpu.VMEM)
SM = pl.BlockSpec(memory_space=pltpu.SMEM)
ANY = pl.BlockSpec(memory_space=pl.ANY)
HBM = pl.BlockSpec(memory_space=pltpu.HBM)


def dot(left, right, dims=NN):
    return lax.dot_general(left, right, dims, preferred_element_type=F32)


def call(body, outs, in_specs, out_specs, scratch, flops, moved, name):
    return pl.pallas_call(
        body,
        out_shape=outs,
        in_specs=in_specs,
        out_specs=out_specs,
        scratch_shapes=scratch,
        compiler_params=pltpu.CompilerParams(vmem_limit_bytes=(60 if name in ("queries", "queries_back") else 18) * 1024 * 1024),
        cost_estimate=pl.CostEstimate(flops=flops // COST, bytes_accessed=moved // COST, transcendentals=0),
        name=name,
    )


class Routes:
    def __init__(self, n):
        lines = n // PLANE
        self.n, self.lines = n, lines
        order = [0] + list(range(1, lines, 2)) + sorted(range(2, lines, 2), reverse=True)
        following = {z: order[(i + 1) % lines] for i, z in enumerate(order)}
        spot = {z: i for i, z in enumerate(order)}
        self.back = np.array([[order[(spot[z] - k) % lines] for z in range(lines)] for k in range(lines)], np.int32)
        self.steps = np.array([[(spot[z] - spot[w]) % lines for w in range(lines)] for z in range(lines)], np.int32)
        self.ring = [
            (f * 2 + c, (following[f // PLANE] * PLANE + f % PLANE) * 2 + c) for f in range(n) for c in range(2)
        ]
        self.one = [(f * 2 + c, (f ^ (1 + c)) * 2 + c) for f in range(n) for c in range(2)]
        self.two = [(f * 2 + c, (f ^ (2 - c)) * 2 + c) for f in range(n) for c in range(2)]

    def send(self, block, route):
        return lax.ppermute(block, AXES, route)

    def swap(self, block):
        return lax.ppermute(block, "mp", [(0, 1), (1, 0)])

    def swap_parts(self, block):
        if SWAPS == 1:
            return self.swap(block)
        rows = block.shape[0] // SWAPS
        return jnp.concatenate([self.swap(block[i * rows : (i + 1) * rows]) for i in range(SWAPS)])

    def member(self, block, distance):
        return lax.ppermute(block, "frames", [(f, f ^ distance) for f in range(self.n)])

    def members(self, blocks):
        return [blocks[0]] + [self.member(blocks[d], d) for d in range(1, PLANE)]

    def up(self, block):
        return lax.ppermute(block, "frames", [(f, f + PLANE) for f in range(self.n - PLANE)])

    def down(self, block):
        return lax.ppermute(block, "frames", [(f + PLANE, f) for f in range(self.n - PLANE)])

    def tables(self):
        frame, core = lax.axis_index("frames"), lax.axis_index("mp")
        low, high = 1 + core, 2 - core
        bits = jnp.arange(2, dtype=jnp.int32)
        line = PLANE * jnp.asarray(self.back)[:, frame // PLANE]
        straight = PLANE * (frame // PLANE ^ jnp.arange(self.lines, dtype=jnp.int32))
        near = ((frame // low) % 2 ^ bits) * low
        far = ((frame // high) % 2 ^ bits) * high
        middle = line[None, :, None] + near[None, None, :] + far[:, None, None]
        first = line[None, None, :] + near[None, :, None] + far[:, None, None]
        direct = straight[None, None, :] + near[None, :, None] + far[:, None, None]
        every = jnp.arange(self.n, dtype=jnp.int32)
        k = jnp.repeat(jnp.asarray(self.steps)[frame // PLANE], PLANE)
        j = (every // low) % 2 ^ (frame // low) % 2
        h = (every // high) % 2 ^ (frame // high) % 2
        half = self.n // 2
        place_middle = h * half + k * 2 + j
        place_first = h * half + j * self.lines + k
        return [t.reshape(-1).astype(jnp.int32) for t in (middle, first, place_middle, place_first, direct)]


class Clock:
    def __init__(self, active):
        self.active, self.waited, self.pending = active, [], []

    def late(self, value):
        if not (self.active and self.waited):
            return value
        return lax.optimization_barrier((value, self.waited))[0]

    def add(self, value):
        self.pending.append(value)
        return value

    def close(self, *values):
        self.waited, self.pending = self.pending + list(values), []


class Gather:
    def __init__(self, routes, clock, shard, line_first, name):
        self.routes, self.clock, self.line_first, self.name = routes, clock, line_first, name
        self.shard, self.pieces, self.direct = shard, [shard], False

    def send(self, block, route, step):
        with jax.named_scope(self.name + step):
            return self.clock.add(self.routes.send(self.clock.late(block), route))

    def ring(self, steps=1):
        for i in range(steps):
            if i:
                moved = self.routes.send(self.pieces[-1], self.routes.ring)
                self.clock.pending[-1] = moved
            else:
                moved = self.send(self.pieces[-1], self.routes.ring, "_ring")
            self.pieces.append(moved)
        if self.line_first and len(self.pieces) == self.routes.lines:
            self.line = jnp.stack(self.pieces)

    def straight(self):
        self.direct = True
        for k in range(1, self.routes.lines):
            with jax.named_scope(self.name + "_line"):
                self.pieces.append(self.clock.add(self.routes.member(self.clock.late(self.shard), PLANE * k)))
        self.line = jnp.stack(self.pieces)

    def one(self):
        if self.line_first:
            self.got = self.send(self.line, self.routes.one, "_one")
        else:
            self.pieces = [jnp.stack([self.shard, self.send(self.shard, self.routes.one, "_one")])]

    def near(self, half):
        if self.line_first:
            return (self.line, self.got)[half]
        if not hasattr(self, "pairs"):
            self.pairs = {}
        if half not in self.pairs:
            self.pairs[half] = jnp.concatenate(self.pieces[2 * half : 2 * half + 2])
        return self.pairs[half]

    def two(self, half):
        far = self.send(self.near(half), self.routes.two, "_two")
        self.far = (self.far if half else []) + [far]

    def end(self, start=0, width=None):
        sources = [self.near(0), self.near(1), *self.far]
        base = (4 if self.direct else 1) * PIECES if self.line_first else 0
        return Weight(sources, base, start, width)


class Scatter:
    def __init__(self, routes, clock, parts, line_last, name):
        self.routes, self.clock, self.line_last, self.name = routes, clock, line_last, name
        self.keep, self.give = parts[:2], parts[2:]
        self.got, self.at, self.run = [None, None], 0, None

    def send(self, block, route, step):
        with jax.named_scope(self.name + step):
            return self.clock.add(self.routes.send(self.clock.late(block), route))

    def two(self, half):
        self.got[half] = self.send(self.give[half], self.routes.two, "_two")

    def one(self):
        if self.line_last:
            block = self.keep[1].astype(F32) + self.got[1].astype(F32)
            self.more = self.send(block.astype(BF), self.routes.one, "_one")
        else:
            self.run = self.run[0] + self.send(self.run[1].astype(BF), self.routes.one, "_one").astype(F32)

    def local(self, k):
        if self.line_last:
            return self.keep[0][k].astype(F32) + self.got[0][k].astype(F32) + self.more[k].astype(F32)
        half, rows = k // 2, slice(2 * (k % 2), 2 * (k % 2) + 2)
        return self.keep[half][rows].astype(F32) + self.got[half][rows].astype(F32)

    def ring(self):
        if self.run is None:
            self.at, self.run = 1, self.local(1)
        moved = self.send(self.run.astype(BF), self.routes.ring, "_ring")
        self.at = (self.at + 1) % self.routes.lines
        self.run = self.local(self.at) + moved.astype(F32)


class Weight:
    def __init__(self, sources, base, start=0, width=None):
        self.sources, self.count = tuple(sources), len(sources)
        self.width = width or self.sources[0].shape[-1]
        self.plan = (base, start, self.width)


class Whole:
    def __init__(self, value):
        self.run = value

    def ring(self, steps=1):
        pass

    def one(self):
        pass

    def straight(self):
        pass

    def two(self, half):
        pass

    def end(self, start=0, width=None):
        return Weight([self.run], None, start, width)


def with_weights(kernel, before, weights):
    def run(*refs):
        at = before
        given = []
        for weight in weights:
            given.append((weight.plan, refs[at : at + weight.count]))
            at += weight.count
        return kernel(*refs[:before], *given, *refs[at:])

    return run


def sources_of(weights):
    return [source for weight in weights for source in weight.sources]


def fetch(meta, plan, sources, into, sems):
    base, start, width = plan
    columns = pl.ds(start, width)
    copies = []
    if base is None:
        rows = into.shape[0] // 4
        for q in range(4):
            part = pl.ds(q * rows, rows)
            copies.append(pltpu.make_async_copy(sources[0].at[part, columns], into.at[part, :], sems.at[q]))
    else:
        rows, quarter = into.shape[0] // PIECES, PIECES // 4
        for q in range(PIECES):
            source = sources[q // quarter].at[q % quarter, :, columns]
            row = pl.multiple_of(meta[base + q] * rows, rows)
            copies.append(pltpu.make_async_copy(source, into.at[pl.ds(row, rows), :], sems.at[q]))
    for copy in copies:
        copy.start()
    return copies


def finish(copies):
    for copy in copies:
        copy.wait()


def norm_parts(values):
    centred = values - jnp.mean(values, axis=-1, keepdims=True)
    scale = lax.rsqrt(jnp.mean(centred * centred, axis=-1, keepdims=True) + ROW_EPS)
    return centred * scale, scale


def head_matrix(width, head):
    row = lax.broadcasted_iota(jnp.int32, (width, width), 0) // head
    column = lax.broadcasted_iota(jnp.int32, (width, width), 1) // head
    return jnp.where(row == column, 1.0 / head, 0.0).astype(BF)


def head_mean(values, matrix):
    high = values.astype(BF)
    low = (values - high.astype(F32)).astype(BF)
    return dot(high, matrix) + dot(low, matrix)


def head_parts(values, matrix):
    centred = values - head_mean(values, matrix)
    scale = lax.rsqrt(head_mean(centred * centred, matrix) + HEAD_EPS)
    return centred * scale, scale


def project(normed, weight, gains, matrix, put, rows=256, lanes=256):
    width = gains.shape[1]
    total = normed.shape[0]
    factor = HEAD_SCALE

    for part in range(3):
        for start in range(0, width, lanes):
            columns = part * width + start

            @pl.loop(0, total // rows)
            def _(i):
                r = pl.ds(pl.multiple_of(i * rows, rows), rows)
                values = dot(normed[r, :], weight[:, columns : columns + lanes])
                if part < 2:
                    unit, _ = head_parts(values, matrix)
                    values = unit * gains[part : part + 1, start : start + lanes]
                values = values.astype(BF)
                if part == 0:
                    values = (values.astype(F32) * factor).astype(BF)
                put(part, r, start, lanes, values)


HEAD_SCALE = 0.125


def only_first(values):
    lane = lax.broadcasted_iota(jnp.int32, values.shape, 1)
    return jnp.where(lane < values.shape[1] // 2, values, jnp.zeros_like(values))


def only_second(values):
    lane = lax.broadcasted_iota(jnp.int32, values.shape, 1)
    return jnp.where(lane < values.shape[1] // 2, jnp.zeros_like(values), values)


def pick(first, second):
    lane = lax.broadcasted_iota(jnp.int32, first.shape, 1)
    return jnp.where(lane < first.shape[1] // 2, first, second)


def gelu_parts(v):
    size = jnp.abs(v)
    bell = jnp.exp(v * v * -0.5)
    t = 1.0 / (1.0 + size * 0.23164189)
    tail = t * (0.127414796 + t * (-0.142248368 + t * (0.7107068705 + t * (-0.7265760135 + t * 0.5307027145))))
    tail = tail * bell
    phi = jnp.where(v >= 0.0, 1.0 - tail, tail)
    return v * phi, phi + v * bell * 0.3989422804014327


def attention_frame_kernel(frame, head, meta, w_in, w_out, rows_ref, norms, gains, normed, qkv, attended, part, weight, out, sems):
    copies = fetch(meta, *w_in, weight, sems.at[0])
    later = fetch(meta, *w_out, out, sems.at[1])
    total, model = rows_ref.shape
    width = gains.shape[1]

    @pl.loop(0, total // 64)
    def _(i):
        r = pl.ds(pl.multiple_of(i * 64, 64), 64)
        unit, _ = norm_parts(rows_ref[r, :].astype(F32))
        normed[r, :] = (unit * norms[0:1, :] + norms[1:2, :]).astype(BF)

    finish(copies)
    matrix = head_matrix(256, head)

    def put(part, r, start, lanes, values):
        qkv[part, r, start : start + lanes] = values

    project(normed, weight, gains, matrix, put)
    pairs = width // 128

    @pl.loop(0, (total // frame) * pairs)
    def _(i):
        r = pl.ds(pl.multiple_of((i // pairs) * frame, frame), frame)
        lanes = pl.ds(pl.multiple_of((i % pairs) * 128, 128), 128)
        q, k, v = qkv[0, r, lanes], qkv[1, r, lanes], qkv[2, r, lanes]
        found = []
        for mask in (only_first, only_second):
            weights = jnp.exp(dot(mask(q), k, NT))
            found.append(dot(weights.astype(BF), v) / jnp.sum(weights, axis=-1, keepdims=True))
        attended[r, lanes] = pick(found[0], found[1]).astype(BF)

    finish(later)
    for start in range(0, model, 256):
        part[:, start : start + 256] = dot(attended[...], out[start : start + 256, :], NT).astype(BF)


def attention_frame(meta, weights, rows, norms, gains, frame, head):
    total, model = rows.shape
    width = gains.shape[1]
    sources = sources_of(weights)
    return call(
        with_weights(functools.partial(attention_frame_kernel, frame, head), 1, weights),
        (
            jax.ShapeDtypeStruct((total, model), BF),
            jax.ShapeDtypeStruct((3, total, width), BF),
            jax.ShapeDtypeStruct((total, width), BF),
            jax.ShapeDtypeStruct((total, model), BF),
        ),
        [SM] + [HBM] * len(sources) + [VM, VM, VM],
        (VM, VM, VM, VM),
        [
            pltpu.VMEM((model, 3 * width), BF),
            pltpu.VMEM((model, width), BF),
            pltpu.SemaphoreType.DMA((2, PIECES)),
        ],
        8 * total * model * width,
        2 * 4 * model * width,
        "attention_frame",
    )(meta, *sources, rows, norms, gains)


def feed_up_kernel(meta, w_up, x, one, two, norms, mid, normed, active, slope, up, sems):
    copies = fetch(meta, *w_up, up, sems)
    total, model = x.shape
    hidden = up.shape[1]

    @pl.loop(0, total // 64)
    def _(i):
        r = pl.ds(pl.multiple_of(i * 64, 64), 64)
        branch = one[r, :].astype(F32) + two[r, :].astype(F32)
        values = x[r, :].astype(F32) + norms[2:3, :] * branch
        mid[r, :] = values
        unit, _ = norm_parts(values)
        normed[r, :] = (unit * norms[3:4, :] + norms[4:5, :]).astype(BF)

    finish(copies)
    step, rows = 512, 256
    for start in range(0, hidden, step):

        @pl.loop(0, total // rows)
        def _(i):
            r = pl.ds(pl.multiple_of(i * rows, rows), rows)
            before = dot(normed[r, :], up[:, start : start + step])
            after_, rise = gelu_parts(before)
            active[r, start : start + step] = after_.astype(BF)
            slope[r, start : start + step] = rise.astype(BF)


def feed_up(meta, up, x, one, two, norms):
    total, model = x.shape
    hidden = up.width
    return call(
        with_weights(feed_up_kernel, 1, [up]),
        (
            jax.ShapeDtypeStruct((total, model), F32),
            jax.ShapeDtypeStruct((total, model), BF),
            jax.ShapeDtypeStruct((total, hidden), BF),
            jax.ShapeDtypeStruct((total, hidden), BF),
        ),
        [SM] + [HBM] * up.count + [VM] * 4,
        (VM,) * 4,
        [pltpu.VMEM((model, hidden), BF), pltpu.SemaphoreType.DMA((PIECES,))],
        2 * total * model * hidden,
        2 * model * hidden,
        "feed_up",
    )(meta, *up.sources, x, one, two, norms)


def feed_down_kernel(meta, w_down, active, part, down, sems):
    model = part.shape[1]
    finish(fetch(meta, *w_down, down, sems))
    for start in range(0, model, 256):
        part[:, start : start + 256] = dot(active[...], down[start : start + 256, :], NT).astype(BF)


def feed_down(meta, down, active, model):
    total, hidden = active.shape
    return call(
        with_weights(feed_down_kernel, 1, [down]),
        jax.ShapeDtypeStruct((total, model), BF),
        [SM] + [HBM] * down.count + [VM],
        VM,
        [pltpu.VMEM((model, hidden), BF), pltpu.SemaphoreType.DMA((PIECES,))],
        2 * total * model * hidden,
        2 * model * hidden,
        "feed_down",
    )(meta, *down.sources, active)


def queries_kernel(head, meta, w_in, mid, one, two, before, norms, gains, x, normed, s0, s1, s2, s3, weight, held, sems):
    copies = fetch(meta, *w_in, weight, sems)
    total, model = mid.shape
    width = gains.shape[1]
    me = meta[META_ME]

    @pl.loop(0, total // 64)
    def _(i):
        r = pl.ds(pl.multiple_of(i * 64, 64), 64)
        values = mid[r, :] + before[5:6, :] * (one[r, :].astype(F32) + two[r, :].astype(F32))
        x[r, :] = values
        unit, _ = norm_parts(values)
        normed[r, :] = (unit * norms[0:1, :] + norms[1:2, :]).astype(BF)

    finish(copies)

    def put(part, r, start, lanes, values):
        held[part, r, start : start + lanes] = values

    project(normed, weight, gains, head_matrix(256, head), put)
    for d, slot in enumerate((s0, s1, s2, s3)):
        lanes = pl.ds(pl.multiple_of((me ^ d) * 128, 128), 128)
        for part in range(3):
            slot[part] = held[part, :, lanes]


def queries(meta, w_in, mid, one, two, before, norms, gains, head):
    total, model = mid.shape
    width = gains.shape[1]
    slot = jax.ShapeDtypeStruct((3, total, 128), BF)
    return call(
        with_weights(functools.partial(queries_kernel, head), 1, [w_in]),
        (jax.ShapeDtypeStruct((total, model), F32), jax.ShapeDtypeStruct((total, model), BF)) + (slot,) * 4,
        [SM] + [HBM] * w_in.count + [VM] * 6,
        (VM,) * 6,
        [
            pltpu.VMEM((model, 3 * width), BF),
            pltpu.VMEM((3, total, width), BF),
            pltpu.SemaphoreType.DMA((PIECES,)),
        ],
        6 * total * model * width,
        8 * model * width,
        "queries",
    )(meta, *w_in.sources, mid, one, two, before, norms, gains)


def edge_kernel(meta, s0, s1, s2, s3, rise, fall):
    me = meta[META_ME]
    for d, slot in enumerate((s0, s1, s2, s3)):
        j = me ^ d

        @pl.when(j >= 1)
        def _():
            rise[jnp.maximum(j - 1, 0)] = slot[1:3]

        @pl.when(j <= REACH - 1)
        def _():
            fall[jnp.minimum(j, REACH - 1)] = slot[1:3]


def edges(meta, slots):
    total = slots[0].shape[1]
    out = jax.ShapeDtypeStruct((REACH, 2, total, 128), BF)
    return call(edge_kernel, (out, out), [SM] + [VM] * 4, (VM, VM), [], 0, 4 * REACH * 2 * total * 128 * 2, "edges")(
        meta, *slots
    )


def load_window(meta, slots, below, above, own, window, sems):
    me = meta[META_ME]
    copies = []
    for d, slot in enumerate(slots):
        j = me ^ d
        copies.append(pltpu.make_async_copy(slot.at[0], own.at[j], sems.at[0, d]))
        copies.append(pltpu.make_async_copy(slot.at[pl.ds(1, 2)], window.at[REACH + j], sems.at[1, d]))
    for k in range(REACH):
        copies.append(pltpu.make_async_copy(below.at[k], window.at[k], sems.at[2, k]))
        copies.append(pltpu.make_async_copy(above.at[k], window.at[REACH + PLANE + k], sems.at[3, k]))
    for copy in copies:
        copy.start()
    return copies


def scene_kernel(frame, meta, s0, s1, s2, s3, below, above, o0, o1, o2, o3, sums, found, own, window, held, sems):
    finish(load_window(meta, (s0, s1, s2, s3), below, above, own, window, sems))
    me = meta[META_ME]
    total = own.shape[1]
    parts = total // frame

    @pl.loop(0, parts * PLANE)
    def _(i):
        m, j = i // PLANE, i % PLANE
        r = pl.ds(pl.multiple_of(m * frame, frame), frame)
        q = own[j, r, :]
        first, second = only_first(q), only_second(q)
        held[...] = jnp.zeros_like(held)

        @pl.loop(meta[META_SCENES + i * 2], meta[META_SCENES + i * 2 + 1])
        def _(w):
            k, v = window[w, 0, r, :], window[w, 1, r, :]
            one = jnp.exp(dot(first, k, NT))
            two = jnp.exp(dot(second, k, NT))
            held[0] += pick(dot(one.astype(BF), v), dot(two.astype(BF), v))
            for h, weights in ((1, one), (2, two)):
                tally = weights[:, 0:128]
                for start in range(128, frame, 128):
                    tally = tally + weights[:, start : start + 128]
                held[h] += tally

        lane = pick(
            jnp.broadcast_to(jnp.sum(held[1], axis=-1, keepdims=True), (frame, 128)),
            jnp.broadcast_to(jnp.sum(held[2], axis=-1, keepdims=True), (frame, 128)),
        )
        inverse = 1.0 / lane
        sums[j, r, :] = inverse
        found[j, r, :] = held[0] * inverse

    for d, out in enumerate((o0, o1, o2, o3)):
        out[...] = found[me ^ d].astype(BF)


def scene(meta, slots, below, above, frame):
    total = slots[0].shape[1]
    out = jax.ShapeDtypeStruct((total, 128), BF)
    wide = 2 * REACH + PLANE
    return call(
        functools.partial(scene_kernel, frame),
        (out,) * 4 + (jax.ShapeDtypeStruct((PLANE, total, 128), F32),) * 2,
        [SM] + [ANY] * 6,
        (VM,) * 6,
        [
            pltpu.VMEM((PLANE, total, 128), BF),
            pltpu.VMEM((wide, 2, total, 128), BF),
            pltpu.VMEM((3, frame, 128), F32),
            pltpu.SemaphoreType.DMA((4, PLANE)),
        ],
        4 * PLANE * total * PLANE * frame * 128 * 2,
        4 * wide * total * 128,
        "scene",
    )(meta, *slots, below, above)


def output_kernel(meta, w_out, o0, o1, o2, o3, attended, part, weight, sems):
    copies = fetch(meta, *w_out, weight, sems)
    me = meta[META_ME]
    model = part.shape[1]
    for d, slot in enumerate((o0, o1, o2, o3)):
        attended[:, pl.ds(pl.multiple_of((me ^ d) * 128, 128), 128)] = slot[...]
    finish(copies)
    for start in range(0, model, 256):
        part[:, start : start + 256] = dot(attended[...], weight[start : start + 256, :], NT).astype(BF)


def outputs(meta, w_out, slots, width, model):
    total = slots[0].shape[0]
    return call(
        with_weights(output_kernel, 1, [w_out]),
        (jax.ShapeDtypeStruct((total, width), BF), jax.ShapeDtypeStruct((total, model), BF)),
        [SM] + [HBM] * w_out.count + [VM] * 4,
        (VM, VM),
        [pltpu.VMEM((model, width), BF), pltpu.SemaphoreType.DMA((PIECES,))],
        2 * total * model * width,
        2 * model * width,
        "outputs",
    )(meta, *w_out.sources, *slots)


def feed_back_kernel(meta, w_down, w_up, g, slope, norms, d_mlp, d_hidden, part, up, down, sems):
    copies = fetch(meta, *w_down, down, sems.at[0])
    later = fetch(meta, *w_up, up, sems.at[1])
    total, model = g.shape
    hidden = up.shape[1]

    @pl.loop(0, total // 64)
    def _(i):
        r = pl.ds(pl.multiple_of(i * 64, 64), 64)
        d_mlp[r, :] = (g[r, :].astype(F32) * norms[5:6, :]).astype(BF)

    finish(copies)
    step = 256
    for start in range(0, hidden, step):
        d_active = dot(d_mlp[...], down[:, start : start + step])
        d_hidden[:, start : start + step] = (d_active * slope[:, start : start + step].astype(F32)).astype(BF)
    finish(later)
    for start in range(0, model, 256):
        part[:, start : start + 256] = dot(d_hidden[...], up[start : start + 256, :], NT).astype(BF)


def feed_back(meta, weights, g, slope, norms):
    total, model = g.shape
    hidden = slope.shape[1]
    sources = sources_of(weights)
    return call(
        with_weights(feed_back_kernel, 1, weights),
        (
            jax.ShapeDtypeStruct((total, model), BF),
            jax.ShapeDtypeStruct((total, hidden), BF),
            jax.ShapeDtypeStruct((total, model), BF),
        ),
        [SM] + [HBM] * len(sources) + [VM] * 3,
        (VM,) * 3,
        [
            pltpu.VMEM((model, hidden), BF),
            pltpu.VMEM((model, hidden), BF),
            pltpu.SemaphoreType.DMA((2, PIECES)),
        ],
        4 * total * model * hidden,
        8 * model * hidden,
        "feed_back",
    )(meta, *sources, g, slope, norms)


def weight_grad_kernel(base, widths, meta, *refs):
    count = len(widths)
    lefts, rights = refs[:count], refs[count : 2 * count]
    model = lefts[0].shape[1]
    if base is None:
        whole = refs[2 * count]
        for b in range(0, model, 256):
            start = 0
            for left, right, width in zip(lefts, rights, widths):
                whole[b : b + 256, start : start + width] = dot(left[:, b : b + 256], right[...], TN).astype(BF)
                start += width
        return
    parts, (staged, sems) = refs[2 * count : 2 * count + 4], refs[2 * count + 4 :]
    quarter, rows = parts[0].shape[0], parts[0].shape[1]
    block = 256
    per = block // rows

    def copy_out(b, act):
        slot = b % 2
        for s in range(per):
            place = meta[base + b * per + s]
            source = staged.at[slot, pl.ds(s * rows, rows), :]
            for part, out in enumerate(parts):

                @pl.when(place // quarter == part)
                def _():
                    getattr(pltpu.make_async_copy(source, out.at[lax.rem(place, quarter)], sems.at[slot, s]), act)()

    for b in range(model // block):
        if b >= 2:
            copy_out(b - 2, "wait")
        start = 0
        for left, right, width in zip(lefts, rights, widths):
            staged[b % 2, :, start : start + width] = dot(
                left[:, b * block : (b + 1) * block], right[...], TN
            ).astype(BF)
            start += width
        copy_out(b, "start")
    for b in range(max(0, model // block - 2), model // block):
        copy_out(b, "wait")


def weight_grad(meta, base, lefts, rights, name):
    widths = [right.shape[1] for right in rights]
    total, model = lefts[0].shape
    rows = model // PIECES
    wide = sum(widths)
    out = jax.ShapeDtypeStruct((PIECES // 4, rows, wide), BF)
    whole = base is None
    return call(
        functools.partial(weight_grad_kernel, base, widths),
        jax.ShapeDtypeStruct((model, wide), BF) if whole else (out,) * 4,
        [SM] + [VM] * (2 * len(widths)),
        VM if whole else (ANY,) * 4,
        [] if whole else [pltpu.VMEM((2, 256, wide), BF), pltpu.SemaphoreType.DMA((2, 256 // rows))],
        2 * total * model * wide,
        2 * model * wide + 2 * total * (model + wide),
        name,
    )(meta, *lefts, *rights)


def norm_back_kernel(frame, count, meta, *refs):
    inner = count > 2
    g, x, one, two, norms = refs[:5]
    if inner:
        pa, pb = refs[5:7]
        ma, mb = refs[7:9] if count > 3 else (None, None)
        out, d_branch, sums, tally = refs[-4:]
        gain = norms[3:4, :]
    else:
        out, sums, tally = refs[-3:]
        gain = norms[0:1, :]
    total, model = x.shape
    core = meta[META_CORE]
    rows = 64
    tally[...] = jnp.zeros_like(tally)

    @pl.loop(0, total // rows)
    def _(i):
        r = pl.ds(pl.multiple_of(i * rows, rows), rows)
        unit, scale = norm_parts(x[r, :].astype(F32))
        d = one[r, :].astype(F32) + two[r, :].astype(F32)
        dg = d * gain
        mean = jnp.mean(dg, axis=-1, keepdims=True)
        slant = jnp.mean(dg * unit, axis=-1, keepdims=True)
        before = g[r, :].astype(F32)
        after = before + scale * (dg - mean - unit * slant)
        out[r, :] = after
        if inner:
            d_branch[r, :] = (after * norms[2:3, :]).astype(BF)

        @pl.when((i // (frame // 2 // rows)) % 2 == core)
        def _():
            def add(k, values):
                tally[k] += jnp.sum(values.reshape(rows // 8, 8, model), axis=0)

            add(0, d * unit)
            add(1, d)
            if inner:
                add(2, after * (pa[r, :].astype(F32) + pb[r, :].astype(F32)))
            if count > 3:
                add(3, before * (ma[r, :].astype(F32) + mb[r, :].astype(F32)))

    sums[...] = jnp.sum(tally[...], axis=1)


def norm_back(meta, g, x, one, two, norms, frame, extra=None):
    total, model = x.shape
    inner = extra is not None
    count = 2 + len(extra) // 2 if inner else 2
    outs = [jax.ShapeDtypeStruct((total, model), F32)]
    if inner:
        outs.append(jax.ShapeDtypeStruct((total, model), BF))
    outs.append(jax.ShapeDtypeStruct((count, model), F32))
    return call(
        functools.partial(norm_back_kernel, frame, count),
        tuple(outs),
        [SM] + [VM] * (5 + len(extra or ())),
        (VM,) * len(outs),
        [pltpu.VMEM((count, 8, model), F32)],
        20 * total * model,
        16 * total * model,
        "norm_back_inner" if inner else "norm_back",
    )(meta, g, x, one, two, norms, *(extra or ()))


def project_back(normed, weight, gains, matrix, take, d_projected, sums):
    width = gains.shape[1]
    total = normed.shape[0]
    rows, lanes = 256, 256
    sums[...] = jnp.zeros_like(sums)
    for part in range(2):
        for start in range(0, width, lanes):
            columns = part * width + start

            @pl.loop(0, total // rows)
            def _(i):
                r = pl.ds(pl.multiple_of(i * rows, rows), rows)
                unit, scale = head_parts(dot(normed[r, :], weight[:, columns : columns + lanes]), matrix)
                d = take(part, r, start, lanes)
                dg = d * gains[part : part + 1, start : start + lanes]
                mean = head_mean(dg, matrix)
                slant = head_mean(dg * unit, matrix)
                d_projected[r, columns : columns + lanes] = (scale * (dg - mean - unit * slant)).astype(BF)
                tally = jnp.sum((d * unit).reshape(rows // 8, 8, lanes), axis=0)
                sums[part * 8 : part * 8 + 8, start : start + lanes] += tally


def frame_back_kernel(frame, head, meta, w_in, w_out, d_branch, normed, qkv, gains, d_projected, part, sums, weight, out, d_att, dq, dk, sems):
    copies = fetch(meta, *w_out, out, sems.at[1])
    later = fetch(meta, *w_in, weight, sems.at[0])
    total, model = normed.shape
    width = gains.shape[1]
    finish(copies)
    for start in range(0, width, 256):
        d_att[:, start : start + 256] = dot(d_branch[...], out[:, start : start + 256]).astype(BF)
    pairs = width // 128

    @pl.loop(0, (total // frame) * pairs)
    def _(i):
        r = pl.ds(pl.multiple_of((i // pairs) * frame, frame), frame)
        column = pl.multiple_of((i % pairs) * 128, 128)
        lanes = pl.ds(column, 128)
        q, k, v = qkv[0, r, lanes], qkv[1, r, lanes], qkv[2, r, lanes]
        d_out = d_att[r, lanes]
        found = []
        for mask in (only_first, only_second):
            weights = jnp.exp(dot(k, mask(q), NT))
            probs = weights * (1.0 / jnp.sum(weights, axis=0, keepdims=True))
            d_probs = dot(v, mask(d_out), NT)
            delta = jnp.sum(probs * d_probs, axis=0, keepdims=True)
            d_scores = (probs * (d_probs - delta)).astype(BF)
            found.append((dot(d_scores, k, TN), dot(d_scores, q), dot(probs.astype(BF), d_out)))
        dq[r, lanes] = pick(found[0][0], found[1][0]) * HEAD_SCALE
        dk[r, lanes] = pick(found[0][1], found[1][1])
        d_projected[r, pl.ds(pl.multiple_of(2 * width + column, 128), 128)] = pick(found[0][2], found[1][2]).astype(BF)

    def take(which, r, start, lanes):
        return (dq, dk)[which][r, start : start + lanes]

    finish(later)
    project_back(normed, weight, gains, head_matrix(256, head), take, d_projected, sums)
    for start in range(0, model, 256):
        part[:, start : start + 256] = dot(d_projected[...], weight[start : start + 256, :], NT).astype(BF)


def frame_back(meta, weights, d_branch, normed, qkv, gains, frame, head):
    total, model = normed.shape
    width = gains.shape[1]
    sources = sources_of(weights)
    return call(
        with_weights(functools.partial(frame_back_kernel, frame, head), 1, weights),
        (
            jax.ShapeDtypeStruct((total, 3 * width), BF),
            jax.ShapeDtypeStruct((total, model), BF),
            jax.ShapeDtypeStruct((16, width), F32),
        ),
        [SM] + [HBM] * len(sources) + [VM] * 4,
        (VM,) * 3,
        [
            pltpu.VMEM((model, 3 * width), BF),
            pltpu.VMEM((model, width), BF),
            pltpu.VMEM((total, width), BF),
            pltpu.VMEM((total, width), F32),
            pltpu.VMEM((total, width), F32),
            pltpu.SemaphoreType.DMA((2, PIECES)),
        ],
        12 * total * model * width,
        8 * model * width,
        "frame_back",
    )(meta, *sources, d_branch, normed, qkv, gains)


def attended_back_kernel(meta, w_out, d_branch, s0, s1, s2, s3, weight, held, sems):
    finish(fetch(meta, *w_out, weight, sems))
    me = meta[META_ME]
    width = weight.shape[1]
    for start in range(0, width, 256):
        held[:, start : start + 256] = dot(d_branch[...], weight[:, start : start + 256]).astype(BF)
    for d, slot in enumerate((s0, s1, s2, s3)):
        slot[...] = held[:, pl.ds(pl.multiple_of((me ^ d) * 128, 128), 128)]


def attended_back(meta, w_out, d_branch, width):
    total, model = d_branch.shape
    return call(
        with_weights(attended_back_kernel, 1, [w_out]),
        (jax.ShapeDtypeStruct((total, 128), BF),) * 4,
        [SM] + [HBM] * w_out.count + [VM],
        (VM,) * 4,
        [
            pltpu.VMEM((model, width), BF),
            pltpu.VMEM((total, width), BF),
            pltpu.SemaphoreType.DMA((PIECES,)),
        ],
        2 * total * model * width,
        2 * model * width,
        "attended_back",
    )(meta, *w_out.sources, d_branch)


def scene_back_kernel(frame, meta, s0, s1, s2, s3, below, above, sums, whole, g0, g1, g2, g3, q0, q1, q2, q3, d_own, d_below, d_above, own, window, d_out, delta, dq, d_window, sems, more):
    copies = load_window(meta, (s0, s1, s2, s3), below, above, own, window, sems)
    me = meta[META_ME]
    for d, slot in enumerate((g0, g1, g2, g3)):
        copies.append(pltpu.make_async_copy(slot, d_out.at[me ^ d], more.at[d]))
        copies[-1].start()
    d_window[...] = jnp.zeros_like(d_window)
    finish(copies)
    total = own.shape[1]
    parts = total // frame

    @pl.loop(0, parts * PLANE)
    def _(i):
        m, j = i // PLANE, i % PLANE
        r = pl.ds(pl.multiple_of(m * frame, frame), frame)
        q, go = own[j, r, :], d_out[j, r, :]
        product = go.astype(F32) * whole[j, r, :]
        inverse = sums[j, r, :]
        heads = []
        for mask, lane in ((only_first, 0), (only_second, 64)):
            heads.append(
                (mask(q), mask(go), inverse[:, lane : lane + 1], jnp.sum(mask(product), axis=-1, keepdims=True))
            )
        dq[...] = jnp.zeros_like(dq)

        @pl.loop(meta[META_SCENES + i * 2], meta[META_SCENES + i * 2 + 1])
        def _(w):
            k, v = window[w, 0, r, :], window[w, 1, r, :]
            found = []
            for head_q, head_go, scale, shift in heads:
                probs = jnp.exp(dot(head_q, k, NT)) * scale
                d_scores = (probs * (dot(head_go, v, NT) - shift)).astype(BF)
                found.append((dot(d_scores, k), dot(d_scores, q, TN), dot(probs.astype(BF), go, TN)))
            dq[...] += pick(found[0][0], found[1][0])
            d_window[w, 0, r, :] += pick(found[0][1], found[1][1])
            d_window[w, 1, r, :] += pick(found[0][2], found[1][2])

        delta[j, r, :] = dq[...] * HEAD_SCALE

    for d, out in enumerate((q0, q1, q2, q3)):
        out[...] = delta[me ^ d].astype(BF)
    for k in range(PLANE):
        d_own[k] = d_window[REACH + k]
    for k in range(REACH):
        d_below[k] = d_window[k].astype(BF)
        d_above[k] = d_window[REACH + PLANE + k].astype(BF)


def scene_back(meta, slots, below, above, sums, found, d_found, frame):
    total = slots[0].shape[1]
    wide = 2 * REACH + PLANE
    out = jax.ShapeDtypeStruct((total, 128), BF)
    edge = jax.ShapeDtypeStruct((REACH, 2, total, 128), BF)
    return call(
        functools.partial(scene_back_kernel, frame),
        (out,) * 4 + (jax.ShapeDtypeStruct((PLANE, 2, total, 128), F32), edge, edge),
        [SM] + [ANY] * 6 + [VM] * 2 + [ANY] * 4,
        (VM,) * 7,
        [
            pltpu.VMEM((PLANE, total, 128), BF),
            pltpu.VMEM((wide, 2, total, 128), BF),
            pltpu.VMEM((PLANE, total, 128), BF),
            pltpu.VMEM((PLANE, total, 128), F32),
            pltpu.VMEM((frame, 128), F32),
            pltpu.VMEM((wide, 2, total, 128), F32),
            pltpu.SemaphoreType.DMA((4, PLANE)),
            pltpu.SemaphoreType.DMA((PLANE,)),
        ],
        10 * PLANE * total * PLANE * frame * 128 * 2,
        8 * wide * total * 128,
        "scene_back",
    )(meta, *slots, below, above, sums, found, *d_found)


def edge_sum_kernel(meta, d_own, from_below, from_above, t0, t1, t2, t3):
    me = meta[META_ME]
    for d, out in enumerate((t0, t1, t2, t3)):
        j = me ^ d
        low = jnp.where(j <= REACH - 1, 1.0, 0.0)
        high = jnp.where(j >= 1, 1.0, 0.0)
        at, top = jnp.minimum(j, REACH - 1), jnp.maximum(j - 1, 0)
        for part in range(2):
            values = d_own[j, part] + low * from_below[at, part].astype(F32)
            out[part] = (values + high * from_above[top, part].astype(F32)).astype(BF)


def edge_sum(meta, d_own, from_below, from_above):
    total = d_own.shape[2]
    out = jax.ShapeDtypeStruct((2, total, 128), BF)
    return call(
        edge_sum_kernel,
        (out,) * 4,
        [SM, VM, VM, VM],
        (VM,) * 4,
        [],
        8 * PLANE * total * 128,
        20 * PLANE * total * 128,
        "edge_sum",
    )(meta, d_own, from_below, from_above)


def queries_back_kernel(head, meta, w_in, q0, q1, q2, q3, t0, t1, t2, t3, normed, gains, d_projected, part, sums, weight, dq, dk, sems):
    copies = fetch(meta, *w_in, weight, sems)
    me = meta[META_ME]
    model = normed.shape[1]
    width = gains.shape[1]
    for d, (query, pair) in enumerate(zip((q0, q1, q2, q3), (t0, t1, t2, t3))):
        column = pl.multiple_of((me ^ d) * 128, 128)
        dq[:, pl.ds(column, 128)] = query[...].astype(F32)
        dk[:, pl.ds(column, 128)] = pair[0].astype(F32)
        d_projected[:, pl.ds(pl.multiple_of(2 * width + column, 128), 128)] = pair[1]
    finish(copies)

    def take(which, r, start, lanes):
        return (dq, dk)[which][r, start : start + lanes]

    project_back(normed, weight, gains, head_matrix(256, head), take, d_projected, sums)
    for start in range(0, model, 256):
        part[:, start : start + 256] = dot(d_projected[...], weight[start : start + 256, :], NT).astype(BF)


def queries_back(meta, w_in, d_queries, d_pairs, normed, gains, head):
    total, model = normed.shape
    width = gains.shape[1]
    return call(
        with_weights(functools.partial(queries_back_kernel, head), 1, [w_in]),
        (
            jax.ShapeDtypeStruct((total, 3 * width), BF),
            jax.ShapeDtypeStruct((total, model), BF),
            jax.ShapeDtypeStruct((16, width), F32),
        ),
        [SM] + [HBM] * w_in.count + [VM] * 10,
        (VM,) * 3,
        [
            pltpu.VMEM((model, 3 * width), BF),
            pltpu.VMEM((total, width), F32),
            pltpu.VMEM((total, width), F32),
            pltpu.SemaphoreType.DMA((PIECES,)),
        ],
        10 * total * model * width,
        8 * model * width,
        "queries_back",
    )(meta, *w_in.sources, *d_queries, *d_pairs, normed, gains)


META_CORE = 5 * PIECES
META_ME = META_CORE + 1
META_SCENES = META_ME + 1


def body(tokens, cotangent, scene_ids, input_weight, output_weight, up_weight, down_weight, norm_params, head_gains):
    portions, _, share, model = tokens.shape
    frame = 2 * share
    total = portions * frame
    head = head_gains.shape[2]
    width = input_weight.shape[3]
    routes = Routes(lax.axis_size("frames"))
    n = routes.n
    index, core = lax.axis_index("frames"), lax.axis_index("mp")
    plain = n != PIECES

    identity = jnp.arange(PIECES, dtype=jnp.int32)
    tables = [identity] * 5 if plain else routes.tables()
    scene_here = scene_ids[:, (index // PLANE) * PLANE + jnp.arange(PLANE)]
    before = jnp.sum(scene_ids[:, None, :] < scene_here[:, :, None], axis=-1)
    until = jnp.sum(scene_ids[:, None, :] <= scene_here[:, :, None], axis=-1)
    spans = jnp.stack([before, until], axis=-1) - (index // PLANE) * PLANE + REACH
    meta = jnp.concatenate(
        [*tables, core[None], (index % PLANE)[None], spans.reshape(-1)]
    ).astype(jnp.int32)

    def all_rows(block):
        own = block[:, 0]
        other = routes.swap(own)
        both = jnp.where(core == 0, jnp.stack([own, other], 1), jnp.stack([other, own], 1))
        return both.reshape(total, model)

    def own_rows(values):
        return lax.dynamic_index_in_dim(values.reshape(portions, 2, share, -1), core, 1, keepdims=True)

    gains = [jnp.tile(head_gains[layer], (1, width // head)) for layer in range(2)]
    clock = Clock(not plain)
    late, close = clock.late, clock.close
    joined = [
        jnp.concatenate([input_weight[layer].reshape(-1, 3 * width), output_weight[layer]], axis=1)
        for layer in range(2)
    ]

    def gather(shard, line_first, name):
        if plain or line_first is None:
            return Whole(lax.all_gather(shard, "frames", axis=0, tiled=True))
        return Gather(routes, clock, shard, line_first, name)

    def scatter(line_last, name, lefts, rights):
        if plain or line_last is None:
            grad = weight_grad(meta, None, lefts, rights, name)
            ready[name] = grad
            summed = lax.psum_scatter(grad.astype(F32) if plain else grad, "frames", scatter_dimension=0, tiled=True)
            return Whole(summed.astype(F32))
        parts = weight_grad(meta, (3 if line_last else 2) * PIECES, lefts, rights, name)
        ready[name] = parts[2]
        return Scatter(routes, clock, parts, line_last, name)

    ready = {}

    ga0 = gather(joined[0], True, "input0")
    gu0 = gather(up_weight[0], True, "up0")
    gd0 = gather(down_weight[0], False, "down0")
    ga1 = gather(joined[1], False, "input1")
    gu1 = gather(up_weight[1], False, "up1")
    gd1 = gather(down_weight[1], False, "down1")
    ga0.ring(3)
    for each in (gd0, ga1, gu1, gd1):
        each.one()
    rows = all_rows(tokens)
    d_result = all_rows(cotangent)
    close(rows, d_result)
    ga0.one()
    ga0.two(0)
    gu0.ring(3)
    close()
    ga0.two(1)
    gd0.ring()
    close()
    in0, out0 = ga0.end(0, 3 * width), ga0.end(3 * width, width)
    gu0.one()
    gd0.ring()
    normed0, qkv0, attended0, a0 = attention_frame(
        meta, [in0, out0], late(rows), norm_params[0], gains[0], frame, head
    )
    close(a0)
    b0 = clock.add(routes.swap(a0))
    gu0.two(0)
    gu0.two(1)
    gd0.ring()
    ga1.ring()
    close()
    up0 = gu0.end()
    gd0.two(0)
    ga1.ring()
    mid0, normed_mid0, active0, slope0 = feed_up(meta, up0, rows, a0, late(b0), norm_params[0])
    close(active0)
    gd0.two(1)
    ga1.ring()
    close()
    down0 = gd0.end()
    ga1.two(0)
    ga1.two(1)
    gu1.ring(2)
    m0 = feed_down(meta, down0, late(active0), model)
    n0 = clock.add(routes.swap(m0))
    close(m0)
    in1, out1 = ga1.end(0, 3 * width), ga1.end(3 * width, width)
    gu1.two(0)
    gu1.ring()
    x1, normed1, *slots = queries(
        meta, in1, mid0, m0, late(n0), norm_params[0], norm_params[1], gains[1], head
    )
    close(slots[0])
    slots = routes.members(late(slots))
    gd1.ring()
    close(*slots[1:])
    rise, fall = edges(meta, late(slots))
    below, above = routes.up(rise), routes.down(fall)
    gu1.two(1)
    close(below, above)
    gd1.ring()
    gd1.two(0)
    *found, sums, whole_found = scene(meta, slots, late(below), above, frame)
    close(found[0])
    home = routes.members(late(found))
    gd1.ring()
    close(*home[1:])
    attended1, a1 = outputs(meta, out1, late(home), width, model)
    b1 = routes.swap(a1)
    close(b1)
    up1 = gu1.end()
    gd1.two(1)
    mid1, normed_mid1, active1, slope1 = feed_up(meta, up1, x1, a1, late(b1), norm_params[1])
    close(active1)

    down1 = gd1.end()
    d_mlp, d_hidden, p = feed_back(meta, [down1, up1], late(d_result), slope1, norm_params[1])
    close(p)
    q = clock.add(routes.swap(p))
    sd1 = scatter(True, "down_grad1", [late(d_mlp)], [active1])
    close(ready["down_grad1"])
    sd1.two(1)
    g, d_branch, inner1 = norm_back(meta, d_result, mid1, p, late(q), norm_params[1], frame, (a1, b1))
    d_home = attended_back(meta, out1, d_branch, width)
    su1 = scatter(True, "up_grad1", [late(normed_mid1)], [d_hidden])
    close(d_home[0], ready["up_grad1"])
    d_found = routes.members(late(d_home))
    close(*d_found[1:])
    sd1.one()
    sd1.two(0)
    *d_queries, d_own, d_below, d_above = scene_back(
        meta, slots, late(below), above, sums, whole_found, d_found, frame
    )
    close(d_own)
    from_above, from_below = routes.down(late(d_below)), routes.up(late(d_above))
    d_queries = routes.members(late(d_queries))
    su1.two(1)
    m1 = feed_down(meta, down1, late(active1), model)
    close(m1, from_above, from_below, *d_queries[1:])
    n1 = clock.add(routes.swap(m1))
    sd1.ring()
    pairs = routes.members(edge_sum(meta, d_own, late(from_below), from_above))
    close(*pairs[1:])
    su1.one()
    sd1.ring()
    d_projected, p, gain1 = queries_back(meta, in1, d_queries, late(pairs), normed1, gains[1], head)
    close(p)
    q = clock.add(routes.swap(p))
    su1.two(0)
    sd1.ring()
    sa1 = scatter(False, "input_grad1", [normed1, d_branch], [late(d_projected), attended1])
    close(ready["input_grad1"])
    sa1.two(0)
    su1.ring()
    own_mlp = own_rows(m1).astype(F32) + own_rows(n1).astype(F32)
    result = own_rows(mid1) + norm_params[1, 5] * own_mlp
    scale1 = jnp.sum(cotangent.astype(F32).reshape(-1, model) * own_mlp.reshape(-1, model), axis=0)
    g, outer1 = norm_back(meta, g, x1, p, late(q), norm_params[1], frame)

    d_mlp, d_hidden, p = feed_back(meta, [down0, up0], g, slope0, norm_params[0])
    close(p)
    q = clock.add(routes.swap(p))
    sa1.two(1)
    sa1.ring()
    su1.ring()
    sd0 = scatter(False, "down_grad0", [late(d_mlp)], [active0])
    close(ready["down_grad0"])
    sd0.two(0)
    sa1.ring()
    su1.ring()
    su0 = scatter(True, "up_grad0", [late(normed_mid0)], [d_hidden])
    g, d_branch, inner0 = norm_back(meta, g, mid0, p, late(q), norm_params[0], frame, (a0, b0, m0, n0))
    close(d_branch, ready["up_grad0"])
    sd0.two(1)
    su0.two(1)
    sa1.ring()
    sd0.ring()
    d_projected, p, gain0 = frame_back(
        meta, [in0, out0], late(d_branch), normed0, qkv0, gains[0], frame, head
    )
    close(p)
    q = clock.add(routes.swap(late(p)))
    su0.two(0)
    sd0.ring()
    sa1.one()
    sa0 = scatter(False, "input_grad0", [normed0, d_branch], [late(d_projected), attended0])
    close(ready["input_grad0"])
    su0.one()
    sa0.two(0)
    sd0.ring()
    g, outer0 = norm_back(meta, g, rows, p, late(q), norm_params[0], frame)
    token_grad = own_rows(g)
    close(g)

    norm_rows = [
        jnp.stack([outer[0], outer[1], inner[2], inner[0], inner[1], scale])
        for outer, inner, scale in ((outer0, inner0, inner0[3]), (outer1, inner1, scale1))
    ]
    gain_rows = [
        jnp.sum(gain.reshape(2, 8, width // head, head), axis=(1, 2)).reshape(1, -1)
        for gain in (gain0, gain1)
    ]
    gain_rows = jnp.pad(jnp.concatenate(gain_rows, axis=1), ((0, 0), (0, model - 4 * head)))
    small = jnp.concatenate([*norm_rows, gain_rows])
    small = small + routes.swap(small)
    distances = [2**i for i in range(n.bit_length() - 1)]

    def sum_step(block, distance):
        return block + clock.add(routes.member(late(block), distance))

    small = sum_step(small, distances[0])
    sa0.two(1)
    sa0.ring()
    su0.ring()
    close()
    small = sum_step(small, distances[1])
    sd0.one()
    sa0.ring()
    su0.ring()
    close()
    for distance in distances[2:]:
        small = sum_step(small, distance)
    sa0.ring()
    su0.ring()
    sa0.one()
    norm_grad = small[: 2 * 6].reshape(2, 6, model)
    gain_grad = small[2 * 6, : 4 * head].reshape(2, 2, head)
    return (
        result.astype(BF),
        token_grad,
        jnp.stack([step.run[:, : 3 * width].reshape(-1, 3, width) for step in (sa0, sa1)]),
        jnp.stack([step.run[:, 3 * width :] for step in (sa0, sa1)]),
        jnp.stack([step.run for step in (su0, su1)]),
        jnp.stack([step.run for step in (sd0, sd1)]),
        norm_grad,
        gain_grad,
    )


def solution(mesh):
    rows = P(None, "frames", "mp", None)
    shard = P(None, "frames", "mp")
    wide = P(None, "frames", None, "mp")
    return jax.shard_map(
        body,
        mesh=mesh,
        in_specs=(rows, rows, P(), wide, shard, shard, shard, P(), P()),
        out_specs=(rows, rows, wide, shard, shard, shard, P(), P()),
        check_vma=False,
    )
```

```python
import functools

import jax
import jax.numpy as jnp
import numpy as np
from jax import lax
from jax.experimental import pallas as pl
from jax.experimental.pallas import tpu as pltpu
from jax.sharding import PartitionSpec as P

BF = jnp.bfloat16
F32 = jnp.float32
ROW_EPS = 1e-06
HEAD_EPS = 1e-05
PIECES = 16
SWAPS = 1
COST = 1
PLANE = 4
REACH = 3
AXES = ("frames", "mp")

NN = (((1,), (0,)), ((), ()))
NT = (((1,), (1,)), ((), ()))
TN = (((0,), (0,)), ((), ()))

VM = pl.BlockSpec(memory_space=pltpu.VMEM)
SM = pl.BlockSpec(memory_space=pltpu.SMEM)
ANY = pl.BlockSpec(memory_space=pl.ANY)
HBM = pl.BlockSpec(memory_space=pltpu.HBM)


def dot(left, right, dims=NN):
    return lax.dot_general(left, right, dims, preferred_element_type=F32)


def call(body, outs, in_specs, out_specs, scratch, flops, moved, name):
    return pl.pallas_call(
        body,
        out_shape=outs,
        in_specs=in_specs,
        out_specs=out_specs,
        scratch_shapes=scratch,
        compiler_params=pltpu.CompilerParams(vmem_limit_bytes=(60 if name in ("queries", "queries_back") else 18) * 1024 * 1024),
        cost_estimate=pl.CostEstimate(flops=flops // COST, bytes_accessed=moved // COST, transcendentals=0),
        name=name,
    )


class Routes:
    def __init__(self, n):
        lines = n // PLANE
        self.n, self.lines = n, lines
        order = [0] + list(range(1, lines, 2)) + sorted(range(2, lines, 2), reverse=True)
        following = {z: order[(i + 1) % lines] for i, z in enumerate(order)}
        spot = {z: i for i, z in enumerate(order)}
        self.back = np.array([[order[(spot[z] - k) % lines] for z in range(lines)] for k in range(lines)], np.int32)
        self.steps = np.array([[(spot[z] - spot[w]) % lines for w in range(lines)] for z in range(lines)], np.int32)
        self.ring = [
            (f * 2 + c, (following[f // PLANE] * PLANE + f % PLANE) * 2 + c) for f in range(n) for c in range(2)
        ]
        self.one = [(f * 2 + c, (f ^ (1 + c)) * 2 + c) for f in range(n) for c in range(2)]
        self.two = [(f * 2 + c, (f ^ (2 - c)) * 2 + c) for f in range(n) for c in range(2)]

    def send(self, block, route):
        return lax.ppermute(block, AXES, route)

    def swap(self, block):
        return lax.ppermute(block, "mp", [(0, 1), (1, 0)])

    def swap_parts(self, block):
        if SWAPS == 1:
            return self.swap(block)
        rows = block.shape[0] // SWAPS
        return jnp.concatenate([self.swap(block[i * rows : (i + 1) * rows]) for i in range(SWAPS)])

    def member(self, block, distance):
        return lax.ppermute(block, "frames", [(f, f ^ distance) for f in range(self.n)])

    def members(self, blocks):
        return [blocks[0]] + [self.member(blocks[d], d) for d in range(1, PLANE)]

    def up(self, block):
        return lax.ppermute(block, "frames", [(f, f + PLANE) for f in range(self.n - PLANE)])

    def down(self, block):
        return lax.ppermute(block, "frames", [(f + PLANE, f) for f in range(self.n - PLANE)])

    def tables(self):
        frame, core = lax.axis_index("frames"), lax.axis_index("mp")
        low, high = 1 + core, 2 - core
        bits = jnp.arange(2, dtype=jnp.int32)
        line = PLANE * jnp.asarray(self.back)[:, frame // PLANE]
        straight = PLANE * (frame // PLANE ^ jnp.arange(self.lines, dtype=jnp.int32))
        near = ((frame // low) % 2 ^ bits) * low
        far = ((frame // high) % 2 ^ bits) * high
        middle = line[None, :, None] + near[None, None, :] + far[:, None, None]
        first = line[None, None, :] + near[None, :, None] + far[:, None, None]
        direct = straight[None, None, :] + near[None, :, None] + far[:, None, None]
        every = jnp.arange(self.n, dtype=jnp.int32)
        k = jnp.repeat(jnp.asarray(self.steps)[frame // PLANE], PLANE)
        j = (every // low) % 2 ^ (frame // low) % 2
        h = (every // high) % 2 ^ (frame // high) % 2
        half = self.n // 2
        place_middle = h * half + k * 2 + j
        place_first = h * half + j * self.lines + k
        return [t.reshape(-1).astype(jnp.int32) for t in (middle, first, place_middle, place_first, direct)]


class Clock:
    def __init__(self, active):
        self.active, self.waited, self.pending = active, [], []

    def late(self, value):
        if not (self.active and self.waited):
            return value
        return lax.optimization_barrier((value, self.waited))[0]

    def add(self, value):
        self.pending.append(value)
        return value

    def step(self, *values):
        self.waited = list(values)

    def close(self, *values):
        self.waited, self.pending = self.pending + list(values), []


class Gather:
    def __init__(self, routes, clock, shard, line_first, name):
        self.routes, self.clock, self.line_first, self.name = routes, clock, line_first, name
        self.shard, self.pieces, self.direct = shard, [shard], False

    def send(self, block, route, step):
        with jax.named_scope(self.name + step):
            return self.clock.add(self.routes.send(self.clock.late(block), route))

    def ring(self, steps=1):
        for i in range(steps):
            if i:
                moved = self.routes.send(self.pieces[-1], self.routes.ring)
                self.clock.pending[-1] = moved
            else:
                moved = self.send(self.pieces[-1], self.routes.ring, "_ring")
            self.pieces.append(moved)
        if self.line_first and len(self.pieces) == self.routes.lines:
            self.line = jnp.stack(self.pieces)

    def straight(self):
        self.direct = True
        for k in range(1, self.routes.lines):
            with jax.named_scope(self.name + "_line"):
                self.pieces.append(self.clock.add(self.routes.member(self.clock.late(self.shard), PLANE * k)))
        self.line = jnp.stack(self.pieces)

    def one(self):
        if self.line_first:
            self.got = self.send(self.line, self.routes.one, "_one")
        else:
            self.pieces = [jnp.stack([self.shard, self.send(self.shard, self.routes.one, "_one")])]

    def near(self, half):
        if self.line_first:
            return (self.line, self.got)[half]
        if not hasattr(self, "pairs"):
            self.pairs = {}
        if half not in self.pairs:
            self.pairs[half] = jnp.concatenate(self.pieces[2 * half : 2 * half + 2])
        return self.pairs[half]

    def two(self, half):
        far = self.send(self.near(half), self.routes.two, "_two")
        self.far = (self.far if half else []) + [far]

    def end(self, start=0, width=None):
        sources = [self.near(0), self.near(1), *self.far]
        base = (4 if self.direct else 1) * PIECES if self.line_first else 0
        return Weight(sources, base, start, width)


class Scatter:
    def __init__(self, routes, clock, parts, line_last, name):
        self.routes, self.clock, self.line_last, self.name = routes, clock, line_last, name
        self.keep, self.give = parts[:2], parts[2:]
        self.got, self.at, self.run = [None, None], 0, None

    def send(self, block, route, step):
        with jax.named_scope(self.name + step):
            return self.clock.add(self.routes.send(self.clock.late(block), route))

    def two(self, half):
        self.got[half] = self.send(self.give[half], self.routes.two, "_two")

    def one(self):
        if self.line_last:
            block = self.keep[1].astype(F32) + self.got[1].astype(F32)
            self.more = self.send(block.astype(BF), self.routes.one, "_one")
        else:
            self.run = self.run[0] + self.send(self.run[1].astype(BF), self.routes.one, "_one").astype(F32)

    def local(self, k):
        if self.line_last:
            return self.keep[0][k].astype(F32) + self.got[0][k].astype(F32) + self.more[k].astype(F32)
        half, rows = k // 2, slice(2 * (k % 2), 2 * (k % 2) + 2)
        return self.keep[half][rows].astype(F32) + self.got[half][rows].astype(F32)

    def ring(self):
        if self.run is None:
            self.at, self.run = 1, self.local(1)
        moved = self.send(self.run.astype(BF), self.routes.ring, "_ring")
        self.at = (self.at + 1) % self.routes.lines
        self.run = self.local(self.at) + moved.astype(F32)


class Weight:
    def __init__(self, sources, base, start=0, width=None):
        self.sources, self.count = tuple(sources), len(sources)
        self.width = width or self.sources[0].shape[-1]
        self.plan = (base, start, self.width)


class Whole:
    def __init__(self, value):
        self.run = value

    def ring(self, steps=1):
        pass

    def one(self):
        pass

    def straight(self):
        pass

    def two(self, half):
        pass

    def end(self, start=0, width=None):
        return Weight([self.run], None, start, width)


def with_weights(kernel, before, weights):
    def run(*refs):
        at = before
        given = []
        for weight in weights:
            given.append((weight.plan, refs[at : at + weight.count]))
            at += weight.count
        return kernel(*refs[:before], *given, *refs[at:])

    return run


def sources_of(weights):
    return [source for weight in weights for source in weight.sources]


def fetch(meta, plan, sources, into, sems):
    base, start, width = plan
    columns = pl.ds(start, width)
    copies = []
    if base is None:
        rows = into.shape[0] // 4
        for q in range(4):
            part = pl.ds(q * rows, rows)
            copies.append(pltpu.make_async_copy(sources[0].at[part, columns], into.at[part, :], sems.at[q]))
    else:
        rows, quarter = into.shape[0] // PIECES, PIECES // 4
        for q in range(PIECES):
            source = sources[q // quarter].at[q % quarter, :, columns]
            row = pl.multiple_of(meta[base + q] * rows, rows)
            copies.append(pltpu.make_async_copy(source, into.at[pl.ds(row, rows), :], sems.at[q]))
    for copy in copies:
        copy.start()
    return copies


def finish(copies):
    for copy in copies:
        copy.wait()


def norm_parts(values):
    centred = values - jnp.mean(values, axis=-1, keepdims=True)
    scale = lax.rsqrt(jnp.mean(centred * centred, axis=-1, keepdims=True) + ROW_EPS)
    return centred * scale, scale


def head_matrix(width, head):
    row = lax.broadcasted_iota(jnp.int32, (width, width), 0) // head
    column = lax.broadcasted_iota(jnp.int32, (width, width), 1) // head
    return jnp.where(row == column, 1.0 / head, 0.0).astype(BF)


def head_mean(values, matrix):
    high = values.astype(BF)
    low = (values - high.astype(F32)).astype(BF)
    return dot(high, matrix) + dot(low, matrix)


def head_parts(values, matrix):
    centred = values - head_mean(values, matrix)
    scale = lax.rsqrt(head_mean(centred * centred, matrix) + HEAD_EPS)
    return centred * scale, scale


def project(normed, weight, gains, matrix, put, rows=256, lanes=256):
    width = gains.shape[1]
    total = normed.shape[0]
    factor = HEAD_SCALE

    for part in range(3):
        for start in range(0, width, lanes):
            columns = part * width + start

            @pl.loop(0, total // rows)
            def _(i):
                r = pl.ds(pl.multiple_of(i * rows, rows), rows)
                values = dot(normed[r, :], weight[:, columns : columns + lanes])
                if part < 2:
                    unit, _ = head_parts(values, matrix)
                    values = unit * gains[part : part + 1, start : start + lanes]
                values = values.astype(BF)
                if part == 0:
                    values = (values.astype(F32) * factor).astype(BF)
                put(part, r, start, lanes, values)


HEAD_SCALE = 0.125


def only_first(values):
    lane = lax.broadcasted_iota(jnp.int32, values.shape, 1)
    return jnp.where(lane < values.shape[1] // 2, values, jnp.zeros_like(values))


def only_second(values):
    lane = lax.broadcasted_iota(jnp.int32, values.shape, 1)
    return jnp.where(lane < values.shape[1] // 2, jnp.zeros_like(values), values)


def pick(first, second):
    lane = lax.broadcasted_iota(jnp.int32, first.shape, 1)
    return jnp.where(lane < first.shape[1] // 2, first, second)


def gelu_parts(v):
    size = jnp.abs(v)
    bell = jnp.exp(v * v * -0.5)
    t = 1.0 / (1.0 + size * 0.23164189)
    tail = t * (0.127414796 + t * (-0.142248368 + t * (0.7107068705 + t * (-0.7265760135 + t * 0.5307027145))))
    tail = tail * bell
    phi = jnp.where(v >= 0.0, 1.0 - tail, tail)
    return v * phi, phi + v * bell * 0.3989422804014327


def attention_frame_kernel(frame, head, meta, w_in, w_out, rows_ref, norms, gains, normed, qkv, attended, part, weight, out, sems):
    copies = fetch(meta, *w_in, weight, sems.at[0])
    later = fetch(meta, *w_out, out, sems.at[1])
    total, model = rows_ref.shape
    width = gains.shape[1]

    @pl.loop(0, total // 64)
    def _(i):
        r = pl.ds(pl.multiple_of(i * 64, 64), 64)
        unit, _ = norm_parts(rows_ref[r, :].astype(F32))
        normed[r, :] = (unit * norms[0:1, :] + norms[1:2, :]).astype(BF)

    finish(copies)
    matrix = head_matrix(256, head)

    def put(part, r, start, lanes, values):
        qkv[part, r, start : start + lanes] = values

    project(normed, weight, gains, matrix, put)
    pairs = width // 128

    @pl.loop(0, (total // frame) * pairs)
    def _(i):
        r = pl.ds(pl.multiple_of((i // pairs) * frame, frame), frame)
        lanes = pl.ds(pl.multiple_of((i % pairs) * 128, 128), 128)
        q, k, v = qkv[0, r, lanes], qkv[1, r, lanes], qkv[2, r, lanes]
        found = []
        for mask in (only_first, only_second):
            weights = jnp.exp(dot(mask(q), k, NT))
            found.append(dot(weights.astype(BF), v) / jnp.sum(weights, axis=-1, keepdims=True))
        attended[r, lanes] = pick(found[0], found[1]).astype(BF)

    finish(later)
    for start in range(0, model, 256):
        part[:, start : start + 256] = dot(attended[...], out[start : start + 256, :], NT).astype(BF)


def attention_frame(meta, weights, rows, norms, gains, frame, head):
    total, model = rows.shape
    width = gains.shape[1]
    sources = sources_of(weights)
    return call(
        with_weights(functools.partial(attention_frame_kernel, frame, head), 1, weights),
        (
            jax.ShapeDtypeStruct((total, model), BF),
            jax.ShapeDtypeStruct((3, total, width), BF),
            jax.ShapeDtypeStruct((total, width), BF),
            jax.ShapeDtypeStruct((total, model), BF),
        ),
        [SM] + [HBM] * len(sources) + [VM, VM, VM],
        (VM, VM, VM, VM),
        [
            pltpu.VMEM((model, 3 * width), BF),
            pltpu.VMEM((model, width), BF),
            pltpu.SemaphoreType.DMA((2, PIECES)),
        ],
        8 * total * model * width,
        2 * 4 * model * width,
        "attention_frame",
    )(meta, *sources, rows, norms, gains)


def feed_up_kernel(meta, w_up, x, one, two, norms, mid, normed, active, slope, up, sems):
    copies = fetch(meta, *w_up, up, sems)
    total, model = x.shape
    hidden = up.shape[1]

    @pl.loop(0, total // 64)
    def _(i):
        r = pl.ds(pl.multiple_of(i * 64, 64), 64)
        branch = one[r, :].astype(F32) + two[r, :].astype(F32)
        values = x[r, :].astype(F32) + norms[2:3, :] * branch
        mid[r, :] = values
        unit, _ = norm_parts(values)
        normed[r, :] = (unit * norms[3:4, :] + norms[4:5, :]).astype(BF)

    finish(copies)
    step, rows = 512, 256
    for start in range(0, hidden, step):

        @pl.loop(0, total // rows)
        def _(i):
            r = pl.ds(pl.multiple_of(i * rows, rows), rows)
            before = dot(normed[r, :], up[:, start : start + step])
            after_, rise = gelu_parts(before)
            active[r, start : start + step] = after_.astype(BF)
            slope[r, start : start + step] = rise.astype(BF)


def feed_up(meta, up, x, one, two, norms):
    total, model = x.shape
    hidden = up.width
    return call(
        with_weights(feed_up_kernel, 1, [up]),
        (
            jax.ShapeDtypeStruct((total, model), F32),
            jax.ShapeDtypeStruct((total, model), BF),
            jax.ShapeDtypeStruct((total, hidden), BF),
            jax.ShapeDtypeStruct((total, hidden), BF),
        ),
        [SM] + [HBM] * up.count + [VM] * 4,
        (VM,) * 4,
        [pltpu.VMEM((model, hidden), BF), pltpu.SemaphoreType.DMA((PIECES,))],
        2 * total * model * hidden,
        2 * model * hidden,
        "feed_up",
    )(meta, *up.sources, x, one, two, norms)


def feed_down_kernel(meta, w_down, active, part, down, sems):
    model = part.shape[1]
    finish(fetch(meta, *w_down, down, sems))
    for start in range(0, model, 256):
        part[:, start : start + 256] = dot(active[...], down[start : start + 256, :], NT).astype(BF)


def feed_down(meta, down, active, model):
    total, hidden = active.shape
    return call(
        with_weights(feed_down_kernel, 1, [down]),
        jax.ShapeDtypeStruct((total, model), BF),
        [SM] + [HBM] * down.count + [VM],
        VM,
        [pltpu.VMEM((model, hidden), BF), pltpu.SemaphoreType.DMA((PIECES,))],
        2 * total * model * hidden,
        2 * model * hidden,
        "feed_down",
    )(meta, *down.sources, active)


def queries_kernel(head, meta, w_in, mid, one, two, before, norms, gains, x, normed, s0, s1, s2, s3, weight, held, sems):
    copies = fetch(meta, *w_in, weight, sems)
    total, model = mid.shape
    width = gains.shape[1]
    me = meta[META_ME]

    @pl.loop(0, total // 64)
    def _(i):
        r = pl.ds(pl.multiple_of(i * 64, 64), 64)
        values = mid[r, :] + before[5:6, :] * (one[r, :].astype(F32) + two[r, :].astype(F32))
        x[r, :] = values
        unit, _ = norm_parts(values)
        normed[r, :] = (unit * norms[0:1, :] + norms[1:2, :]).astype(BF)

    finish(copies)

    def put(part, r, start, lanes, values):
        held[part, r, start : start + lanes] = values

    project(normed, weight, gains, head_matrix(256, head), put)
    for d, slot in enumerate((s0, s1, s2, s3)):
        lanes = pl.ds(pl.multiple_of((me ^ d) * 128, 128), 128)
        for part in range(3):
            slot[part] = held[part, :, lanes]


def queries(meta, w_in, mid, one, two, before, norms, gains, head):
    total, model = mid.shape
    width = gains.shape[1]
    slot = jax.ShapeDtypeStruct((3, total, 128), BF)
    return call(
        with_weights(functools.partial(queries_kernel, head), 1, [w_in]),
        (jax.ShapeDtypeStruct((total, model), F32), jax.ShapeDtypeStruct((total, model), BF)) + (slot,) * 4,
        [SM] + [HBM] * w_in.count + [VM] * 6,
        (VM,) * 6,
        [
            pltpu.VMEM((model, 3 * width), BF),
            pltpu.VMEM((3, total, width), BF),
            pltpu.SemaphoreType.DMA((PIECES,)),
        ],
        6 * total * model * width,
        8 * model * width,
        "queries",
    )(meta, *w_in.sources, mid, one, two, before, norms, gains)


def edge_kernel(meta, s0, s1, s2, s3, rise, fall):
    me = meta[META_ME]
    for d, slot in enumerate((s0, s1, s2, s3)):
        j = me ^ d

        @pl.when(j >= 1)
        def _():
            rise[jnp.maximum(j - 1, 0)] = slot[1:3]

        @pl.when(j <= REACH - 1)
        def _():
            fall[jnp.minimum(j, REACH - 1)] = slot[1:3]


def edges(meta, slots):
    total = slots[0].shape[1]
    out = jax.ShapeDtypeStruct((REACH, 2, total, 128), BF)
    return call(edge_kernel, (out, out), [SM] + [VM] * 4, (VM, VM), [], 0, 4 * REACH * 2 * total * 128 * 2, "edges")(
        meta, *slots
    )


def load_window(meta, slots, below, above, own, window, sems):
    me = meta[META_ME]
    copies = []
    for d, slot in enumerate(slots):
        j = me ^ d
        copies.append(pltpu.make_async_copy(slot.at[0], own.at[j], sems.at[0, d]))
        copies.append(pltpu.make_async_copy(slot.at[pl.ds(1, 2)], window.at[REACH + j], sems.at[1, d]))
    for k in range(REACH):
        copies.append(pltpu.make_async_copy(below.at[k], window.at[k], sems.at[2, k]))
        copies.append(pltpu.make_async_copy(above.at[k], window.at[REACH + PLANE + k], sems.at[3, k]))
    for copy in copies:
        copy.start()
    return copies


def scene_kernel(frame, meta, s0, s1, s2, s3, below, above, o0, o1, o2, o3, sums, found, own, window, held, sems):
    finish(load_window(meta, (s0, s1, s2, s3), below, above, own, window, sems))
    me = meta[META_ME]
    total = own.shape[1]
    parts = total // frame

    @pl.loop(0, parts * PLANE)
    def _(i):
        m, j = i // PLANE, i % PLANE
        r = pl.ds(pl.multiple_of(m * frame, frame), frame)
        q = own[j, r, :]
        first, second = only_first(q), only_second(q)
        held[...] = jnp.zeros_like(held)

        @pl.loop(meta[META_SCENES + i * 2], meta[META_SCENES + i * 2 + 1])
        def _(w):
            k, v = window[w, 0, r, :], window[w, 1, r, :]
            one = jnp.exp(dot(first, k, NT))
            two = jnp.exp(dot(second, k, NT))
            held[0] += pick(dot(one.astype(BF), v), dot(two.astype(BF), v))
            for h, weights in ((1, one), (2, two)):
                tally = weights[:, 0:128]
                for start in range(128, frame, 128):
                    tally = tally + weights[:, start : start + 128]
                held[h] += tally

        lane = pick(
            jnp.broadcast_to(jnp.sum(held[1], axis=-1, keepdims=True), (frame, 128)),
            jnp.broadcast_to(jnp.sum(held[2], axis=-1, keepdims=True), (frame, 128)),
        )
        inverse = 1.0 / lane
        sums[j, r, :] = inverse
        found[j, r, :] = held[0] * inverse

    for d, out in enumerate((o0, o1, o2, o3)):
        out[...] = found[me ^ d].astype(BF)


def scene(meta, slots, below, above, frame):
    total = slots[0].shape[1]
    out = jax.ShapeDtypeStruct((total, 128), BF)
    wide = 2 * REACH + PLANE
    return call(
        functools.partial(scene_kernel, frame),
        (out,) * 4 + (jax.ShapeDtypeStruct((PLANE, total, 128), F32),) * 2,
        [SM] + [ANY] * 6,
        (VM,) * 6,
        [
            pltpu.VMEM((PLANE, total, 128), BF),
            pltpu.VMEM((wide, 2, total, 128), BF),
            pltpu.VMEM((3, frame, 128), F32),
            pltpu.SemaphoreType.DMA((4, PLANE)),
        ],
        4 * PLANE * total * PLANE * frame * 128 * 2,
        4 * wide * total * 128,
        "scene",
    )(meta, *slots, below, above)


def output_kernel(meta, w_out, o0, o1, o2, o3, attended, part, weight, sems):
    copies = fetch(meta, *w_out, weight, sems)
    me = meta[META_ME]
    model = part.shape[1]
    for d, slot in enumerate((o0, o1, o2, o3)):
        attended[:, pl.ds(pl.multiple_of((me ^ d) * 128, 128), 128)] = slot[...]
    finish(copies)
    for start in range(0, model, 256):
        part[:, start : start + 256] = dot(attended[...], weight[start : start + 256, :], NT).astype(BF)


def outputs(meta, w_out, slots, width, model):
    total = slots[0].shape[0]
    return call(
        with_weights(output_kernel, 1, [w_out]),
        (jax.ShapeDtypeStruct((total, width), BF), jax.ShapeDtypeStruct((total, model), BF)),
        [SM] + [HBM] * w_out.count + [VM] * 4,
        (VM, VM),
        [pltpu.VMEM((model, width), BF), pltpu.SemaphoreType.DMA((PIECES,))],
        2 * total * model * width,
        2 * model * width,
        "outputs",
    )(meta, *w_out.sources, *slots)


def feed_back_kernel(meta, w_down, w_up, g, slope, norms, d_mlp, d_hidden, part, up, down, sems):
    copies = fetch(meta, *w_down, down, sems.at[0])
    later = fetch(meta, *w_up, up, sems.at[1])
    total, model = g.shape
    hidden = up.shape[1]

    @pl.loop(0, total // 64)
    def _(i):
        r = pl.ds(pl.multiple_of(i * 64, 64), 64)
        d_mlp[r, :] = (g[r, :].astype(F32) * norms[5:6, :]).astype(BF)

    finish(copies)
    step = 256
    for start in range(0, hidden, step):
        d_active = dot(d_mlp[...], down[:, start : start + step])
        d_hidden[:, start : start + step] = (d_active * slope[:, start : start + step].astype(F32)).astype(BF)
    finish(later)
    for start in range(0, model, 256):
        part[:, start : start + 256] = dot(d_hidden[...], up[start : start + 256, :], NT).astype(BF)


def feed_back(meta, weights, g, slope, norms):
    total, model = g.shape
    hidden = slope.shape[1]
    sources = sources_of(weights)
    return call(
        with_weights(feed_back_kernel, 1, weights),
        (
            jax.ShapeDtypeStruct((total, model), BF),
            jax.ShapeDtypeStruct((total, hidden), BF),
            jax.ShapeDtypeStruct((total, model), BF),
        ),
        [SM] + [HBM] * len(sources) + [VM] * 3,
        (VM,) * 3,
        [
            pltpu.VMEM((model, hidden), BF),
            pltpu.VMEM((model, hidden), BF),
            pltpu.SemaphoreType.DMA((2, PIECES)),
        ],
        4 * total * model * hidden,
        8 * model * hidden,
        "feed_back",
    )(meta, *sources, g, slope, norms)


def weight_grad_kernel(base, widths, meta, *refs):
    count = len(widths)
    lefts, rights = refs[:count], refs[count : 2 * count]
    model = lefts[0].shape[1]
    if base is None:
        whole = refs[2 * count]
        for b in range(0, model, 256):
            start = 0
            for left, right, width in zip(lefts, rights, widths):
                whole[b : b + 256, start : start + width] = dot(left[:, b : b + 256], right[...], TN).astype(BF)
                start += width
        return
    parts, (staged, sems) = refs[2 * count : 2 * count + 4], refs[2 * count + 4 :]
    quarter, rows = parts[0].shape[0], parts[0].shape[1]
    block = 256
    per = block // rows

    def copy_out(b, act):
        slot = b % 2
        for s in range(per):
            place = meta[base + b * per + s]
            source = staged.at[slot, pl.ds(s * rows, rows), :]
            for part, out in enumerate(parts):

                @pl.when(place // quarter == part)
                def _():
                    getattr(pltpu.make_async_copy(source, out.at[lax.rem(place, quarter)], sems.at[slot, s]), act)()

    for b in range(model // block):
        if b >= 2:
            copy_out(b - 2, "wait")
        start = 0
        for left, right, width in zip(lefts, rights, widths):
            staged[b % 2, :, start : start + width] = dot(
                left[:, b * block : (b + 1) * block], right[...], TN
            ).astype(BF)
            start += width
        copy_out(b, "start")
    for b in range(max(0, model // block - 2), model // block):
        copy_out(b, "wait")


def weight_grad(meta, base, lefts, rights, name):
    widths = [right.shape[1] for right in rights]
    total, model = lefts[0].shape
    rows = model // PIECES
    wide = sum(widths)
    out = jax.ShapeDtypeStruct((PIECES // 4, rows, wide), BF)
    whole = base is None
    return call(
        functools.partial(weight_grad_kernel, base, widths),
        jax.ShapeDtypeStruct((model, wide), BF) if whole else (out,) * 4,
        [SM] + [VM] * (2 * len(widths)),
        VM if whole else (ANY,) * 4,
        [] if whole else [pltpu.VMEM((2, 256, wide), BF), pltpu.SemaphoreType.DMA((2, 256 // rows))],
        2 * total * model * wide,
        2 * model * wide + 2 * total * (model + wide),
        name,
    )(meta, *lefts, *rights)


def norm_back_kernel(frame, count, meta, *refs):
    inner = count > 2
    g, x, one, two, norms = refs[:5]
    if inner:
        pa, pb = refs[5:7]
        ma, mb = refs[7:9] if count > 3 else (None, None)
        out, d_branch, sums, tally = refs[-4:]
        gain = norms[3:4, :]
    else:
        out, sums, tally = refs[-3:]
        gain = norms[0:1, :]
    total, model = x.shape
    core = meta[META_CORE]
    rows = 64
    tally[...] = jnp.zeros_like(tally)

    @pl.loop(0, total // rows)
    def _(i):
        r = pl.ds(pl.multiple_of(i * rows, rows), rows)
        unit, scale = norm_parts(x[r, :].astype(F32))
        d = one[r, :].astype(F32) + two[r, :].astype(F32)
        dg = d * gain
        mean = jnp.mean(dg, axis=-1, keepdims=True)
        slant = jnp.mean(dg * unit, axis=-1, keepdims=True)
        before = g[r, :].astype(F32)
        after = before + scale * (dg - mean - unit * slant)
        out[r, :] = after
        if inner:
            d_branch[r, :] = (after * norms[2:3, :]).astype(BF)

        @pl.when((i // (frame // 2 // rows)) % 2 == core)
        def _():
            def add(k, values):
                tally[k] += jnp.sum(values.reshape(rows // 8, 8, model), axis=0)

            add(0, d * unit)
            add(1, d)
            if inner:
                add(2, after * (pa[r, :].astype(F32) + pb[r, :].astype(F32)))
            if count > 3:
                add(3, before * (ma[r, :].astype(F32) + mb[r, :].astype(F32)))

    sums[...] = jnp.sum(tally[...], axis=1)


def norm_back(meta, g, x, one, two, norms, frame, extra=None):
    total, model = x.shape
    inner = extra is not None
    count = 2 + len(extra) // 2 if inner else 2
    outs = [jax.ShapeDtypeStruct((total, model), F32)]
    if inner:
        outs.append(jax.ShapeDtypeStruct((total, model), BF))
    outs.append(jax.ShapeDtypeStruct((count, model), F32))
    return call(
        functools.partial(norm_back_kernel, frame, count),
        tuple(outs),
        [SM] + [VM] * (5 + len(extra or ())),
        (VM,) * len(outs),
        [pltpu.VMEM((count, 8, model), F32)],
        20 * total * model,
        16 * total * model,
        "norm_back_inner" if inner else "norm_back",
    )(meta, g, x, one, two, norms, *(extra or ()))


def project_back(normed, weight, gains, matrix, take, d_projected, sums):
    width = gains.shape[1]
    total = normed.shape[0]
    rows, lanes = 256, 256
    sums[...] = jnp.zeros_like(sums)
    for part in range(2):
        for start in range(0, width, lanes):
            columns = part * width + start

            @pl.loop(0, total // rows)
            def _(i):
                r = pl.ds(pl.multiple_of(i * rows, rows), rows)
                unit, scale = head_parts(dot(normed[r, :], weight[:, columns : columns + lanes]), matrix)
                d = take(part, r, start, lanes)
                dg = d * gains[part : part + 1, start : start + lanes]
                mean = head_mean(dg, matrix)
                slant = head_mean(dg * unit, matrix)
                d_projected[r, columns : columns + lanes] = (scale * (dg - mean - unit * slant)).astype(BF)
                tally = jnp.sum((d * unit).reshape(rows // 8, 8, lanes), axis=0)
                sums[part * 8 : part * 8 + 8, start : start + lanes] += tally


def frame_back_kernel(frame, head, meta, w_in, w_out, d_branch, normed, qkv, gains, d_projected, part, sums, weight, out, d_att, dq, dk, sems):
    copies = fetch(meta, *w_out, out, sems.at[1])
    later = fetch(meta, *w_in, weight, sems.at[0])
    total, model = normed.shape
    width = gains.shape[1]
    finish(copies)
    for start in range(0, width, 256):
        d_att[:, start : start + 256] = dot(d_branch[...], out[:, start : start + 256]).astype(BF)
    pairs = width // 128

    @pl.loop(0, (total // frame) * pairs)
    def _(i):
        r = pl.ds(pl.multiple_of((i // pairs) * frame, frame), frame)
        column = pl.multiple_of((i % pairs) * 128, 128)
        lanes = pl.ds(column, 128)
        q, k, v = qkv[0, r, lanes], qkv[1, r, lanes], qkv[2, r, lanes]
        d_out = d_att[r, lanes]
        found = []
        for mask in (only_first, only_second):
            weights = jnp.exp(dot(k, mask(q), NT))
            probs = weights * (1.0 / jnp.sum(weights, axis=0, keepdims=True))
            d_probs = dot(v, mask(d_out), NT)
            delta = jnp.sum(probs * d_probs, axis=0, keepdims=True)
            d_scores = (probs * (d_probs - delta)).astype(BF)
            found.append((dot(d_scores, k, TN), dot(d_scores, q), dot(probs.astype(BF), d_out)))
        dq[r, lanes] = pick(found[0][0], found[1][0]) * HEAD_SCALE
        dk[r, lanes] = pick(found[0][1], found[1][1])
        d_projected[r, pl.ds(pl.multiple_of(2 * width + column, 128), 128)] = pick(found[0][2], found[1][2]).astype(BF)

    def take(which, r, start, lanes):
        return (dq, dk)[which][r, start : start + lanes]

    finish(later)
    project_back(normed, weight, gains, head_matrix(256, head), take, d_projected, sums)
    for start in range(0, model, 256):
        part[:, start : start + 256] = dot(d_projected[...], weight[start : start + 256, :], NT).astype(BF)


def frame_back(meta, weights, d_branch, normed, qkv, gains, frame, head):
    total, model = normed.shape
    width = gains.shape[1]
    sources = sources_of(weights)
    return call(
        with_weights(functools.partial(frame_back_kernel, frame, head), 1, weights),
        (
            jax.ShapeDtypeStruct((total, 3 * width), BF),
            jax.ShapeDtypeStruct((total, model), BF),
            jax.ShapeDtypeStruct((16, width), F32),
        ),
        [SM] + [HBM] * len(sources) + [VM] * 4,
        (VM,) * 3,
        [
            pltpu.VMEM((model, 3 * width), BF),
            pltpu.VMEM((model, width), BF),
            pltpu.VMEM((total, width), BF),
            pltpu.VMEM((total, width), F32),
            pltpu.VMEM((total, width), F32),
            pltpu.SemaphoreType.DMA((2, PIECES)),
        ],
        12 * total * model * width,
        8 * model * width,
        "frame_back",
    )(meta, *sources, d_branch, normed, qkv, gains)


def attended_back_kernel(meta, w_out, d_branch, s0, s1, s2, s3, weight, held, sems):
    finish(fetch(meta, *w_out, weight, sems))
    me = meta[META_ME]
    width = weight.shape[1]
    for start in range(0, width, 256):
        held[:, start : start + 256] = dot(d_branch[...], weight[:, start : start + 256]).astype(BF)
    for d, slot in enumerate((s0, s1, s2, s3)):
        slot[...] = held[:, pl.ds(pl.multiple_of((me ^ d) * 128, 128), 128)]


def attended_back(meta, w_out, d_branch, width):
    total, model = d_branch.shape
    return call(
        with_weights(attended_back_kernel, 1, [w_out]),
        (jax.ShapeDtypeStruct((total, 128), BF),) * 4,
        [SM] + [HBM] * w_out.count + [VM],
        (VM,) * 4,
        [
            pltpu.VMEM((model, width), BF),
            pltpu.VMEM((total, width), BF),
            pltpu.SemaphoreType.DMA((PIECES,)),
        ],
        2 * total * model * width,
        2 * model * width,
        "attended_back",
    )(meta, *w_out.sources, d_branch)


def scene_back_kernel(frame, meta, s0, s1, s2, s3, below, above, sums, whole, g0, g1, g2, g3, q0, q1, q2, q3, d_own, d_below, d_above, own, window, d_out, delta, dq, d_window, sems, more):
    copies = load_window(meta, (s0, s1, s2, s3), below, above, own, window, sems)
    me = meta[META_ME]
    for d, slot in enumerate((g0, g1, g2, g3)):
        copies.append(pltpu.make_async_copy(slot, d_out.at[me ^ d], more.at[d]))
        copies[-1].start()
    d_window[...] = jnp.zeros_like(d_window)
    finish(copies)
    total = own.shape[1]
    parts = total // frame

    @pl.loop(0, parts * PLANE)
    def _(i):
        m, j = i // PLANE, i % PLANE
        r = pl.ds(pl.multiple_of(m * frame, frame), frame)
        q, go = own[j, r, :], d_out[j, r, :]
        product = go.astype(F32) * whole[j, r, :]
        inverse = sums[j, r, :]
        heads = []
        for mask, lane in ((only_first, 0), (only_second, 64)):
            heads.append(
                (mask(q), mask(go), inverse[:, lane : lane + 1], jnp.sum(mask(product), axis=-1, keepdims=True))
            )
        dq[...] = jnp.zeros_like(dq)

        @pl.loop(meta[META_SCENES + i * 2], meta[META_SCENES + i * 2 + 1])
        def _(w):
            k, v = window[w, 0, r, :], window[w, 1, r, :]
            found = []
            for head_q, head_go, scale, shift in heads:
                probs = jnp.exp(dot(head_q, k, NT)) * scale
                d_scores = (probs * (dot(head_go, v, NT) - shift)).astype(BF)
                found.append((dot(d_scores, k), dot(d_scores, q, TN), dot(probs.astype(BF), go, TN)))
            dq[...] += pick(found[0][0], found[1][0])
            d_window[w, 0, r, :] += pick(found[0][1], found[1][1])
            d_window[w, 1, r, :] += pick(found[0][2], found[1][2])

        delta[j, r, :] = dq[...] * HEAD_SCALE

    for d, out in enumerate((q0, q1, q2, q3)):
        out[...] = delta[me ^ d].astype(BF)
    for k in range(PLANE):
        d_own[k] = d_window[REACH + k]
    for k in range(REACH):
        d_below[k] = d_window[k].astype(BF)
        d_above[k] = d_window[REACH + PLANE + k].astype(BF)


def scene_back(meta, slots, below, above, sums, found, d_found, frame):
    total = slots[0].shape[1]
    wide = 2 * REACH + PLANE
    out = jax.ShapeDtypeStruct((total, 128), BF)
    edge = jax.ShapeDtypeStruct((REACH, 2, total, 128), BF)
    return call(
        functools.partial(scene_back_kernel, frame),
        (out,) * 4 + (jax.ShapeDtypeStruct((PLANE, 2, total, 128), F32), edge, edge),
        [SM] + [ANY] * 6 + [VM] * 2 + [ANY] * 4,
        (VM,) * 7,
        [
            pltpu.VMEM((PLANE, total, 128), BF),
            pltpu.VMEM((wide, 2, total, 128), BF),
            pltpu.VMEM((PLANE, total, 128), BF),
            pltpu.VMEM((PLANE, total, 128), F32),
            pltpu.VMEM((frame, 128), F32),
            pltpu.VMEM((wide, 2, total, 128), F32),
            pltpu.SemaphoreType.DMA((4, PLANE)),
            pltpu.SemaphoreType.DMA((PLANE,)),
        ],
        10 * PLANE * total * PLANE * frame * 128 * 2,
        8 * wide * total * 128,
        "scene_back",
    )(meta, *slots, below, above, sums, found, *d_found)


def edge_sum_kernel(meta, d_own, from_below, from_above, t0, t1, t2, t3):
    me = meta[META_ME]
    for d, out in enumerate((t0, t1, t2, t3)):
        j = me ^ d
        low = jnp.where(j <= REACH - 1, 1.0, 0.0)
        high = jnp.where(j >= 1, 1.0, 0.0)
        at, top = jnp.minimum(j, REACH - 1), jnp.maximum(j - 1, 0)
        for part in range(2):
            values = d_own[j, part] + low * from_below[at, part].astype(F32)
            out[part] = (values + high * from_above[top, part].astype(F32)).astype(BF)


def edge_sum(meta, d_own, from_below, from_above):
    total = d_own.shape[2]
    out = jax.ShapeDtypeStruct((2, total, 128), BF)
    return call(
        edge_sum_kernel,
        (out,) * 4,
        [SM, VM, VM, VM],
        (VM,) * 4,
        [],
        8 * PLANE * total * 128,
        20 * PLANE * total * 128,
        "edge_sum",
    )(meta, d_own, from_below, from_above)


def queries_back_kernel(head, meta, w_in, q0, q1, q2, q3, t0, t1, t2, t3, normed, gains, d_projected, part, sums, weight, dq, dk, sems):
    copies = fetch(meta, *w_in, weight, sems)
    me = meta[META_ME]
    model = normed.shape[1]
    width = gains.shape[1]
    for d, (query, pair) in enumerate(zip((q0, q1, q2, q3), (t0, t1, t2, t3))):
        column = pl.multiple_of((me ^ d) * 128, 128)
        dq[:, pl.ds(column, 128)] = query[...].astype(F32)
        dk[:, pl.ds(column, 128)] = pair[0].astype(F32)
        d_projected[:, pl.ds(pl.multiple_of(2 * width + column, 128), 128)] = pair[1]
    finish(copies)

    def take(which, r, start, lanes):
        return (dq, dk)[which][r, start : start + lanes]

    project_back(normed, weight, gains, head_matrix(256, head), take, d_projected, sums)
    for start in range(0, model, 256):
        part[:, start : start + 256] = dot(d_projected[...], weight[start : start + 256, :], NT).astype(BF)


def queries_back(meta, w_in, d_queries, d_pairs, normed, gains, head):
    total, model = normed.shape
    width = gains.shape[1]
    return call(
        with_weights(functools.partial(queries_back_kernel, head), 1, [w_in]),
        (
            jax.ShapeDtypeStruct((total, 3 * width), BF),
            jax.ShapeDtypeStruct((total, model), BF),
            jax.ShapeDtypeStruct((16, width), F32),
        ),
        [SM] + [HBM] * w_in.count + [VM] * 10,
        (VM,) * 3,
        [
            pltpu.VMEM((model, 3 * width), BF),
            pltpu.VMEM((total, width), F32),
            pltpu.VMEM((total, width), F32),
            pltpu.SemaphoreType.DMA((PIECES,)),
        ],
        10 * total * model * width,
        8 * model * width,
        "queries_back",
    )(meta, *w_in.sources, *d_queries, *d_pairs, normed, gains)


META_CORE = 5 * PIECES
META_ME = META_CORE + 1
META_SCENES = META_ME + 1


def body(tokens, cotangent, scene_ids, input_weight, output_weight, up_weight, down_weight, norm_params, head_gains):
    portions, _, share, model = tokens.shape
    frame = 2 * share
    total = portions * frame
    head = head_gains.shape[2]
    width = input_weight.shape[3]
    routes = Routes(lax.axis_size("frames"))
    n = routes.n
    index, core = lax.axis_index("frames"), lax.axis_index("mp")
    plain = n != PIECES

    identity = jnp.arange(PIECES, dtype=jnp.int32)
    tables = [identity] * 5 if plain else routes.tables()
    scene_here = scene_ids[:, (index // PLANE) * PLANE + jnp.arange(PLANE)]
    before = jnp.sum(scene_ids[:, None, :] < scene_here[:, :, None], axis=-1)
    until = jnp.sum(scene_ids[:, None, :] <= scene_here[:, :, None], axis=-1)
    spans = jnp.stack([before, until], axis=-1) - (index // PLANE) * PLANE + REACH
    meta = jnp.concatenate(
        [*tables, core[None], (index % PLANE)[None], spans.reshape(-1)]
    ).astype(jnp.int32)

    def all_rows(block):
        own = block[:, 0]
        other = routes.swap(own)
        both = jnp.where(core == 0, jnp.stack([own, other], 1), jnp.stack([other, own], 1))
        return both.reshape(total, model)

    def own_rows(values):
        return lax.dynamic_index_in_dim(values.reshape(portions, 2, share, -1), core, 1, keepdims=True)

    gains = [jnp.tile(head_gains[layer], (1, width // head)) for layer in range(2)]
    clock = Clock(not plain)
    late, close = clock.late, clock.close
    joined = [
        jnp.concatenate([input_weight[layer].reshape(-1, 3 * width), output_weight[layer]], axis=1)
        for layer in range(2)
    ]

    def gather(shard, line_first, name):
        if plain or line_first is None:
            return Whole(lax.all_gather(shard, "frames", axis=0, tiled=True))
        return Gather(routes, clock, shard, line_first, name)

    def scatter(line_last, name, lefts, rights):
        if plain or line_last is None:
            grad = weight_grad(meta, None, lefts, rights, name)
            ready[name] = grad
            summed = lax.psum_scatter(grad.astype(F32) if plain else grad, "frames", scatter_dimension=0, tiled=True)
            return Whole(summed.astype(F32))
        parts = weight_grad(meta, (3 if line_last else 2) * PIECES, lefts, rights, name)
        ready[name] = parts[2]
        return Scatter(routes, clock, parts, line_last, name)

    ready = {}

    ga0 = gather(joined[0], True, "input0")
    gu0 = gather(up_weight[0], True, "up0")
    gd0 = gather(down_weight[0], False, "down0")
    ga1 = gather(joined[1], False, "input1")
    gu1 = gather(up_weight[1], False, "up1")
    gd1 = gather(down_weight[1], False, "down1")
    ga0.ring(3)
    for each in (gd0, ga1, gu1, gd1):
        each.one()
    rows = all_rows(tokens)
    d_result = all_rows(cotangent)
    close(rows, d_result)
    ga0.one()
    ga0.two(0)
    gu0.ring(3)
    close()
    ga0.two(1)
    gd0.ring()
    close()
    in0, out0 = ga0.end(0, 3 * width), ga0.end(3 * width, width)
    gu0.one()
    gd0.ring()
    normed0, qkv0, attended0, a0 = attention_frame(
        meta, [in0, out0], late(rows), norm_params[0], gains[0], frame, head
    )
    close(a0)
    b0 = clock.add(routes.swap(a0))
    gu0.two(0)
    gu0.two(1)
    gd0.ring()
    ga1.ring()
    close()
    up0 = gu0.end()
    gd0.two(0)
    ga1.ring()
    mid0, normed_mid0, active0, slope0 = feed_up(meta, up0, rows, a0, late(b0), norm_params[0])
    close(active0)
    gd0.two(1)
    ga1.ring()
    close()
    down0 = gd0.end()
    ga1.two(0)
    ga1.two(1)
    gu1.ring(2)
    m0 = feed_down(meta, down0, late(active0), model)
    n0 = clock.add(routes.swap(m0))
    close(m0)
    in1, out1 = ga1.end(0, 3 * width), ga1.end(3 * width, width)
    gu1.two(0)
    gu1.ring()
    x1, normed1, *slots = queries(
        meta, in1, mid0, m0, late(n0), norm_params[0], norm_params[1], gains[1], head
    )
    close(slots[0])
    slots = routes.members(late(slots))
    gd1.ring()
    close(*slots[1:])
    rise, fall = edges(meta, late(slots))
    below, above = routes.up(rise), routes.down(fall)
    gu1.two(1)
    close(below, above)
    gd1.ring()
    gd1.two(0)
    *found, sums, whole_found = scene(meta, slots, late(below), above, frame)
    close(found[0])
    home = routes.members(late(found))
    gd1.ring()
    close(*home[1:])
    attended1, a1 = outputs(meta, out1, late(home), width, model)
    b1 = routes.swap(a1)
    close(b1)
    up1 = gu1.end()
    gd1.two(1)
    mid1, normed_mid1, active1, slope1 = feed_up(meta, up1, x1, a1, late(b1), norm_params[1])
    close(active1)

    down1 = gd1.end()
    d_mlp, d_hidden, p = feed_back(meta, [down1, up1], late(d_result), slope1, norm_params[1])
    close(p)
    q = clock.add(routes.swap(p))
    sd1 = scatter(True, "down_grad1", [late(d_mlp)], [active1])
    close(ready["down_grad1"])
    sd1.two(1)
    g, d_branch, inner1 = norm_back(meta, d_result, mid1, p, late(q), norm_params[1], frame, (a1, b1))
    d_home = attended_back(meta, out1, d_branch, width)
    su1 = scatter(True, "up_grad1", [late(normed_mid1)], [d_hidden])
    close(d_home[0], ready["up_grad1"])
    d_found = routes.members(late(d_home))
    close(*d_found[1:])
    sd1.one()
    sd1.two(0)
    *d_queries, d_own, d_below, d_above = scene_back(
        meta, slots, late(below), above, sums, whole_found, d_found, frame
    )
    close(d_own)
    from_above, from_below = routes.down(late(d_below)), routes.up(late(d_above))
    d_queries = routes.members(late(d_queries))
    su1.two(1)
    m1 = feed_down(meta, down1, late(active1), model)
    close(m1, from_above, from_below, *d_queries[1:])
    n1 = clock.add(routes.swap(m1))
    sd1.ring()
    pairs = routes.members(edge_sum(meta, d_own, late(from_below), from_above))
    close(*pairs[1:])
    su1.one()
    sd1.ring()
    d_projected, p, gain1 = queries_back(meta, in1, d_queries, late(pairs), normed1, gains[1], head)
    close(p)
    q = clock.add(routes.swap(p))
    su1.two(0)
    sd1.ring()
    sa1 = scatter(False, "input_grad1", [normed1, d_branch], [late(d_projected), attended1])
    close(ready["input_grad1"])
    sa1.two(0)
    su1.ring()
    own_mlp = own_rows(m1).astype(F32) + own_rows(n1).astype(F32)
    result = own_rows(mid1) + norm_params[1, 5] * own_mlp
    scale1 = jnp.sum(cotangent.astype(F32).reshape(-1, model) * own_mlp.reshape(-1, model), axis=0)
    g, outer1 = norm_back(meta, g, x1, p, late(q), norm_params[1], frame)

    d_mlp, d_hidden, p = feed_back(meta, [down0, up0], g, slope0, norm_params[0])
    close(p)
    q = clock.add(routes.swap(p))
    sa1.two(1)
    sa1.ring()
    su1.ring()
    sd0 = scatter(False, "down_grad0", [late(d_mlp)], [active0])
    if not plain:
        clock.step(ready["down_grad0"])
    sd0.two(0)
    sa1.ring()
    su1.ring()
    su0 = scatter(True, "up_grad0", [late(normed_mid0)], [d_hidden])
    g, d_branch, inner0 = norm_back(meta, g, mid0, p, late(q), norm_params[0], frame, (a0, b0, m0, n0))
    close(d_branch, ready["up_grad0"])
    sd0.two(1)
    su0.two(1)
    sa1.ring()
    sd0.ring()
    d_projected, p, gain0 = frame_back(
        meta, [in0, out0], late(d_branch), normed0, qkv0, gains[0], frame, head
    )
    close(p)
    q = clock.add(routes.swap(late(p)))
    su0.two(0)
    sd0.ring()
    sa1.one()
    sa0 = scatter(False, "input_grad0", [normed0, d_branch], [late(d_projected), attended0])
    if not plain:
        clock.step(ready["input_grad0"])
    su0.one()
    sa0.two(0)
    sd0.ring()
    g, outer0 = norm_back(meta, g, rows, p, late(q), norm_params[0], frame)
    token_grad = own_rows(g)
    close(g)

    norm_rows = [
        jnp.stack([outer[0], outer[1], inner[2], inner[0], inner[1], scale])
        for outer, inner, scale in ((outer0, inner0, inner0[3]), (outer1, inner1, scale1))
    ]
    gain_rows = [
        jnp.sum(gain.reshape(2, 8, width // head, head), axis=(1, 2)).reshape(1, -1)
        for gain in (gain0, gain1)
    ]
    gain_rows = jnp.pad(jnp.concatenate(gain_rows, axis=1), ((0, 0), (0, model - 4 * head)))
    small = jnp.concatenate([*norm_rows, gain_rows])
    small = small + routes.swap(small)
    distances = [2**i for i in range(n.bit_length() - 1)]

    def sum_step(block, distance):
        return block + clock.add(routes.member(late(block), distance))

    small = sum_step(small, distances[0])
    sa0.two(1)
    sa0.ring()
    su0.ring()
    close()
    small = sum_step(small, distances[1])
    sd0.one()
    sa0.ring()
    su0.ring()
    close()
    for distance in distances[2:]:
        small = sum_step(small, distance)
    sa0.ring()
    su0.ring()
    sa0.one()
    norm_grad = small[: 2 * 6].reshape(2, 6, model)
    gain_grad = small[2 * 6, : 4 * head].reshape(2, 2, head)
    return (
        result.astype(BF),
        token_grad,
        jnp.stack([step.run[:, : 3 * width].reshape(-1, 3, width) for step in (sa0, sa1)]),
        jnp.stack([step.run[:, 3 * width :] for step in (sa0, sa1)]),
        jnp.stack([step.run for step in (su0, su1)]),
        jnp.stack([step.run for step in (sd0, sd1)]),
        norm_grad,
        gain_grad,
    )


def solution(mesh):
    rows = P(None, "frames", "mp", None)
    shard = P(None, "frames", "mp")
    wide = P(None, "frames", None, "mp")
    return jax.shard_map(
        body,
        mesh=mesh,
        in_specs=(rows, rows, P(), wide, shard, shard, shard, P(), P()),
        out_specs=(rows, rows, wide, shard, shard, shard, P(), P()),
        check_vma=False,
    )
```

```python
import functools

import jax
import jax.numpy as jnp
import numpy as np
from jax import lax
from jax.experimental import pallas as pl
from jax.experimental.pallas import tpu as pltpu
from jax.sharding import PartitionSpec as P

BF = jnp.bfloat16
F32 = jnp.float32
ROW_EPS = 1e-06
HEAD_EPS = 1e-05
PIECES = 16
SWAPS = 1
COST = 1
PLANE = 4
REACH = 3
AXES = ("frames", "mp")

NN = (((1,), (0,)), ((), ()))
NT = (((1,), (1,)), ((), ()))
TN = (((0,), (0,)), ((), ()))

VM = pl.BlockSpec(memory_space=pltpu.VMEM)
SM = pl.BlockSpec(memory_space=pltpu.SMEM)
ANY = pl.BlockSpec(memory_space=pl.ANY)
HBM = pl.BlockSpec(memory_space=pltpu.HBM)


def dot(left, right, dims=NN):
    return lax.dot_general(left, right, dims, preferred_element_type=F32)


def call(body, outs, in_specs, out_specs, scratch, flops, moved, name):
    return pl.pallas_call(
        body,
        out_shape=outs,
        in_specs=in_specs,
        out_specs=out_specs,
        scratch_shapes=scratch,
        compiler_params=pltpu.CompilerParams(vmem_limit_bytes=(60 if name in ("queries", "queries_back") else 18) * 1024 * 1024),
        cost_estimate=pl.CostEstimate(flops=flops // COST, bytes_accessed=moved // COST, transcendentals=0),
        name=name,
    )


class Routes:
    def __init__(self, n):
        lines = n // PLANE
        self.n, self.lines = n, lines
        order = [0] + list(range(1, lines, 2)) + sorted(range(2, lines, 2), reverse=True)
        following = {z: order[(i + 1) % lines] for i, z in enumerate(order)}
        spot = {z: i for i, z in enumerate(order)}
        self.back = np.array([[order[(spot[z] - k) % lines] for z in range(lines)] for k in range(lines)], np.int32)
        self.steps = np.array([[(spot[z] - spot[w]) % lines for w in range(lines)] for z in range(lines)], np.int32)
        self.ring = [
            (f * 2 + c, (following[f // PLANE] * PLANE + f % PLANE) * 2 + c) for f in range(n) for c in range(2)
        ]
        self.one = [(f * 2 + c, (f ^ (1 + c)) * 2 + c) for f in range(n) for c in range(2)]
        self.two = [(f * 2 + c, (f ^ (2 - c)) * 2 + c) for f in range(n) for c in range(2)]

    def send(self, block, route):
        return lax.ppermute(block, AXES, route)

    def swap(self, block):
        return lax.ppermute(block, "mp", [(0, 1), (1, 0)])

    def swap_parts(self, block):
        if SWAPS == 1:
            return self.swap(block)
        rows = block.shape[0] // SWAPS
        return jnp.concatenate([self.swap(block[i * rows : (i + 1) * rows]) for i in range(SWAPS)])

    def member(self, block, distance):
        return lax.ppermute(block, "frames", [(f, f ^ distance) for f in range(self.n)])

    def members(self, blocks):
        return [blocks[0]] + [self.member(blocks[d], d) for d in range(1, PLANE)]

    def up(self, block):
        return lax.ppermute(block, "frames", [(f, f + PLANE) for f in range(self.n - PLANE)])

    def down(self, block):
        return lax.ppermute(block, "frames", [(f + PLANE, f) for f in range(self.n - PLANE)])

    def tables(self):
        frame, core = lax.axis_index("frames"), lax.axis_index("mp")
        low, high = 1 + core, 2 - core
        bits = jnp.arange(2, dtype=jnp.int32)
        line = PLANE * jnp.asarray(self.back)[:, frame // PLANE]
        straight = PLANE * (frame // PLANE ^ jnp.arange(self.lines, dtype=jnp.int32))
        near = ((frame // low) % 2 ^ bits) * low
        far = ((frame // high) % 2 ^ bits) * high
        middle = line[None, :, None] + near[None, None, :] + far[:, None, None]
        first = line[None, None, :] + near[None, :, None] + far[:, None, None]
        direct = straight[None, None, :] + near[None, :, None] + far[:, None, None]
        every = jnp.arange(self.n, dtype=jnp.int32)
        k = jnp.repeat(jnp.asarray(self.steps)[frame // PLANE], PLANE)
        j = (every // low) % 2 ^ (frame // low) % 2
        h = (every // high) % 2 ^ (frame // high) % 2
        half = self.n // 2
        place_middle = h * half + k * 2 + j
        place_first = h * half + j * self.lines + k
        return [t.reshape(-1).astype(jnp.int32) for t in (middle, first, place_middle, place_first, direct)]


class Clock:
    def __init__(self, active):
        self.active, self.waited, self.pending = active, [], []

    def late(self, value):
        if not (self.active and self.waited):
            return value
        return lax.optimization_barrier((value, self.waited))[0]

    def add(self, value):
        self.pending.append(value)
        return value

    def step(self, *values):
        self.waited = list(values)

    def close(self, *values):
        self.waited, self.pending = self.pending + list(values), []


class Gather:
    def __init__(self, routes, clock, shard, line_first, name):
        self.routes, self.clock, self.line_first, self.name = routes, clock, line_first, name
        self.shard, self.pieces, self.direct = shard, [shard], False

    def send(self, block, route, step):
        with jax.named_scope(self.name + step):
            return self.clock.add(self.routes.send(self.clock.late(block), route))

    def ring(self, steps=1):
        for i in range(steps):
            if i:
                moved = self.routes.send(self.pieces[-1], self.routes.ring)
                self.clock.pending[-1] = moved
            else:
                moved = self.send(self.pieces[-1], self.routes.ring, "_ring")
            self.pieces.append(moved)
        if self.line_first and len(self.pieces) == self.routes.lines:
            self.line = jnp.stack(self.pieces)

    def straight(self):
        self.direct = True
        for k in range(1, self.routes.lines):
            with jax.named_scope(self.name + "_line"):
                self.pieces.append(self.clock.add(self.routes.member(self.clock.late(self.shard), PLANE * k)))
        self.line = jnp.stack(self.pieces)

    def one(self):
        if self.line_first:
            self.got = self.send(self.line, self.routes.one, "_one")
        else:
            self.pieces = [jnp.stack([self.shard, self.send(self.shard, self.routes.one, "_one")])]

    def near(self, half):
        if self.line_first:
            return (self.line, self.got)[half]
        if not hasattr(self, "pairs"):
            self.pairs = {}
        if half not in self.pairs:
            self.pairs[half] = jnp.concatenate(self.pieces[2 * half : 2 * half + 2])
        return self.pairs[half]

    def two(self, half):
        far = self.send(self.near(half), self.routes.two, "_two")
        self.far = (self.far if half else []) + [far]

    def end(self, start=0, width=None):
        sources = [self.near(0), self.near(1), *self.far]
        base = (4 if self.direct else 1) * PIECES if self.line_first else 0
        return Weight(sources, base, start, width)


class Scatter:
    def __init__(self, routes, clock, parts, line_last, name):
        self.routes, self.clock, self.line_last, self.name = routes, clock, line_last, name
        self.keep, self.give = parts[:2], parts[2:]
        self.got, self.at, self.run = [None, None], 0, None

    def send(self, block, route, step):
        with jax.named_scope(self.name + step):
            return self.clock.add(self.routes.send(self.clock.late(block), route))

    def two(self, half):
        self.got[half] = self.send(self.give[half], self.routes.two, "_two")

    def one(self):
        if self.line_last:
            block = self.keep[1].astype(F32) + self.got[1].astype(F32)
            self.more = self.send(block.astype(BF), self.routes.one, "_one")
        else:
            self.run = self.run[0] + self.send(self.run[1].astype(BF), self.routes.one, "_one").astype(F32)

    def local(self, k):
        if self.line_last:
            return self.keep[0][k].astype(F32) + self.got[0][k].astype(F32) + self.more[k].astype(F32)
        half, rows = k // 2, slice(2 * (k % 2), 2 * (k % 2) + 2)
        return self.keep[half][rows].astype(F32) + self.got[half][rows].astype(F32)

    def ring(self):
        if self.run is None:
            self.at, self.run = 1, self.local(1)
        moved = self.send(self.run.astype(BF), self.routes.ring, "_ring")
        self.at = (self.at + 1) % self.routes.lines
        self.run = self.local(self.at) + moved.astype(F32)


class Weight:
    def __init__(self, sources, base, start=0, width=None):
        self.sources, self.count = tuple(sources), len(sources)
        self.width = width or self.sources[0].shape[-1]
        self.plan = (base, start, self.width)


class Whole:
    def __init__(self, value):
        self.run = value

    def ring(self, steps=1):
        pass

    def one(self):
        pass

    def straight(self):
        pass

    def two(self, half):
        pass

    def end(self, start=0, width=None):
        return Weight([self.run], None, start, width)


def with_weights(kernel, before, weights):
    def run(*refs):
        at = before
        given = []
        for weight in weights:
            given.append((weight.plan, refs[at : at + weight.count]))
            at += weight.count
        return kernel(*refs[:before], *given, *refs[at:])

    return run


def sources_of(weights):
    return [source for weight in weights for source in weight.sources]


def fetch(meta, plan, sources, into, sems):
    base, start, width = plan
    columns = pl.ds(start, width)
    copies = []
    if base is None:
        rows = into.shape[0] // 4
        for q in range(4):
            part = pl.ds(q * rows, rows)
            copies.append(pltpu.make_async_copy(sources[0].at[part, columns], into.at[part, :], sems.at[q]))
    else:
        rows, quarter = into.shape[0] // PIECES, PIECES // 4
        for q in range(PIECES):
            source = sources[q // quarter].at[q % quarter, :, columns]
            row = pl.multiple_of(meta[base + q] * rows, rows)
            copies.append(pltpu.make_async_copy(source, into.at[pl.ds(row, rows), :], sems.at[q]))
    for copy in copies:
        copy.start()
    return copies


def finish(copies):
    for copy in copies:
        copy.wait()


def norm_parts(values):
    centred = values - jnp.mean(values, axis=-1, keepdims=True)
    scale = lax.rsqrt(jnp.mean(centred * centred, axis=-1, keepdims=True) + ROW_EPS)
    return centred * scale, scale


def head_matrix(width, head):
    row = lax.broadcasted_iota(jnp.int32, (width, width), 0) // head
    column = lax.broadcasted_iota(jnp.int32, (width, width), 1) // head
    return jnp.where(row == column, 1.0 / head, 0.0).astype(BF)


def head_mean(values, matrix):
    high = values.astype(BF)
    low = (values - high.astype(F32)).astype(BF)
    return dot(high, matrix) + dot(low, matrix)


def head_parts(values, matrix):
    centred = values - head_mean(values, matrix)
    scale = lax.rsqrt(head_mean(centred * centred, matrix) + HEAD_EPS)
    return centred * scale, scale


def project(normed, weight, gains, matrix, put, rows=256, lanes=256):
    width = gains.shape[1]
    total = normed.shape[0]
    factor = HEAD_SCALE

    for part in range(3):
        for start in range(0, width, lanes):
            columns = part * width + start

            @pl.loop(0, total // rows)
            def _(i):
                r = pl.ds(pl.multiple_of(i * rows, rows), rows)
                values = dot(normed[r, :], weight[:, columns : columns + lanes])
                if part < 2:
                    unit, _ = head_parts(values, matrix)
                    values = unit * gains[part : part + 1, start : start + lanes]
                values = values.astype(BF)
                if part == 0:
                    values = (values.astype(F32) * factor).astype(BF)
                put(part, r, start, lanes, values)


HEAD_SCALE = 0.125


def only_first(values):
    lane = lax.broadcasted_iota(jnp.int32, values.shape, 1)
    return jnp.where(lane < values.shape[1] // 2, values, jnp.zeros_like(values))


def only_second(values):
    lane = lax.broadcasted_iota(jnp.int32, values.shape, 1)
    return jnp.where(lane < values.shape[1] // 2, jnp.zeros_like(values), values)


def pick(first, second):
    lane = lax.broadcasted_iota(jnp.int32, first.shape, 1)
    return jnp.where(lane < first.shape[1] // 2, first, second)


def gelu_parts(v):
    size = jnp.abs(v)
    bell = jnp.exp(v * v * -0.5)
    t = 1.0 / (1.0 + size * 0.23164189)
    tail = t * (0.127414796 + t * (-0.142248368 + t * (0.7107068705 + t * (-0.7265760135 + t * 0.5307027145))))
    tail = tail * bell
    phi = jnp.where(v >= 0.0, 1.0 - tail, tail)
    return v * phi, phi + v * bell * 0.3989422804014327


def attention_frame_kernel(frame, head, meta, w_in, w_out, rows_ref, norms, gains, normed, qkv, attended, part, weight, out, sems):
    copies = fetch(meta, *w_in, weight, sems.at[0])
    later = fetch(meta, *w_out, out, sems.at[1])
    total, model = rows_ref.shape
    width = gains.shape[1]

    @pl.loop(0, total // 64)
    def _(i):
        r = pl.ds(pl.multiple_of(i * 64, 64), 64)
        unit, _ = norm_parts(rows_ref[r, :].astype(F32))
        normed[r, :] = (unit * norms[0:1, :] + norms[1:2, :]).astype(BF)

    finish(copies)
    matrix = head_matrix(256, head)

    def put(part, r, start, lanes, values):
        qkv[part, r, start : start + lanes] = values

    project(normed, weight, gains, matrix, put)
    pairs = width // 128

    @pl.loop(0, (total // frame) * pairs)
    def _(i):
        r = pl.ds(pl.multiple_of((i // pairs) * frame, frame), frame)
        lanes = pl.ds(pl.multiple_of((i % pairs) * 128, 128), 128)
        q, k, v = qkv[0, r, lanes], qkv[1, r, lanes], qkv[2, r, lanes]
        found = []
        for mask in (only_first, only_second):
            weights = jnp.exp(dot(mask(q), k, NT))
            found.append(dot(weights.astype(BF), v) / jnp.sum(weights, axis=-1, keepdims=True))
        attended[r, lanes] = pick(found[0], found[1]).astype(BF)

    finish(later)
    for start in range(0, model, 256):
        part[:, start : start + 256] = dot(attended[...], out[start : start + 256, :], NT).astype(BF)


def attention_frame(meta, weights, rows, norms, gains, frame, head):
    total, model = rows.shape
    width = gains.shape[1]
    sources = sources_of(weights)
    return call(
        with_weights(functools.partial(attention_frame_kernel, frame, head), 1, weights),
        (
            jax.ShapeDtypeStruct((total, model), BF),
            jax.ShapeDtypeStruct((3, total, width), BF),
            jax.ShapeDtypeStruct((total, width), BF),
            jax.ShapeDtypeStruct((total, model), BF),
        ),
        [SM] + [HBM] * len(sources) + [VM, VM, VM],
        (VM, VM, VM, VM),
        [
            pltpu.VMEM((model, 3 * width), BF),
            pltpu.VMEM((model, width), BF),
            pltpu.SemaphoreType.DMA((2, PIECES)),
        ],
        8 * total * model * width,
        2 * 4 * model * width,
        "attention_frame",
    )(meta, *sources, rows, norms, gains)


def feed_up_kernel(meta, w_up, x, one, two, norms, mid, normed, active, slope, up, sems):
    copies = fetch(meta, *w_up, up, sems)
    total, model = x.shape
    hidden = up.shape[1]

    @pl.loop(0, total // 64)
    def _(i):
        r = pl.ds(pl.multiple_of(i * 64, 64), 64)
        branch = one[r, :].astype(F32) + two[r, :].astype(F32)
        values = x[r, :].astype(F32) + norms[2:3, :] * branch
        mid[r, :] = values
        unit, _ = norm_parts(values)
        normed[r, :] = (unit * norms[3:4, :] + norms[4:5, :]).astype(BF)

    finish(copies)
    step, rows = 512, 256
    for start in range(0, hidden, step):

        @pl.loop(0, total // rows)
        def _(i):
            r = pl.ds(pl.multiple_of(i * rows, rows), rows)
            before = dot(normed[r, :], up[:, start : start + step])
            after_, rise = gelu_parts(before)
            active[r, start : start + step] = after_.astype(BF)
            slope[r, start : start + step] = rise.astype(BF)


def feed_up(meta, up, x, one, two, norms):
    total, model = x.shape
    hidden = up.width
    return call(
        with_weights(feed_up_kernel, 1, [up]),
        (
            jax.ShapeDtypeStruct((total, model), F32),
            jax.ShapeDtypeStruct((total, model), BF),
            jax.ShapeDtypeStruct((total, hidden), BF),
            jax.ShapeDtypeStruct((total, hidden), BF),
        ),
        [SM] + [HBM] * up.count + [VM] * 4,
        (VM,) * 4,
        [pltpu.VMEM((model, hidden), BF), pltpu.SemaphoreType.DMA((PIECES,))],
        2 * total * model * hidden,
        2 * model * hidden,
        "feed_up",
    )(meta, *up.sources, x, one, two, norms)


def feed_down_kernel(meta, w_down, active, part, down, sems):
    model = part.shape[1]
    finish(fetch(meta, *w_down, down, sems))
    for start in range(0, model, 256):
        part[:, start : start + 256] = dot(active[...], down[start : start + 256, :], NT).astype(BF)


def feed_down(meta, down, active, model):
    total, hidden = active.shape
    return call(
        with_weights(feed_down_kernel, 1, [down]),
        jax.ShapeDtypeStruct((total, model), BF),
        [SM] + [HBM] * down.count + [VM],
        VM,
        [pltpu.VMEM((model, hidden), BF), pltpu.SemaphoreType.DMA((PIECES,))],
        2 * total * model * hidden,
        2 * model * hidden,
        "feed_down",
    )(meta, *down.sources, active)


def queries_kernel(head, meta, w_in, mid, one, two, before, norms, gains, x, normed, s0, s1, s2, s3, weight, held, sems):
    copies = fetch(meta, *w_in, weight, sems)
    total, model = mid.shape
    width = gains.shape[1]
    me = meta[META_ME]

    @pl.loop(0, total // 64)
    def _(i):
        r = pl.ds(pl.multiple_of(i * 64, 64), 64)
        values = mid[r, :] + before[5:6, :] * (one[r, :].astype(F32) + two[r, :].astype(F32))
        x[r, :] = values
        unit, _ = norm_parts(values)
        normed[r, :] = (unit * norms[0:1, :] + norms[1:2, :]).astype(BF)

    finish(copies)

    def put(part, r, start, lanes, values):
        held[part, r, start : start + lanes] = values

    project(normed, weight, gains, head_matrix(256, head), put)
    for d, slot in enumerate((s0, s1, s2, s3)):
        lanes = pl.ds(pl.multiple_of((me ^ d) * 128, 128), 128)
        for part in range(3):
            slot[part] = held[part, :, lanes]


def queries(meta, w_in, mid, one, two, before, norms, gains, head):
    total, model = mid.shape
    width = gains.shape[1]
    slot = jax.ShapeDtypeStruct((3, total, 128), BF)
    return call(
        with_weights(functools.partial(queries_kernel, head), 1, [w_in]),
        (jax.ShapeDtypeStruct((total, model), F32), jax.ShapeDtypeStruct((total, model), BF)) + (slot,) * 4,
        [SM] + [HBM] * w_in.count + [VM] * 6,
        (VM,) * 6,
        [
            pltpu.VMEM((model, 3 * width), BF),
            pltpu.VMEM((3, total, width), BF),
            pltpu.SemaphoreType.DMA((PIECES,)),
        ],
        6 * total * model * width,
        8 * model * width,
        "queries",
    )(meta, *w_in.sources, mid, one, two, before, norms, gains)


def edge_kernel(meta, s0, s1, s2, s3, rise, fall):
    me = meta[META_ME]
    for d, slot in enumerate((s0, s1, s2, s3)):
        j = me ^ d

        @pl.when(j >= 1)
        def _():
            rise[jnp.maximum(j - 1, 0)] = slot[1:3]

        @pl.when(j <= REACH - 1)
        def _():
            fall[jnp.minimum(j, REACH - 1)] = slot[1:3]


def edges(meta, slots):
    total = slots[0].shape[1]
    out = jax.ShapeDtypeStruct((REACH, 2, total, 128), BF)
    return call(edge_kernel, (out, out), [SM] + [VM] * 4, (VM, VM), [], 0, 4 * REACH * 2 * total * 128 * 2, "edges")(
        meta, *slots
    )


def load_window(meta, slots, below, above, own, window, sems):
    me = meta[META_ME]
    copies = []
    for d, slot in enumerate(slots):
        j = me ^ d
        copies.append(pltpu.make_async_copy(slot.at[0], own.at[j], sems.at[0, d]))
        copies.append(pltpu.make_async_copy(slot.at[pl.ds(1, 2)], window.at[REACH + j], sems.at[1, d]))
    for k in range(REACH):
        copies.append(pltpu.make_async_copy(below.at[k], window.at[k], sems.at[2, k]))
        copies.append(pltpu.make_async_copy(above.at[k], window.at[REACH + PLANE + k], sems.at[3, k]))
    for copy in copies:
        copy.start()
    return copies


def scene_kernel(frame, meta, s0, s1, s2, s3, below, above, o0, o1, o2, o3, sums, found, own, window, held, sems):
    finish(load_window(meta, (s0, s1, s2, s3), below, above, own, window, sems))
    me = meta[META_ME]
    total = own.shape[1]
    parts = total // frame

    @pl.loop(0, parts * PLANE)
    def _(i):
        m, j = i // PLANE, i % PLANE
        r = pl.ds(pl.multiple_of(m * frame, frame), frame)
        q = own[j, r, :]
        first, second = only_first(q), only_second(q)
        held[...] = jnp.zeros_like(held)

        @pl.loop(meta[META_SCENES + i * 2], meta[META_SCENES + i * 2 + 1])
        def _(w):
            k, v = window[w, 0, r, :], window[w, 1, r, :]
            one = jnp.exp(dot(first, k, NT))
            two = jnp.exp(dot(second, k, NT))
            held[0] += pick(dot(one.astype(BF), v), dot(two.astype(BF), v))
            for h, weights in ((1, one), (2, two)):
                tally = weights[:, 0:128]
                for start in range(128, frame, 128):
                    tally = tally + weights[:, start : start + 128]
                held[h] += tally

        lane = pick(
            jnp.broadcast_to(jnp.sum(held[1], axis=-1, keepdims=True), (frame, 128)),
            jnp.broadcast_to(jnp.sum(held[2], axis=-1, keepdims=True), (frame, 128)),
        )
        inverse = 1.0 / lane
        sums[j, r, :] = inverse
        found[j, r, :] = held[0] * inverse

    for d, out in enumerate((o0, o1, o2, o3)):
        out[...] = found[me ^ d].astype(BF)


def scene(meta, slots, below, above, frame):
    total = slots[0].shape[1]
    out = jax.ShapeDtypeStruct((total, 128), BF)
    wide = 2 * REACH + PLANE
    return call(
        functools.partial(scene_kernel, frame),
        (out,) * 4 + (jax.ShapeDtypeStruct((PLANE, total, 128), F32),) * 2,
        [SM] + [ANY] * 6,
        (VM,) * 6,
        [
            pltpu.VMEM((PLANE, total, 128), BF),
            pltpu.VMEM((wide, 2, total, 128), BF),
            pltpu.VMEM((3, frame, 128), F32),
            pltpu.SemaphoreType.DMA((4, PLANE)),
        ],
        4 * PLANE * total * PLANE * frame * 128 * 2,
        4 * wide * total * 128,
        "scene",
    )(meta, *slots, below, above)


def output_kernel(meta, w_out, o0, o1, o2, o3, attended, part, weight, sems):
    copies = fetch(meta, *w_out, weight, sems)
    me = meta[META_ME]
    model = part.shape[1]
    for d, slot in enumerate((o0, o1, o2, o3)):
        attended[:, pl.ds(pl.multiple_of((me ^ d) * 128, 128), 128)] = slot[...]
    finish(copies)
    for start in range(0, model, 256):
        part[:, start : start + 256] = dot(attended[...], weight[start : start + 256, :], NT).astype(BF)


def outputs(meta, w_out, slots, width, model):
    total = slots[0].shape[0]
    return call(
        with_weights(output_kernel, 1, [w_out]),
        (jax.ShapeDtypeStruct((total, width), BF), jax.ShapeDtypeStruct((total, model), BF)),
        [SM] + [HBM] * w_out.count + [VM] * 4,
        (VM, VM),
        [pltpu.VMEM((model, width), BF), pltpu.SemaphoreType.DMA((PIECES,))],
        2 * total * model * width,
        2 * model * width,
        "outputs",
    )(meta, *w_out.sources, *slots)


def feed_back_kernel(meta, w_down, w_up, g, slope, norms, d_mlp, d_hidden, part, up, down, sems):
    copies = fetch(meta, *w_down, down, sems.at[0])
    later = fetch(meta, *w_up, up, sems.at[1])
    total, model = g.shape
    hidden = up.shape[1]

    @pl.loop(0, total // 64)
    def _(i):
        r = pl.ds(pl.multiple_of(i * 64, 64), 64)
        d_mlp[r, :] = (g[r, :].astype(F32) * norms[5:6, :]).astype(BF)

    finish(copies)
    step = 256
    for start in range(0, hidden, step):
        d_active = dot(d_mlp[...], down[:, start : start + step])
        d_hidden[:, start : start + step] = (d_active * slope[:, start : start + step].astype(F32)).astype(BF)
    finish(later)
    for start in range(0, model, 256):
        part[:, start : start + 256] = dot(d_hidden[...], up[start : start + 256, :], NT).astype(BF)


def feed_back(meta, weights, g, slope, norms):
    total, model = g.shape
    hidden = slope.shape[1]
    sources = sources_of(weights)
    return call(
        with_weights(feed_back_kernel, 1, weights),
        (
            jax.ShapeDtypeStruct((total, model), BF),
            jax.ShapeDtypeStruct((total, hidden), BF),
            jax.ShapeDtypeStruct((total, model), BF),
        ),
        [SM] + [HBM] * len(sources) + [VM] * 3,
        (VM,) * 3,
        [
            pltpu.VMEM((model, hidden), BF),
            pltpu.VMEM((model, hidden), BF),
            pltpu.SemaphoreType.DMA((2, PIECES)),
        ],
        4 * total * model * hidden,
        8 * model * hidden,
        "feed_back",
    )(meta, *sources, g, slope, norms)


def weight_grad_kernel(base, widths, meta, *refs):
    count = len(widths)
    lefts, rights = refs[:count], refs[count : 2 * count]
    model = lefts[0].shape[1]
    if base is None:
        whole = refs[2 * count]
        for b in range(0, model, 256):
            start = 0
            for left, right, width in zip(lefts, rights, widths):
                whole[b : b + 256, start : start + width] = dot(left[:, b : b + 256], right[...], TN).astype(BF)
                start += width
        return
    parts, (staged, sems) = refs[2 * count : 2 * count + 4], refs[2 * count + 4 :]
    quarter, rows = parts[0].shape[0], parts[0].shape[1]
    block = 256
    per = block // rows

    def copy_out(b, act):
        slot = b % 2
        for s in range(per):
            place = meta[base + b * per + s]
            source = staged.at[slot, pl.ds(s * rows, rows), :]
            for part, out in enumerate(parts):

                @pl.when(place // quarter == part)
                def _():
                    getattr(pltpu.make_async_copy(source, out.at[lax.rem(place, quarter)], sems.at[slot, s]), act)()

    for b in range(model // block):
        if b >= 2:
            copy_out(b - 2, "wait")
        start = 0
        for left, right, width in zip(lefts, rights, widths):
            staged[b % 2, :, start : start + width] = dot(
                left[:, b * block : (b + 1) * block], right[...], TN
            ).astype(BF)
            start += width
        copy_out(b, "start")
    for b in range(max(0, model // block - 2), model // block):
        copy_out(b, "wait")


def weight_grad(meta, base, lefts, rights, name):
    widths = [right.shape[1] for right in rights]
    total, model = lefts[0].shape
    rows = model // PIECES
    wide = sum(widths)
    out = jax.ShapeDtypeStruct((PIECES // 4, rows, wide), BF)
    whole = base is None
    return call(
        functools.partial(weight_grad_kernel, base, widths),
        jax.ShapeDtypeStruct((model, wide), BF) if whole else (out,) * 4,
        [SM] + [VM] * (2 * len(widths)),
        VM if whole else (ANY,) * 4,
        [] if whole else [pltpu.VMEM((2, 256, wide), BF), pltpu.SemaphoreType.DMA((2, 256 // rows))],
        2 * total * model * wide,
        2 * model * wide + 2 * total * (model + wide),
        name,
    )(meta, *lefts, *rights)


def norm_back_kernel(frame, count, meta, *refs):
    inner = count > 2
    g, x, one, two, norms = refs[:5]
    if inner:
        pa, pb = refs[5:7]
        ma, mb = refs[7:9] if count > 3 else (None, None)
        out, d_branch, sums, tally = refs[-4:]
        gain = norms[3:4, :]
    else:
        out, sums, tally = refs[-3:]
        gain = norms[0:1, :]
    total, model = x.shape
    core = meta[META_CORE]
    rows = 64
    tally[...] = jnp.zeros_like(tally)

    @pl.loop(0, total // rows)
    def _(i):
        r = pl.ds(pl.multiple_of(i * rows, rows), rows)
        unit, scale = norm_parts(x[r, :].astype(F32))
        d = one[r, :].astype(F32) + two[r, :].astype(F32)
        dg = d * gain
        mean = jnp.mean(dg, axis=-1, keepdims=True)
        slant = jnp.mean(dg * unit, axis=-1, keepdims=True)
        before = g[r, :].astype(F32)
        after = before + scale * (dg - mean - unit * slant)
        out[r, :] = after
        if inner:
            d_branch[r, :] = (after * norms[2:3, :]).astype(BF)

        @pl.when((i // (frame // 2 // rows)) % 2 == core)
        def _():
            def add(k, values):
                tally[k] += jnp.sum(values.reshape(rows // 8, 8, model), axis=0)

            add(0, d * unit)
            add(1, d)
            if inner:
                add(2, after * (pa[r, :].astype(F32) + pb[r, :].astype(F32)))
            if count > 3:
                add(3, before * (ma[r, :].astype(F32) + mb[r, :].astype(F32)))

    sums[...] = jnp.sum(tally[...], axis=1)


def norm_back(meta, g, x, one, two, norms, frame, extra=None):
    total, model = x.shape
    inner = extra is not None
    count = 2 + len(extra) // 2 if inner else 2
    outs = [jax.ShapeDtypeStruct((total, model), F32)]
    if inner:
        outs.append(jax.ShapeDtypeStruct((total, model), BF))
    outs.append(jax.ShapeDtypeStruct((count, model), F32))
    return call(
        functools.partial(norm_back_kernel, frame, count),
        tuple(outs),
        [SM] + [VM] * (5 + len(extra or ())),
        (VM,) * len(outs),
        [pltpu.VMEM((count, 8, model), F32)],
        20 * total * model,
        16 * total * model,
        "norm_back_inner" if inner else "norm_back",
    )(meta, g, x, one, two, norms, *(extra or ()))


def project_back(normed, weight, gains, matrix, take, d_projected, sums):
    width = gains.shape[1]
    total = normed.shape[0]
    rows, lanes = 256, 256
    sums[...] = jnp.zeros_like(sums)
    for part in range(2):
        for start in range(0, width, lanes):
            columns = part * width + start

            @pl.loop(0, total // rows)
            def _(i):
                r = pl.ds(pl.multiple_of(i * rows, rows), rows)
                unit, scale = head_parts(dot(normed[r, :], weight[:, columns : columns + lanes]), matrix)
                d = take(part, r, start, lanes)
                dg = d * gains[part : part + 1, start : start + lanes]
                mean = head_mean(dg, matrix)
                slant = head_mean(dg * unit, matrix)
                d_projected[r, columns : columns + lanes] = (scale * (dg - mean - unit * slant)).astype(BF)
                tally = jnp.sum((d * unit).reshape(rows // 8, 8, lanes), axis=0)
                sums[part * 8 : part * 8 + 8, start : start + lanes] += tally


def frame_back_kernel(frame, head, meta, w_in, w_out, d_branch, normed, qkv, gains, d_projected, part, sums, weight, out, d_att, dq, dk, sems):
    copies = fetch(meta, *w_out, out, sems.at[1])
    later = fetch(meta, *w_in, weight, sems.at[0])
    total, model = normed.shape
    width = gains.shape[1]
    finish(copies)
    for start in range(0, width, 256):
        d_att[:, start : start + 256] = dot(d_branch[...], out[:, start : start + 256]).astype(BF)
    pairs = width // 128

    @pl.loop(0, (total // frame) * pairs)
    def _(i):
        r = pl.ds(pl.multiple_of((i // pairs) * frame, frame), frame)
        column = pl.multiple_of((i % pairs) * 128, 128)
        lanes = pl.ds(column, 128)
        q, k, v = qkv[0, r, lanes], qkv[1, r, lanes], qkv[2, r, lanes]
        d_out = d_att[r, lanes]
        found = []
        for mask in (only_first, only_second):
            weights = jnp.exp(dot(k, mask(q), NT))
            probs = weights * (1.0 / jnp.sum(weights, axis=0, keepdims=True))
            d_probs = dot(v, mask(d_out), NT)
            delta = jnp.sum(probs * d_probs, axis=0, keepdims=True)
            d_scores = (probs * (d_probs - delta)).astype(BF)
            found.append((dot(d_scores, k, TN), dot(d_scores, q), dot(probs.astype(BF), d_out)))
        dq[r, lanes] = pick(found[0][0], found[1][0]) * HEAD_SCALE
        dk[r, lanes] = pick(found[0][1], found[1][1])
        d_projected[r, pl.ds(pl.multiple_of(2 * width + column, 128), 128)] = pick(found[0][2], found[1][2]).astype(BF)

    def take(which, r, start, lanes):
        return (dq, dk)[which][r, start : start + lanes]

    finish(later)
    project_back(normed, weight, gains, head_matrix(256, head), take, d_projected, sums)
    for start in range(0, model, 256):
        part[:, start : start + 256] = dot(d_projected[...], weight[start : start + 256, :], NT).astype(BF)


def frame_back(meta, weights, d_branch, normed, qkv, gains, frame, head):
    total, model = normed.shape
    width = gains.shape[1]
    sources = sources_of(weights)
    return call(
        with_weights(functools.partial(frame_back_kernel, frame, head), 1, weights),
        (
            jax.ShapeDtypeStruct((total, 3 * width), BF),
            jax.ShapeDtypeStruct((total, model), BF),
            jax.ShapeDtypeStruct((16, width), F32),
        ),
        [SM] + [HBM] * len(sources) + [VM] * 4,
        (VM,) * 3,
        [
            pltpu.VMEM((model, 3 * width), BF),
            pltpu.VMEM((model, width), BF),
            pltpu.VMEM((total, width), BF),
            pltpu.VMEM((total, width), F32),
            pltpu.VMEM((total, width), F32),
            pltpu.SemaphoreType.DMA((2, PIECES)),
        ],
        12 * total * model * width,
        8 * model * width,
        "frame_back",
    )(meta, *sources, d_branch, normed, qkv, gains)


def attended_back_kernel(meta, w_out, d_branch, s0, s1, s2, s3, weight, held, sems):
    finish(fetch(meta, *w_out, weight, sems))
    me = meta[META_ME]
    width = weight.shape[1]
    for start in range(0, width, 256):
        held[:, start : start + 256] = dot(d_branch[...], weight[:, start : start + 256]).astype(BF)
    for d, slot in enumerate((s0, s1, s2, s3)):
        slot[...] = held[:, pl.ds(pl.multiple_of((me ^ d) * 128, 128), 128)]


def attended_back(meta, w_out, d_branch, width):
    total, model = d_branch.shape
    return call(
        with_weights(attended_back_kernel, 1, [w_out]),
        (jax.ShapeDtypeStruct((total, 128), BF),) * 4,
        [SM] + [HBM] * w_out.count + [VM],
        (VM,) * 4,
        [
            pltpu.VMEM((model, width), BF),
            pltpu.VMEM((total, width), BF),
            pltpu.SemaphoreType.DMA((PIECES,)),
        ],
        2 * total * model * width,
        2 * model * width,
        "attended_back",
    )(meta, *w_out.sources, d_branch)


def scene_back_kernel(frame, meta, s0, s1, s2, s3, below, above, sums, whole, g0, g1, g2, g3, q0, q1, q2, q3, d_own, d_below, d_above, own, window, d_out, delta, dq, d_window, sems, more):
    copies = load_window(meta, (s0, s1, s2, s3), below, above, own, window, sems)
    me = meta[META_ME]
    for d, slot in enumerate((g0, g1, g2, g3)):
        copies.append(pltpu.make_async_copy(slot, d_out.at[me ^ d], more.at[d]))
        copies[-1].start()
    d_window[...] = jnp.zeros_like(d_window)
    finish(copies)
    total = own.shape[1]
    parts = total // frame

    @pl.loop(0, parts * PLANE)
    def _(i):
        m, j = i // PLANE, i % PLANE
        r = pl.ds(pl.multiple_of(m * frame, frame), frame)
        q, go = own[j, r, :], d_out[j, r, :]
        product = go.astype(F32) * whole[j, r, :]
        inverse = sums[j, r, :]
        heads = []
        for mask, lane in ((only_first, 0), (only_second, 64)):
            heads.append(
                (mask(q), mask(go), inverse[:, lane : lane + 1], jnp.sum(mask(product), axis=-1, keepdims=True))
            )
        dq[...] = jnp.zeros_like(dq)

        @pl.loop(meta[META_SCENES + i * 2], meta[META_SCENES + i * 2 + 1])
        def _(w):
            k, v = window[w, 0, r, :], window[w, 1, r, :]
            found = []
            for head_q, head_go, scale, shift in heads:
                probs = jnp.exp(dot(head_q, k, NT)) * scale
                d_scores = (probs * (dot(head_go, v, NT) - shift)).astype(BF)
                found.append((dot(d_scores, k), dot(d_scores, q, TN), dot(probs.astype(BF), go, TN)))
            dq[...] += pick(found[0][0], found[1][0])
            d_window[w, 0, r, :] += pick(found[0][1], found[1][1])
            d_window[w, 1, r, :] += pick(found[0][2], found[1][2])

        delta[j, r, :] = dq[...] * HEAD_SCALE

    for d, out in enumerate((q0, q1, q2, q3)):
        out[...] = delta[me ^ d].astype(BF)
    for k in range(PLANE):
        d_own[k] = d_window[REACH + k]
    for k in range(REACH):
        d_below[k] = d_window[k].astype(BF)
        d_above[k] = d_window[REACH + PLANE + k].astype(BF)


def scene_back(meta, slots, below, above, sums, found, d_found, frame):
    total = slots[0].shape[1]
    wide = 2 * REACH + PLANE
    out = jax.ShapeDtypeStruct((total, 128), BF)
    edge = jax.ShapeDtypeStruct((REACH, 2, total, 128), BF)
    return call(
        functools.partial(scene_back_kernel, frame),
        (out,) * 4 + (jax.ShapeDtypeStruct((PLANE, 2, total, 128), F32), edge, edge),
        [SM] + [ANY] * 6 + [VM] * 2 + [ANY] * 4,
        (VM,) * 7,
        [
            pltpu.VMEM((PLANE, total, 128), BF),
            pltpu.VMEM((wide, 2, total, 128), BF),
            pltpu.VMEM((PLANE, total, 128), BF),
            pltpu.VMEM((PLANE, total, 128), F32),
            pltpu.VMEM((frame, 128), F32),
            pltpu.VMEM((wide, 2, total, 128), F32),
            pltpu.SemaphoreType.DMA((4, PLANE)),
            pltpu.SemaphoreType.DMA((PLANE,)),
        ],
        10 * PLANE * total * PLANE * frame * 128 * 2,
        8 * wide * total * 128,
        "scene_back",
    )(meta, *slots, below, above, sums, found, *d_found)


def edge_sum_kernel(meta, d_own, from_below, from_above, t0, t1, t2, t3):
    me = meta[META_ME]
    for d, out in enumerate((t0, t1, t2, t3)):
        j = me ^ d
        low = jnp.where(j <= REACH - 1, 1.0, 0.0)
        high = jnp.where(j >= 1, 1.0, 0.0)
        at, top = jnp.minimum(j, REACH - 1), jnp.maximum(j - 1, 0)
        for part in range(2):
            values = d_own[j, part] + low * from_below[at, part].astype(F32)
            out[part] = (values + high * from_above[top, part].astype(F32)).astype(BF)


def edge_sum(meta, d_own, from_below, from_above):
    total = d_own.shape[2]
    out = jax.ShapeDtypeStruct((2, total, 128), BF)
    return call(
        edge_sum_kernel,
        (out,) * 4,
        [SM, VM, VM, VM],
        (VM,) * 4,
        [],
        8 * PLANE * total * 128,
        20 * PLANE * total * 128,
        "edge_sum",
    )(meta, d_own, from_below, from_above)


def queries_back_kernel(head, meta, w_in, q0, q1, q2, q3, t0, t1, t2, t3, normed, gains, d_projected, part, sums, weight, dq, dk, sems):
    copies = fetch(meta, *w_in, weight, sems)
    me = meta[META_ME]
    model = normed.shape[1]
    width = gains.shape[1]
    for d, (query, pair) in enumerate(zip((q0, q1, q2, q3), (t0, t1, t2, t3))):
        column = pl.multiple_of((me ^ d) * 128, 128)
        dq[:, pl.ds(column, 128)] = query[...].astype(F32)
        dk[:, pl.ds(column, 128)] = pair[0].astype(F32)
        d_projected[:, pl.ds(pl.multiple_of(2 * width + column, 128), 128)] = pair[1]
    finish(copies)

    def take(which, r, start, lanes):
        return (dq, dk)[which][r, start : start + lanes]

    project_back(normed, weight, gains, head_matrix(256, head), take, d_projected, sums)
    for start in range(0, model, 256):
        part[:, start : start + 256] = dot(d_projected[...], weight[start : start + 256, :], NT).astype(BF)


def queries_back(meta, w_in, d_queries, d_pairs, normed, gains, head):
    total, model = normed.shape
    width = gains.shape[1]
    return call(
        with_weights(functools.partial(queries_back_kernel, head), 1, [w_in]),
        (
            jax.ShapeDtypeStruct((total, 3 * width), BF),
            jax.ShapeDtypeStruct((total, model), BF),
            jax.ShapeDtypeStruct((16, width), F32),
        ),
        [SM] + [HBM] * w_in.count + [VM] * 10,
        (VM,) * 3,
        [
            pltpu.VMEM((model, 3 * width), BF),
            pltpu.VMEM((total, width), F32),
            pltpu.VMEM((total, width), F32),
            pltpu.SemaphoreType.DMA((PIECES,)),
        ],
        10 * total * model * width,
        8 * model * width,
        "queries_back",
    )(meta, *w_in.sources, *d_queries, *d_pairs, normed, gains)


META_CORE = 5 * PIECES
META_ME = META_CORE + 1
META_SCENES = META_ME + 1


def body(tokens, cotangent, scene_ids, input_weight, output_weight, up_weight, down_weight, norm_params, head_gains):
    portions, _, share, model = tokens.shape
    frame = 2 * share
    total = portions * frame
    head = head_gains.shape[2]
    width = input_weight.shape[3]
    routes = Routes(lax.axis_size("frames"))
    n = routes.n
    index, core = lax.axis_index("frames"), lax.axis_index("mp")
    plain = n != PIECES

    identity = jnp.arange(PIECES, dtype=jnp.int32)
    tables = [identity] * 5 if plain else routes.tables()
    scene_here = scene_ids[:, (index // PLANE) * PLANE + jnp.arange(PLANE)]
    before = jnp.sum(scene_ids[:, None, :] < scene_here[:, :, None], axis=-1)
    until = jnp.sum(scene_ids[:, None, :] <= scene_here[:, :, None], axis=-1)
    spans = jnp.stack([before, until], axis=-1) - (index // PLANE) * PLANE + REACH
    meta = jnp.concatenate(
        [*tables, core[None], (index % PLANE)[None], spans.reshape(-1)]
    ).astype(jnp.int32)

    def all_rows(block):
        own = block[:, 0]
        other = routes.swap(own)
        both = jnp.where(core == 0, jnp.stack([own, other], 1), jnp.stack([other, own], 1))
        return both.reshape(total, model)

    def own_rows(values):
        return lax.dynamic_index_in_dim(values.reshape(portions, 2, share, -1), core, 1, keepdims=True)

    gains = [jnp.tile(head_gains[layer], (1, width // head)) for layer in range(2)]
    clock = Clock(not plain)
    late, close = clock.late, clock.close
    joined = [
        jnp.concatenate([input_weight[layer].reshape(-1, 3 * width), output_weight[layer]], axis=1)
        for layer in range(2)
    ]

    def gather(shard, line_first, name):
        if plain or line_first is None:
            return Whole(lax.all_gather(shard, "frames", axis=0, tiled=True))
        return Gather(routes, clock, shard, line_first, name)

    def scatter(line_last, name, lefts, rights):
        if plain or line_last is None:
            grad = weight_grad(meta, None, lefts, rights, name)
            ready[name] = grad
            summed = lax.psum_scatter(grad.astype(F32) if plain else grad, "frames", scatter_dimension=0, tiled=True)
            return Whole(summed.astype(F32))
        parts = weight_grad(meta, (3 if line_last else 2) * PIECES, lefts, rights, name)
        ready[name] = parts[2]
        return Scatter(routes, clock, parts, line_last, name)

    ready = {}

    ga0 = gather(joined[0], True, "input0")
    gu0 = gather(up_weight[0], True, "up0")
    gd0 = gather(down_weight[0], False, "down0")
    ga1 = gather(joined[1], False, "input1")
    gu1 = gather(up_weight[1], False, "up1")
    gd1 = gather(down_weight[1], False, "down1")
    ga0.ring(3)
    for each in (gd0, ga1, gu1, gd1):
        each.one()
    rows = all_rows(tokens)
    d_result = all_rows(cotangent)
    close(rows, d_result)
    ga0.one()
    ga0.two(0)
    gu0.ring(3)
    close()
    ga0.two(1)
    gd0.ring()
    close()
    in0, out0 = ga0.end(0, 3 * width), ga0.end(3 * width, width)
    gu0.one()
    gd0.ring()
    normed0, qkv0, attended0, a0 = attention_frame(
        meta, [in0, out0], late(rows), norm_params[0], gains[0], frame, head
    )
    close(a0)
    b0 = clock.add(routes.swap(a0))
    gu0.two(0)
    gu0.two(1)
    gd0.ring()
    ga1.ring()
    close()
    up0 = gu0.end()
    gd0.two(0)
    ga1.ring()
    mid0, normed_mid0, active0, slope0 = feed_up(meta, up0, rows, a0, late(b0), norm_params[0])
    close(active0)
    gd0.two(1)
    ga1.ring()
    close()
    down0 = gd0.end()
    ga1.two(0)
    ga1.two(1)
    gu1.ring(2)
    m0 = feed_down(meta, down0, late(active0), model)
    n0 = clock.add(routes.swap(m0))
    close(m0)
    in1, out1 = ga1.end(0, 3 * width), ga1.end(3 * width, width)
    gu1.two(0)
    gu1.ring()
    x1, normed1, *slots = queries(
        meta, in1, mid0, m0, late(n0), norm_params[0], norm_params[1], gains[1], head
    )
    close(slots[0])
    slots = routes.members(late(slots))
    gd1.ring()
    close(*slots[1:])
    rise, fall = edges(meta, late(slots))
    below, above = routes.up(rise), routes.down(fall)
    gu1.two(1)
    close(below, above)
    gd1.ring()
    gd1.two(0)
    *found, sums, whole_found = scene(meta, slots, late(below), above, frame)
    close(found[0])
    home = routes.members(late(found))
    gd1.ring()
    close(*home[1:])
    attended1, a1 = outputs(meta, out1, late(home), width, model)
    b1 = routes.swap(a1)
    close(b1)
    up1 = gu1.end()
    gd1.two(1)
    mid1, normed_mid1, active1, slope1 = feed_up(meta, up1, x1, a1, late(b1), norm_params[1])
    close(active1)

    down1 = gd1.end()
    d_mlp, d_hidden, p = feed_back(meta, [down1, up1], late(d_result), slope1, norm_params[1])
    close(p)
    q = clock.add(routes.swap(p))
    sd1 = scatter(True, "down_grad1", [late(d_mlp)], [active1])
    close(ready["down_grad1"])
    sd1.two(1)
    g, d_branch, inner1 = norm_back(meta, d_result, mid1, p, late(q), norm_params[1], frame, (a1, b1))
    d_home = attended_back(meta, out1, d_branch, width)
    su1 = scatter(True, "up_grad1", [late(normed_mid1)], [d_hidden])
    close(d_home[0], ready["up_grad1"])
    d_found = routes.members(late(d_home))
    close(*d_found[1:])
    sd1.one()
    sd1.two(0)
    *d_queries, d_own, d_below, d_above = scene_back(
        meta, slots, late(below), above, sums, whole_found, d_found, frame
    )
    close(d_own)
    from_above, from_below = routes.down(late(d_below)), routes.up(late(d_above))
    d_queries = routes.members(late(d_queries))
    su1.two(1)
    m1 = feed_down(meta, down1, late(active1), model)
    close(m1, from_above, from_below, *d_queries[1:])
    n1 = clock.add(routes.swap(m1))
    sd1.ring()
    pairs = routes.members(edge_sum(meta, d_own, late(from_below), from_above))
    close(*pairs[1:])
    su1.one()
    sd1.ring()
    d_projected, p, gain1 = queries_back(meta, in1, d_queries, late(pairs), normed1, gains[1], head)
    close(p)
    q = clock.add(routes.swap(p))
    su1.two(0)
    sd1.ring()
    sa1 = scatter(False, "input_grad1", [normed1, d_branch], [late(d_projected), attended1])
    close(ready["input_grad1"])
    sa1.two(0)
    su1.ring()
    own_mlp = own_rows(m1).astype(F32) + own_rows(n1).astype(F32)
    result = own_rows(mid1) + norm_params[1, 5] * own_mlp
    scale1 = jnp.sum(cotangent.astype(F32).reshape(-1, model) * own_mlp.reshape(-1, model), axis=0)
    g, outer1 = norm_back(meta, g, x1, p, late(q), norm_params[1], frame)

    d_mlp, d_hidden, p = feed_back(meta, [down0, up0], g, slope0, norm_params[0])
    close(p)
    q = clock.add(routes.swap(p))
    sa1.two(1)
    sa1.ring()
    su1.ring()
    sd0 = scatter(False, "down_grad0", [late(d_mlp)], [active0])
    if not plain:
        clock.step(ready["down_grad0"])
    sd0.two(0)
    sa1.ring()
    su1.ring()
    su0 = scatter(True, "up_grad0", [late(normed_mid0)], [d_hidden])
    g, d_branch, inner0 = norm_back(meta, g, mid0, p, late(q), norm_params[0], frame, (a0, b0, m0, n0))
    close(d_branch, ready["up_grad0"])
    sd0.two(1)
    su0.two(1)
    sa1.ring()
    sd0.ring()
    d_projected, p, gain0 = frame_back(
        meta, [in0, out0], late(d_branch), normed0, qkv0, gains[0], frame, head
    )
    close(p)
    q = clock.add(routes.swap(late(p)))
    su0.two(0)
    sd0.ring()
    sa1.one()
    sa0 = scatter(False, "input_grad0", [normed0, d_branch], [late(d_projected), attended0])
    close(ready["input_grad0"])
    su0.one()
    sa0.two(0)
    sd0.ring()
    g, outer0 = norm_back(meta, g, rows, p, late(q), norm_params[0], frame)
    token_grad = own_rows(g)
    close(g)

    norm_rows = [
        jnp.stack([outer[0], outer[1], inner[2], inner[0], inner[1], scale])
        for outer, inner, scale in ((outer0, inner0, inner0[3]), (outer1, inner1, scale1))
    ]
    gain_rows = [
        jnp.sum(gain.reshape(2, 8, width // head, head), axis=(1, 2)).reshape(1, -1)
        for gain in (gain0, gain1)
    ]
    gain_rows = jnp.pad(jnp.concatenate(gain_rows, axis=1), ((0, 0), (0, model - 4 * head)))
    small = jnp.concatenate([*norm_rows, gain_rows])
    small = small + routes.swap(small)
    distances = [2**i for i in range(n.bit_length() - 1)]

    def sum_step(block, distance):
        return block + clock.add(routes.member(late(block), distance))

    small = sum_step(small, distances[0])
    sa0.two(1)
    sa0.ring()
    su0.ring()
    close()
    small = sum_step(small, distances[1])
    sd0.one()
    sa0.ring()
    su0.ring()
    close()
    for distance in distances[2:]:
        small = sum_step(small, distance)
    sa0.ring()
    su0.ring()
    sa0.one()
    norm_grad = small[: 2 * 6].reshape(2, 6, model)
    gain_grad = small[2 * 6, : 4 * head].reshape(2, 2, head)
    return (
        result.astype(BF),
        token_grad,
        jnp.stack([step.run[:, : 3 * width].reshape(-1, 3, width) for step in (sa0, sa1)]),
        jnp.stack([step.run[:, 3 * width :] for step in (sa0, sa1)]),
        jnp.stack([step.run for step in (su0, su1)]),
        jnp.stack([step.run for step in (sd0, sd1)]),
        norm_grad,
        gain_grad,
    )


def solution(mesh):
    rows = P(None, "frames", "mp", None)
    shard = P(None, "frames", "mp")
    wide = P(None, "frames", None, "mp")
    return jax.shard_map(
        body,
        mesh=mesh,
        in_specs=(rows, rows, P(), wide, shard, shard, shard, P(), P()),
        out_specs=(rows, rows, wide, shard, shard, shard, P(), P()),
        check_vma=False,
    )
```
